128 devices in a mesh: tiles: 128 (over z, x, y, core).
Axes of the slice: x: 4, y: 4, z: 4, core: 2. Of those that a mesh axis runs over, the one named last changes fastest.
Arguments:
- fields: bfloat16 [192, 8, 16384], P(None, None, 'tiles'), may hold values from -6 to 6
- cotangent: bfloat16 [192, 8, 16384], P(None, None, 'tiles'), may hold values from -6 to 6
- weights: bfloat16 [3, 9, 192, 192], replicated, may hold values from -0.21875 to 0.21875
- biases: float32 [3, 192], replicated, may hold values from -3 to 3
- ocean_tiles: int32 [1, 128], P(None, 'tiles'), may hold values 0 or 1
- velocity_mask: int32 [192], replicated, may hold values 0 or 1
Outputs:
- output: bfloat16 [192, 8, 16384], P(None, None, 'tiles')
- field_grad: bfloat16 [192, 8, 16384], P(None, None, 'tiles')
- weight_grad: float32 [3, 9, 192, 192], replicated
- bias_grad: float32 [3, 192], replicated
The draws below stay inside these ranges and needn't reach their ends.
All inputs are finite; a program needn't handle non-finite values. No bound on the sum of `ocean_tiles` on one device may be relied on, other than what follows from the above.
Results may differ from the reference program's by a relative error of at most 0.011.
Values may be sent and summed in bfloat16 or wider, within the bound.
A program may use at most 128 MiB of HBM per device.

```python
import jax
import jax.numpy as jnp

C = 192
TW = 128
TH = 8
TILES_DEV = 1
ROWS = 8
COLS = 16384
N_TILES = 128


def with_ends(entries, own_key, smallest, top_value):
    shape = entries.shape
    place = [jax.random.randint(jax.random.fold_in(own_key, axis), (), 0, shape[axis]) for axis in range(len(shape))]
    entries = entries.at[tuple(place)].set(smallest)
    longest = shape.index(max(shape))
    place[longest] = (place[longest] + 1) % shape[longest]
    return entries.at[tuple(place)].set(top_value)


def levels(own_key, dims, pieces, low, largest):
    level, own = 1.0, jax.random.fold_in(own_key, 6)
    for axis_at, blocks in pieces:
        draws = jnp.exp(jax.random.uniform(jax.random.fold_in(own, axis_at), (blocks,), jnp.float32, low / len(pieces), largest / len(pieces)))
        level = level * jnp.repeat(draws, dims[axis_at] // blocks).reshape([-1 if axis == axis_at else 1 for axis in range(len(dims))])
    return level


def noise(stream_key, shape, deviation, most, shards=(), kind=jnp.bfloat16):
    drawn = jax.random.normal(stream_key, shape, jnp.float32) * deviation
    if len(shards) > 0:
        drawn = levels(stream_key, shape, shards, -0.22, 0.18) * drawn
    return jnp.clip(drawn, min=-most, max=most).astype(kind)


def setup_inputs(seed: int = 0) -> dict:
    arg_keys = jax.random.split(jax.random.key(seed), 7)
    return {
        "fields": noise(arg_keys[0], (C, ROWS, COLS), 1.0, 6.0, ((2, 128),)),
        "cotangent": noise(arg_keys[1], (C, ROWS, COLS), 1.0, 6.0, ((2, 128),)),
        "weights": noise(arg_keys[2], (3, 9, C, C), (4 * C) ** -0.5, 0.21875),
        "biases": noise(arg_keys[3], (3, C), 0.5, 3.0, (), jnp.float32),
        "ocean_tiles": with_ends((jax.random.randint(arg_keys[4], (TILES_DEV, N_TILES), 0, 4) < 3).astype(jnp.int32), jax.random.fold_in(arg_keys[4], 1), 0, 1),
        "velocity_mask": with_ends((jax.random.randint(arg_keys[5], (C,), 0, 4) < 1).astype(jnp.int32), jax.random.fold_in(arg_keys[5], 1), 0, 1),
    }


offsets = tuple((vertical, lateral) for vertical in (-1, 0, 1) for lateral in (-1, 0, 1))


def extend_field(current, spread, flip_sign):
    channels, row_count, col_count = current.shape
    mirrored = (current[:, row_count - spread:, ::-1][:, ::-1, :].astype(jnp.float32) * flip_sign).astype(current.dtype)
    stacked = jnp.concatenate([jnp.zeros((channels, spread, col_count), current.dtype), current, mirrored], axis=1)
    return jnp.concatenate([stacked[:, :, col_count - spread:], stacked, stacked[:, :, :spread]], axis=2)


def forward_conv(padded, kernel, bias_row, spread, row_count, col_count):
    running = jnp.zeros((kernel.shape[1], row_count, col_count), jnp.float32)
    for number, (vertical, lateral) in enumerate(offsets):
        top_row = spread * (1 + vertical)
        left_col = spread * (1 + lateral)
        shifted = padded[:, top_row:top_row + row_count, left_col:left_col + col_count].astype(jnp.float32)
        running = running + jnp.einsum("oc,crw->orw", kernel[number].astype(jnp.float32), shifted)
    return running + bias_row[:, None, None]


def backward_conv(padded, delta, kernel, spread):
    channels, row_count, col_count = delta.shape
    delta_wide = delta.astype(jnp.float32)
    extended = jnp.pad(delta_wide, ((0, 0), (2 * spread, 2 * spread), (2 * spread, 2 * spread)))
    spill = jnp.zeros((channels, row_count + 2 * spread, col_count + 2 * spread), jnp.float32)
    kernel_terms = []
    for number, (vertical, lateral) in enumerate(offsets):
        top_row = spread * (1 - vertical)
        left_col = spread * (1 - lateral)
        source = extended[:, top_row:top_row + row_count + 2 * spread, left_col:left_col + col_count + 2 * spread]
        spill = spill + jnp.einsum("oc,orw->crw", kernel[number].astype(jnp.float32), source)
        shifted = padded[:, spread * (1 + vertical):spread * (1 + vertical) + row_count, spread * (1 + lateral):spread * (1 + lateral) + col_count].astype(jnp.float32)
        kernel_terms.append(jnp.einsum("orw,crw->oc", delta_wide, shifted))
    return spill, jnp.stack(kernel_terms), jnp.sum(delta_wide, axis=(1, 2))


def reference(fields, cotangent, weights, biases, ocean_tiles, velocity_mask):
    channels, row_count, col_count = fields.shape
    cell_mask = jnp.repeat(jnp.repeat(ocean_tiles.astype(jnp.float32), TH, axis=0), TW, axis=1)[None]
    flip_sign = (1 - 2 * velocity_mask).astype(jnp.float32)[:, None, None]
    current = (fields.astype(jnp.float32) * cell_mask).astype(jnp.bfloat16)
    stored = []
    for layer_index in range(3):
        spread = 2 ** layer_index
        padded = extend_field(current, spread, flip_sign)
        before = forward_conv(padded, weights[layer_index], biases[layer_index], spread, row_count, col_count)
        current = (cell_mask * (current.astype(jnp.float32) + jax.nn.silu(before))).astype(jnp.bfloat16)
        stored.append((padded, before))
    output = current
    grad_now = cell_mask * cotangent.astype(jnp.float32)
    kernel_grads = [None, None, None]
    bias_grads = [None, None, None]
    for layer_index in (2, 1, 0):
        spread = 2 ** layer_index
        padded, before = stored[layer_index]
        masked = cell_mask * grad_now
        sigmoid = jax.nn.sigmoid(before)
        delta = (masked * sigmoid * (1.0 + before * (1.0 - sigmoid))).astype(jnp.bfloat16)
        spill, kernel_part, bias_part = backward_conv(padded, delta, weights[layer_index], spread)
        core = spill[:, :, spread:col_count + spread]
        core = core.at[:, :, col_count - spread:].add(spill[:, :, :spread])
        core = core.at[:, :, :spread].add(spill[:, :, col_count + spread:])
        returned = flip_sign * core[:, row_count + spread:, ::-1][:, ::-1, :]
        grad_now = masked + core[:, spread:row_count + spread, :]
        grad_now = grad_now.at[:, row_count - spread:, :].add(returned)
        kernel_grads[layer_index] = kernel_part
        bias_grads[layer_index] = bias_part
    field_grad = (cell_mask * grad_now).astype(jnp.bfloat16)
    return output, field_grad, jnp.stack(kernel_grads), jnp.stack(bias_grads)
```

```python
import jax
import jax.numpy as jnp
from jax import lax
from jax.sharding import PartitionSpec as P

offsets = tuple(((vertical, lateral) for vertical in (-1, 0, 1) for lateral in (-1, 0, 1)))


def padded_2(block, sides, width):
    for axis, dim in sides:
        count = lax.axis_size(axis)
        forward = [(i, i + 1) for i in range(count - 1)]
        forward.append((count - 1, 0))
        backward = [(target, source) for source, target in forward]
        low = lax.ppermute(
            lax.slice_in_dim(block, block.shape[dim] - width, None, axis=dim), axis, forward
        )
        high = lax.ppermute(lax.slice_in_dim(block, 0, width, axis=dim), axis, backward)
        block = jnp.concatenate([low, block, high], axis=dim)
    return block


def passed_along(array, axis, by):
    devices = lax.axis_size(axis)
    return lax.ppermute(array, axis, [(i, (i + by) % devices) for i in range(devices)])


def fold_ahead(top_strip):
    devices = lax.axis_size("tiles")
    return lax.ppermute(top_strip, "tiles", [(i, devices - 1 - i) for i in range(devices)])


def fold_behind(top_strip):
    return fold_ahead(top_strip.astype(jnp.bfloat16)).astype(top_strip.dtype)


def forward_tiles(padded, kernel, bias_row, column, spread, tile_rows):
    channels = padded.shape[0]
    col_count = padded.shape[2] - 2 * spread

    def apply_kernel(window):
        running = jnp.zeros((channels, tile_rows, col_count), jnp.float32)
        for number, (vertical, lateral) in enumerate(offsets):
            top_row = spread * (1 + vertical)
            left_col = spread * (1 + lateral)
            shifted = window[:, top_row : top_row + tile_rows, left_col : left_col + col_count]
            running = running + jnp.einsum(
                "oc,crw->orw", kernel[number], shifted, preferred_element_type=jnp.float32
            )
        return running + bias_row[:, None, None]

    def forward_per_tile(totals, tile_index):
        result = apply_kernel(padded)
        return (totals, result)

    unused, stacked = lax.scan(
        forward_per_tile, jnp.zeros((), jnp.float32), jnp.arange(column.shape[0])
    )
    return jnp.transpose(stacked, (1, 0, 2, 3)).reshape(channels, -1, col_count)


def backward_tiles(padded, delta, kernel, column, spread, tile_rows):
    channels, row_count, col_count = delta.shape
    tile_count = column.shape[0]
    wide_cols = col_count + 2 * spread

    def transpose_kernel(inputs):
        window, delta_tile = inputs
        extended = jnp.pad(delta_tile, ((0, 0), (2 * spread, 2 * spread), (2 * spread, 2 * spread)))
        spill = jnp.zeros((channels, tile_rows + 2 * spread, wide_cols), jnp.float32)
        kernel_terms = []
        for number, (vertical, lateral) in enumerate(offsets):
            top_row = spread * (1 - vertical)
            left_col = spread * (1 - lateral)
            source = extended[
                :, top_row : top_row + tile_rows + 2 * spread, left_col : left_col + wide_cols
            ]
            spill = spill + jnp.einsum(
                "oc,orw->crw", kernel[number], source, preferred_element_type=jnp.float32
            )
            shifted = window[
                :,
                spread * (1 + vertical) : spread * (1 + vertical) + tile_rows,
                spread * (1 + lateral) : spread * (1 + lateral) + col_count,
            ]
            kernel_terms.append(
                jnp.einsum("orw,crw->oc", delta_tile, shifted, preferred_element_type=jnp.float32)
            )
        return (
            spill,
            jnp.stack(kernel_terms),
            jnp.sum(delta_tile.astype(jnp.float32), axis=(1, 2)),
        )

    def backward_per_tile(totals, tile_index):
        result = transpose_kernel((padded, delta))
        spill, kernel_part, bias_part = result
        return ((totals[0] + kernel_part, totals[1] + bias_part), spill)

    start_totals = (
        jnp.zeros((9, channels, channels), jnp.float32),
        jnp.zeros((channels,), jnp.float32),
    )
    (kernel_total, bias_total), spills = lax.scan(
        backward_per_tile, start_totals, jnp.arange(tile_count)
    )
    heads = jnp.transpose(spills[:, :, :tile_rows], (1, 0, 2, 3)).reshape(
        channels, row_count, wide_cols
    )
    tails = jnp.pad(spills[:, :, tile_rows:], ((0, 0), (0, 0), (0, tile_rows - 2 * spread), (0, 0)))
    tails = jnp.transpose(tails, (1, 0, 2, 3)).reshape(channels, row_count, wide_cols)
    input_spill = jnp.pad(heads, ((0, 0), (0, 2 * spread), (0, 0)))
    input_spill = (
        input_spill + jnp.pad(tails, ((0, 0), (tile_rows, 0), (0, 0)))[:, : row_count + 2 * spread]
    )
    return (input_spill, kernel_total, bias_total)


def shards(fields, cotangent, weights, biases, ocean_tiles, velocity_mask):
    channels, row_count, col_count = fields.shape
    tile_count = ocean_tiles.shape[0]
    tile_rows = row_count // tile_count
    column = ocean_tiles[:, 0]
    cell_mask = jnp.repeat(column.astype(jnp.float32), tile_rows)[None, :, None]
    flip_sign = (1 - 2 * velocity_mask).astype(jnp.float32)[:, None, None]
    current = (fields.astype(jnp.float32) * cell_mask).astype(jnp.bfloat16)
    stored = []
    for layer_index in range(3):
        spread = 2**layer_index
        partner_top = fold_ahead(current[:, row_count - spread :, :])
        mirrored = (partner_top[:, ::-1, ::-1].astype(jnp.float32) * flip_sign).astype(jnp.bfloat16)
        stacked = jnp.concatenate(
            [jnp.zeros((channels, spread, col_count), jnp.bfloat16), current, mirrored], axis=1
        )
        padded = padded_2(stacked, (("tiles", 2),), spread)
        before = forward_tiles(
            padded, weights[layer_index], biases[layer_index], column, spread, tile_rows
        )
        current = (cell_mask * (current.astype(jnp.float32) + jax.nn.silu(before))).astype(
            jnp.bfloat16
        )
        stored.append((padded, before))
    grad_now = cell_mask * cotangent.astype(jnp.float32)
    kernel_grads = [None, None, None]
    bias_grads = [None, None, None]
    for layer_index in (2, 1, 0):
        spread = 2**layer_index
        padded, before = stored[layer_index]
        masked = cell_mask * grad_now
        sigmoid = jax.nn.sigmoid(before)
        delta = (masked * sigmoid * (1.0 + before * (1.0 - sigmoid))).astype(jnp.bfloat16)
        input_spill, kernel_part, bias_part = backward_tiles(
            padded, delta, weights[layer_index], column, spread, tile_rows
        )
        from_east = passed_along(
            input_spill[:, :, :spread].astype(jnp.bfloat16), "tiles", -1
        ).astype(jnp.float32)
        from_west = passed_along(
            input_spill[:, :, col_count + spread :].astype(jnp.bfloat16), "tiles", 1
        ).astype(jnp.float32)
        core = input_spill[:, :, spread : col_count + spread]
        core = core.at[:, :, col_count - spread :].add(from_east)
        core = core.at[:, :, :spread].add(from_west)
        returned = fold_behind(flip_sign * core[:, row_count + spread :, ::-1][:, ::-1, :])
        grad_now = masked + core[:, spread : row_count + spread, :]
        grad_now = grad_now.at[:, row_count - spread :, :].add(returned)
        kernel_grads[layer_index] = kernel_part
        bias_grads[layer_index] = bias_part
    kernel_stack = jnp.stack(kernel_grads)
    bias_stack = jnp.stack(bias_grads)
    kernel_stack = lax.psum(kernel_stack.astype(jnp.bfloat16), "tiles").astype(jnp.float32)
    bias_stack = lax.psum(bias_stack, "tiles")
    field_grad = (cell_mask * grad_now).astype(jnp.bfloat16)
    return (current, field_grad, kernel_stack, bias_stack)


def solution(mesh):
    placed = (P(None, None, "tiles"), P(None, None, "tiles"), P(), P(), P(None, "tiles"), P())
    return jax.shard_map(
        shards,
        mesh=mesh,
        in_specs=placed,
        out_specs=(P(None, None, "tiles"), P(None, None, "tiles"), P(), P()),
        check_vma=False,
    )
```

```python
import functools

import jax
import jax.numpy as jnp
from jax import lax
from jax.experimental import pallas as pl
from jax.experimental.pallas import tpu as pltpu
from jax.sharding import PartitionSpec as P

C = 192
ROWS = 8
LANES = 128
CELLS = ROWS * LANES
WIDE = 640
TOTAL = 2048
HALF = TOTAL // 2
BAND = C // 4
PART = HALF // 4
BF = jnp.bfloat16
F32 = jnp.float32
MESH = pl.DeviceIdType.MESH

CORE = (1, 2)
Y = (2, 4)
X = (8, 4)
Z = (32, 4)
ORDERS = ((Y, X, Z), (Z, Y, X), (X, Z, Y))


def coordinate(me, axis):
    return lax.rem(lax.div(me, axis[0]), axis[1])


def with_coordinate(me, axis, value):
    return me + (value - coordinate(me, axis)) * axis[0]


def copy_to(src, dst, send_sem, recv_sem, device):
    return pltpu.make_async_remote_copy(
        src_ref=src,
        dst_ref=dst,
        send_sem=send_sem,
        recv_sem=recv_sem,
        device_id=(device,),
        device_id_type=MESH,
    )


def start_if(condition, copy):
    @pl.when(condition)
    def _():
        copy.start()


def dot(a, b):
    return jnp.dot(a, b, preferred_element_type=F32)


def dot_nt(a, b):
    return lax.dot_general(a, b, (((1,), (1,)), ((), ())), preferred_element_type=F32)


def kernel(
    n,
    x_ref,
    ct_ref,
    w_ref,
    cols_ref,
    out_ref,
    fg_ref,
    dw_ref,
    s0,
    s1,
    s2,
    t0,
    t1,
    t2,
    slope,
    acc,
    grad,
    wf,
    wt,
    packed,
    turned,
    rims,
    partial,
    to_mate,
    from_mate,
    a_out,
    a_in,
    b_out,
    b_in,
    c_in,
    full,
    ex_send,
    ex_recv,
    ar_send,
    ar_recv,
):
    me = lax.axis_index("tiles")
    east = lax.rem(me + 1, n)
    west = lax.rem(me + n - 1, n)
    mirror = n - 1 - me
    fold_a = lax.rem(n - me, n)
    fold_b = lax.rem(2 * n - 2 - me, n)
    mate = with_coordinate(me, CORE, 1 - coordinate(me, CORE))
    core = coordinate(me, CORE)
    a_away = fold_a != me
    b_away = fold_b != me

    barrier = pltpu.get_barrier_semaphore()
    partners = [east, west, mirror, mate]
    for axis in (Y, X, Z):
        for step in (1, 2, 3):
            partners.append(
                with_coordinate(me, axis, lax.rem(coordinate(me, axis) + step, axis[1]))
            )
    for partner in partners:
        pl.semaphore_signal(barrier, inc=1, device_id=(partner,), device_id_type=MESH)

    @pl.when(a_away)
    def _():
        pl.semaphore_signal(barrier, inc=1, device_id=(fold_a,), device_id_type=MESH)

    @pl.when(b_away)
    def _():
        pl.semaphore_signal(barrier, inc=1, device_id=(fold_b,), device_id_type=MESH)

    lane = lax.broadcasted_iota(jnp.int32, (C, LANES), 1)
    flip_matrix = (
        lax.broadcasted_iota(jnp.int32, (LANES, LANES), 0)
        + lax.broadcasted_iota(jnp.int32, (LANES, LANES), 1)
        == LANES - 1
    ).astype(F32).astype(BF)
    flip_sign = cols_ref[:, 3:4]
    mask = cols_ref[:, 4:5]
    sends = []

    def columns(row):
        return slice(row * LANES, (row + 1) * LANES)

    def send_rims(e, buf, d, signed):
        pack = jnp.zeros((C, LANES), F32)
        for k in range(d):
            turn = dot(buf[C : 2 * C, columns(ROWS - 1 - k)], flip_matrix)
            if signed:
                turn = turn * flip_sign
            turned[e, :, columns(k)] = turn.astype(BF)
            at = 2 * d * (ROWS + k)
            here = jnp.logical_and(lane >= at, lane < at + 2 * d)
            pack = jnp.where(here, pltpu.roll(turn, (at + d) % LANES, 1), pack)
        if e == 0:
            pl.semaphore_wait(
                barrier,
                len(partners) + a_away.astype(jnp.int32) + b_away.astype(jnp.int32),
            )

        fold = copy_to(
            turned.at[e, :, pl.ds(0, d * LANES)],
            buf.at[pl.ds(C, C), pl.ds(CELLS, d * LANES)],
            ex_send.at[e, 4],
            ex_recv.at[e, 4],
            mirror,
        )
        fold.start()
        for r in range(ROWS):
            at = 2 * d * r
            here = jnp.logical_and(lane >= at, lane < at + 2 * d)
            row = buf[C : 2 * C, columns(r)].astype(F32)
            pack = jnp.where(here, pltpu.roll(row, (at + d) % LANES, 1), pack)
        packed[e] = pack.astype(BF)
        copies = []
        for slot, target in enumerate((east, west, fold_a, fold_b)):
            copies.append(
                copy_to(
                    packed.at[e],
                    rims.at[e, slot],
                    ex_send.at[e, slot],
                    ex_recv.at[e, slot],
                    target,
                )
            )
        copies[0].start()
        copies[1].start()
        start_if(a_away, copies[2])
        start_if(b_away, copies[3])
        sends.append((None, fold))
        sends.append((None, copies[0]))
        sends.append((None, copies[1]))
        sends.append((a_away, copies[2]))
        sends.append((b_away, copies[3]))
        return copies, fold

    def receive_rims(e, buf, d, waits):
        copies, fold = waits
        copies[0].wait_recv()
        copies[1].wait_recv()
        for away, slot in ((a_away, 2), (b_away, 3)):

            @pl.when(away)
            def _():
                copies[slot].wait_recv()

            @pl.when(jnp.logical_not(away))
            def _():
                rims[e, slot] = packed[e]

        fold.wait_recv()
        low = lax.rem(lane, 2 * d) < d
        rim = [rims[e, slot].astype(F32) for slot in range(4)]
        rim = jnp.where(
            lane < 2 * d * ROWS, jnp.where(low, rim[0], rim[1]), jnp.where(low, rim[2], rim[3])
        )
        for r in range(ROWS + d):
            row = buf[C : 2 * C, columns(r)].astype(F32)
            edge = pltpu.roll(rim, (-(2 * d * r + d)) % LANES, 1)
            buf[0:C, columns(r)] = pltpu.roll(
                jnp.where(lane >= LANES - d, edge, row), d, 1
            ).astype(BF)
            buf[2 * C : 3 * C, columns(r)] = pltpu.roll(
                jnp.where(lane < d, edge, row), LANES - d, 1
            ).astype(BF)

    def all_reduce(l):
        axis_a, axis_b, axis_c = ORDERS[l]
        place_a, place_b, place_c = (coordinate(me, axis) for axis in ORDERS[l])
        half = pl.ds(pl.multiple_of(core * HALF, LANES), HALF)
        other = pl.ds(pl.multiple_of((1 - core) * HALF, LANES), HALF)
        band = pl.ds(pl.multiple_of(place_a * BAND, 16), BAND)
        count = [0]

        def post(src, dst, target):
            number = count[0]
            count[0] += 1
            copy = copy_to(src, dst, ar_send.at[l, number], ar_recv.at[l, number], target)
            copy.start()
            sends.append((None, copy))
            return copy

        def around(axis, place):
            for step in (1, 2, 3):
                to = lax.rem(place + step, 4)
                yield step - 1, to, with_coordinate(me, axis, to)

        to_mate[l] = partial[l, :, other].astype(BF)
        copy = post(to_mate.at[l], from_mate.at[l], mate)
        yield
        copy.wait_recv()
        a_out[l] = (partial[l, :, half] + from_mate[l].astype(F32)).astype(BF)
        copies = [
            post(
                a_out.at[l, pl.ds(pl.multiple_of(to * BAND, 16), BAND)], a_in.at[l, slot], target
            )
            for slot, to, target in around(axis_a, place_a)
        ]
        yield
        for copy in copies:
            copy.wait_recv()
        total = a_out[l, band].astype(F32)
        for slot in range(3):
            total = total + a_in[l, slot].astype(F32)
        b_out[l] = total.astype(BF)
        copies = [
            post(
                b_out.at[l, :, pl.ds(pl.multiple_of(to * PART, LANES), PART)],
                b_in.at[l, slot],
                target,
            )
            for slot, to, target in around(axis_b, place_b)
        ]
        yield
        for copy in copies:
            copy.wait_recv()
        total = b_out[l, :, pl.ds(pl.multiple_of(place_b * PART, LANES), PART)].astype(F32)
        for slot in range(3):
            total = total + b_in[l, slot].astype(F32)
        c_in[l, place_c] = total.astype(BF)
        copies = [
            post(c_in.at[l, place_c], c_in.at[l, place_c], target)
            for slot, to, target in around(axis_c, place_c)
        ]
        yield
        for copy in copies:
            copy.wait_recv()
        total = c_in[l, 0].astype(F32)
        for slot in range(1, 4):
            total = total + c_in[l, slot].astype(F32)
        mine = pl.ds(pl.multiple_of(core * HALF + place_b * PART, LANES), PART)
        full[l, band, mine] = total.astype(BF)
        copies = [
            post(full.at[l, band, mine], full.at[l, band, mine], target)
            for slot, to, target in around(axis_b, place_b)
        ]
        yield
        for copy in copies:
            copy.wait_recv()
        final = [post(full.at[l, band, half], full.at[l, band, half], mate)]
        copies = [
            post(full.at[l, band, half], full.at[l, band, half], target)
            for slot, to, target in around(axis_a, place_a)
        ]
        yield
        for step, copy in enumerate(copies):
            copy.wait_recv()
            source = lax.rem(place_a + 3 - step, 4)
            piece = full.at[l, pl.ds(pl.multiple_of(source * BAND, 16), BAND), half]
            final.append(post(piece, piece, mate))
        yield
        for copy in final:
            copy.wait_recv()
        dw_ref[l] = full[l]
        yield

    forward_buffers = (s0, s1, s2)
    backward_buffers = (t0, t1, t2)

    for r in range(ROWS):
        s0[C : 2 * C, columns(r)] = (x_ref[r].astype(F32) * mask).astype(BF)

    for l in range(3):
        d = 2**l
        buf = forward_buffers[l]
        waits = send_rims(l, buf, d, True)
        for a in range(3):
            for b in range(3):
                tap = w_ref[l, 3 * a + b]
                wf[l, a, :, b * C : (b + 1) * C] = tap
                wt[l, a, :, (2 - b) * C : (3 - b) * C] = tap.T
        if l > 0:
            v = slope[l - 1]
            s = jax.nn.sigmoid(v)
            slope[l - 1] = s * (1.0 + v * (1.0 - s))
        receive_rims(l, buf, d, waits)
        acc[...] = dot(wf[l, 1], buf[:, 0:CELLS]) + cols_ref[:, l : l + 1]
        acc[...] += dot(wf[l, 2], buf[:, d * LANES : CELLS + d * LANES])
        acc[:, d * LANES : CELLS] += dot(wf[l, 0], buf[:, 0 : CELLS - d * LANES])
        v = acc[...]
        slope[l] = v
        after = (
            mask * (buf[C : 2 * C, 0:CELLS].astype(F32) + v * jax.nn.sigmoid(v))
        ).astype(BF)
        if l < 2:
            forward_buffers[l + 1][C : 2 * C, 0:CELLS] = after
        else:
            for r in range(ROWS):
                out_ref[r] = after[:, columns(r)]

    v = slope[2]
    s = jax.nn.sigmoid(v)
    slope[2] = s * (1.0 + v * (1.0 - s))
    for r in range(ROWS):
        grad[:, columns(r)] = mask * ct_ref[r].astype(F32)

    running = []
    for l in (2, 1, 0):
        d = 2**l
        stored = forward_buffers[l]
        buf = backward_buffers[l]
        delta = (grad[...] * slope[l]).astype(BF)
        buf[C : 2 * C, 0:CELLS] = delta
        waits = send_rims(5 - l, buf, d, False)
        for reduction in running:
            next(reduction)
        partial[l, :, 512:640] = jnp.zeros((C, LANES), F32)
        partial[l, :, 1152:1280] = jnp.zeros((C, LANES), F32)
        partial[l, :, 1792:1920] = jnp.zeros((C, LANES), F32)
        partial[l, :, 0:576] = dot_nt(
            buf[C : 2 * C, d * LANES : CELLS], stored[:, 0 : CELLS - d * LANES]
        )
        partial[l, :, 640:1216] = dot_nt(buf[C : 2 * C, 0:CELLS], stored[:, 0:CELLS])
        partial[l, :, 1280:1856] = dot_nt(
            buf[C : 2 * C, 0:CELLS], stored[:, d * LANES : CELLS + d * LANES]
        )
        partial[l, :, 1920:2048] = jnp.broadcast_to(
            jnp.sum(buf[C : 2 * C, 0:CELLS].astype(F32), axis=1, keepdims=True), (C, LANES)
        )
        reduction = all_reduce(l)
        next(reduction)
        running.append(reduction)
        receive_rims(5 - l, buf, d, waits)
        rest = CELLS - d * LANES
        acc[...] = dot(wt[l, 1], buf[:, 0:CELLS])
        acc[:, d * LANES : CELLS] += dot(wt[l, 2], buf[:, 0:rest])
        acc[:, 0:rest] += dot(wt[l, 0], buf[:, d * LANES : CELLS])
        over = dot(wt[l, 2, :, 0:C], buf[2 * C : 3 * C, CELLS : CELLS + d * LANES])
        over += dot(wt[l, 2, :, C : 2 * C], buf[C : 2 * C, CELLS : CELLS + d * LANES])
        over += dot(wt[l, 2, :, 2 * C : 3 * C], buf[0:C, CELLS : CELLS + d * LANES])
        acc[:, rest:CELLS] += flip_sign * over
        grad[...] = mask * (grad[...] + acc[...])

    for r in range(ROWS):
        fg_ref[r] = grad[:, columns(r)].astype(BF)
    done = object()
    while running:
        running = [reduction for reduction in running if next(reduction, done) is not done]
    for condition, copy in sends:
        if condition is None:
            copy.wait_send()
        else:

            @pl.when(condition)
            def _():
                copy.wait_send()


def shards(fields, cotangent, weights, biases, ocean_tiles, velocity_mask):
    n = lax.axis_size("tiles")
    cols = jnp.concatenate(
        [
            biases.T,
            (1 - 2 * velocity_mask).astype(F32)[:, None],
            jnp.broadcast_to(ocean_tiles.astype(F32), (C, 1)),
        ],
        axis=1,
    )
    cols = jnp.pad(cols, ((0, 0), (0, LANES - cols.shape[1])))
    vmem = pl.BlockSpec(memory_space=pltpu.VMEM)
    out, field_grad, summed = pl.pallas_call(
        functools.partial(kernel, n),
        out_shape=(
            jax.ShapeDtypeStruct((ROWS, C, LANES), BF),
            jax.ShapeDtypeStruct((ROWS, C, LANES), BF),
            jax.ShapeDtypeStruct((3, C, TOTAL), BF),
        ),
        in_specs=[vmem] * 4,
        out_specs=(vmem,) * 3,
        scratch_shapes=[
            pltpu.VMEM((3 * C, CELLS + LANES), BF),
            pltpu.VMEM((3 * C, CELLS + 2 * LANES), BF),
            pltpu.VMEM((3 * C, CELLS + 4 * LANES), BF),
            pltpu.VMEM((3 * C, CELLS + LANES), BF),
            pltpu.VMEM((3 * C, CELLS + 2 * LANES), BF),
            pltpu.VMEM((3 * C, CELLS + 4 * LANES), BF),
            pltpu.VMEM((3, C, CELLS), F32),
            pltpu.VMEM((C, CELLS), F32),
            pltpu.VMEM((C, CELLS), F32),
            pltpu.VMEM((3, 3, C, 3 * C), BF),
            pltpu.VMEM((3, 3, C, 3 * C), BF),
            pltpu.VMEM((6, C, LANES), BF),
            pltpu.VMEM((6, C, 4 * LANES), BF),
            pltpu.VMEM((6, 4, C, LANES), BF),
            pltpu.VMEM((3, C, TOTAL), F32),
            pltpu.VMEM((3, C, HALF), BF),
            pltpu.VMEM((3, C, HALF), BF),
            pltpu.VMEM((3, C, HALF), BF),
            pltpu.VMEM((3, 3, BAND, HALF), BF),
            pltpu.VMEM((3, BAND, HALF), BF),
            pltpu.VMEM((3, 3, BAND, PART), BF),
            pltpu.VMEM((3, 4, BAND, PART), BF),
            pltpu.VMEM((3, C, TOTAL), BF),
            pltpu.SemaphoreType.DMA((6, 5)),
            pltpu.SemaphoreType.DMA((6, 5)),
            pltpu.SemaphoreType.DMA((3, 20)),
            pltpu.SemaphoreType.DMA((3, 20)),
        ],
        compiler_params=pltpu.CompilerParams(
            collective_id=0, has_side_effects=True, vmem_limit_bytes=56 * 1024 * 1024
        ),
        cost_estimate=pl.CostEstimate(
            flops=18 * 9 * C * C * CELLS, bytes_accessed=8 * 1024 * 1024, transcendentals=9 * C * CELLS
        ),
    )(jnp.transpose(fields, (1, 0, 2)), jnp.transpose(cotangent, (1, 0, 2)), weights, cols)
    taps = summed[:, :, : 3 * WIDE].reshape(3, C, 3, WIDE)[..., : 3 * C].reshape(3, C, 3, 3, C)
    kernel_grad = jnp.transpose(taps, (0, 2, 3, 1, 4)).reshape(3, 9, C, C).astype(F32)
    bias_grad = summed[:, :, 3 * WIDE].astype(F32)
    return (
        jnp.transpose(out, (1, 0, 2)),
        jnp.transpose(field_grad, (1, 0, 2)),
        kernel_grad,
        bias_grad,
    )


def solution(mesh):
    placed = (P(None, None, "tiles"), P(None, None, "tiles"), P(), P(), P(None, "tiles"), P())
    return jax.shard_map(
        shards,
        mesh=mesh,
        in_specs=placed,
        out_specs=(P(None, None, "tiles"), P(None, None, "tiles"), P(), P()),
        check_vma=False,
    )
```

```python
import functools

import jax
import jax.numpy as jnp
from jax import lax
from jax.experimental import pallas as pl
from jax.experimental.pallas import tpu as pltpu
from jax.sharding import PartitionSpec as P

C = 192
ROWS = 8
LANES = 128
CELLS = ROWS * LANES
WIDE = 640
TOTAL = 2048
HALF = TOTAL // 2
BAND = C // 4
PART = HALF // 4
BF = jnp.bfloat16
F32 = jnp.float32
MESH = pl.DeviceIdType.MESH

CORE = (1, 2)
Y = (2, 4)
X = (8, 4)
Z = (32, 4)
ORDERS = ((Y, X, Z), (Z, Y, X), (X, Z, Y))


def coordinate(me, axis):
    return lax.rem(lax.div(me, axis[0]), axis[1])


def with_coordinate(me, axis, value):
    return me + (value - coordinate(me, axis)) * axis[0]


def copy_to(src, dst, send_sem, recv_sem, device):
    return pltpu.make_async_remote_copy(
        src_ref=src,
        dst_ref=dst,
        send_sem=send_sem,
        recv_sem=recv_sem,
        device_id=(device,),
        device_id_type=MESH,
    )


def start_if(condition, copy):
    @pl.when(condition)
    def _():
        copy.start()


def dot(a, b):
    return jnp.dot(a, b, preferred_element_type=F32)


def dot_nt(a, b):
    return lax.dot_general(a, b, (((1,), (1,)), ((), ())), preferred_element_type=F32)


def kernel(
    n,
    x_ref,
    ct_ref,
    w_ref,
    bias_ref,
    ocean_ref,
    velocity_ref,
    out_ref,
    fg_ref,
    dw_ref,
    s0,
    s1,
    s2,
    t0,
    t1,
    t2,
    spread_rows,
    cols_ref,
    slope,
    acc,
    grad,
    wf,
    wt,
    packed,
    turned,
    rims,
    partial,
    to_mate,
    from_mate,
    a_out,
    a_in,
    b_out,
    b_in,
    c_in,
    full,
    ex_send,
    ex_recv,
    ar_send,
    ar_recv,
):
    me = lax.axis_index("tiles")
    east = lax.rem(me + 1, n)
    west = lax.rem(me + n - 1, n)
    mirror = n - 1 - me
    fold_a = lax.rem(n - me, n)
    fold_b = lax.rem(2 * n - 2 - me, n)
    mate = with_coordinate(me, CORE, 1 - coordinate(me, CORE))
    core = coordinate(me, CORE)
    a_away = fold_a != me
    b_away = fold_b != me

    barrier = pltpu.get_barrier_semaphore()
    partners = [east, west, mirror, mate]
    for axis in (Y, X, Z):
        for step in (1, 2, 3):
            partners.append(
                with_coordinate(me, axis, lax.rem(coordinate(me, axis) + step, axis[1]))
            )
    for partner in partners:
        pl.semaphore_signal(barrier, inc=1, device_id=(partner,), device_id_type=MESH)

    @pl.when(a_away)
    def _():
        pl.semaphore_signal(barrier, inc=1, device_id=(fold_a,), device_id_type=MESH)

    @pl.when(b_away)
    def _():
        pl.semaphore_signal(barrier, inc=1, device_id=(fold_b,), device_id_type=MESH)

    lane = lax.broadcasted_iota(jnp.int32, (C, LANES), 1)
    flip_matrix = (
        lax.broadcasted_iota(jnp.int32, (LANES, LANES), 0)
        + lax.broadcasted_iota(jnp.int32, (LANES, LANES), 1)
        == LANES - 1
    ).astype(F32).astype(BF)
    cols_ref[...] = jnp.zeros((LANES, 2 * LANES), F32)
    cols_ref[0:3, 0:C] = bias_ref[...]
    cols_ref[3:4, 0:C] = (1 - 2 * velocity_ref[...]).astype(F32).reshape(1, C)
    turned_cols = cols_ref[...].T[0:C]
    bias_cols = [turned_cols[:, l : l + 1] for l in range(3)]
    flip_sign = turned_cols[:, 3:4]
    mask = ocean_ref[0, 0].astype(F32)
    sends = []

    def columns(row):
        return slice(row * LANES, (row + 1) * LANES)

    def send_rims(e, buf, d, signed):
        pack = jnp.zeros((C, LANES), F32)
        for k in range(d):
            turn = dot(buf[C : 2 * C, columns(ROWS - 1 - k)], flip_matrix)
            if signed:
                turn = turn * flip_sign
            turned[e, :, columns(k)] = turn.astype(BF)
            at = 2 * d * (ROWS + k)
            here = jnp.logical_and(lane >= at, lane < at + 2 * d)
            pack = jnp.where(here, pltpu.roll(turn, (at + d) % LANES, 1), pack)
        if e == 0:
            pl.semaphore_wait(
                barrier,
                len(partners) + a_away.astype(jnp.int32) + b_away.astype(jnp.int32),
            )

        fold = copy_to(
            turned.at[e, :, pl.ds(0, d * LANES)],
            buf.at[pl.ds(C, C), pl.ds(CELLS, d * LANES)],
            ex_send.at[e, 4],
            ex_recv.at[e, 4],
            mirror,
        )
        fold.start()
        for r in range(ROWS):
            at = 2 * d * r
            here = jnp.logical_and(lane >= at, lane < at + 2 * d)
            row = buf[C : 2 * C, columns(r)].astype(F32)
            pack = jnp.where(here, pltpu.roll(row, (at + d) % LANES, 1), pack)
        packed[e] = pack.astype(BF)
        copies = []
        for slot, target in enumerate((east, west, fold_a, fold_b)):
            copies.append(
                copy_to(
                    packed.at[e],
                    rims.at[e, slot],
                    ex_send.at[e, slot],
                    ex_recv.at[e, slot],
                    target,
                )
            )
        copies[0].start()
        copies[1].start()
        start_if(a_away, copies[2])
        start_if(b_away, copies[3])
        sends.append((None, fold))
        sends.append((None, copies[0]))
        sends.append((None, copies[1]))
        sends.append((a_away, copies[2]))
        sends.append((b_away, copies[3]))
        return copies, fold

    def receive_rims(e, buf, d, waits):
        copies, fold = waits
        copies[0].wait_recv()
        copies[1].wait_recv()
        for away, slot in ((a_away, 2), (b_away, 3)):

            @pl.when(away)
            def _():
                copies[slot].wait_recv()

            @pl.when(jnp.logical_not(away))
            def _():
                rims[e, slot] = packed[e]

        fold.wait_recv()
        low = lax.rem(lane, 2 * d) < d
        rim = [rims[e, slot].astype(F32) for slot in range(4)]
        rim = jnp.where(
            lane < 2 * d * ROWS, jnp.where(low, rim[0], rim[1]), jnp.where(low, rim[2], rim[3])
        )
        for r in range(ROWS + d):
            row = buf[C : 2 * C, columns(r)].astype(F32)
            edge = pltpu.roll(rim, (-(2 * d * r + d)) % LANES, 1)
            buf[0:C, columns(r)] = pltpu.roll(
                jnp.where(lane >= LANES - d, edge, row), d, 1
            ).astype(BF)
            buf[2 * C : 3 * C, columns(r)] = pltpu.roll(
                jnp.where(lane < d, edge, row), LANES - d, 1
            ).astype(BF)

    def all_reduce(l):
        axis_a, axis_b, axis_c = ORDERS[l]
        place_a, place_b, place_c = (coordinate(me, axis) for axis in ORDERS[l])
        half = pl.ds(pl.multiple_of(core * HALF, LANES), HALF)
        other = pl.ds(pl.multiple_of((1 - core) * HALF, LANES), HALF)
        band = pl.ds(pl.multiple_of(place_a * BAND, 16), BAND)
        count = [0]

        def post(src, dst, target):
            number = count[0]
            count[0] += 1
            copy = copy_to(src, dst, ar_send.at[l, number], ar_recv.at[l, number], target)
            copy.start()
            sends.append((None, copy))
            return copy

        def around(axis, place):
            for step in (1, 2, 3):
                to = lax.rem(place + step, 4)
                yield step - 1, to, with_coordinate(me, axis, to)

        to_mate[l] = partial[l, :, other].astype(BF)
        copy = post(to_mate.at[l], from_mate.at[l], mate)
        yield
        copy.wait_recv()
        a_out[l] = (partial[l, :, half] + from_mate[l].astype(F32)).astype(BF)
        copies = [
            post(
                a_out.at[l, pl.ds(pl.multiple_of(to * BAND, 16), BAND)], a_in.at[l, slot], target
            )
            for slot, to, target in around(axis_a, place_a)
        ]
        yield
        for copy in copies:
            copy.wait_recv()
        total = a_out[l, band].astype(F32)
        for slot in range(3):
            total = total + a_in[l, slot].astype(F32)
        b_out[l] = total.astype(BF)
        copies = [
            post(
                b_out.at[l, :, pl.ds(pl.multiple_of(to * PART, LANES), PART)],
                b_in.at[l, slot],
                target,
            )
            for slot, to, target in around(axis_b, place_b)
        ]
        yield
        for copy in copies:
            copy.wait_recv()
        total = b_out[l, :, pl.ds(pl.multiple_of(place_b * PART, LANES), PART)].astype(F32)
        for slot in range(3):
            total = total + b_in[l, slot].astype(F32)
        c_in[l, place_c] = total.astype(BF)
        copies = [
            post(c_in.at[l, place_c], c_in.at[l, place_c], target)
            for slot, to, target in around(axis_c, place_c)
        ]
        yield
        for copy in copies:
            copy.wait_recv()
        total = c_in[l, 0].astype(F32)
        for slot in range(1, 4):
            total = total + c_in[l, slot].astype(F32)
        mine = pl.ds(pl.multiple_of(core * HALF + place_b * PART, LANES), PART)
        full[l, band, mine] = total.astype(BF)
        copies = [
            post(full.at[l, band, mine], full.at[l, band, mine], target)
            for slot, to, target in around(axis_b, place_b)
        ]
        yield
        for copy in copies:
            copy.wait_recv()
        final = [post(full.at[l, band, half], full.at[l, band, half], mate)]
        copies = [
            post(full.at[l, band, half], full.at[l, band, half], target)
            for slot, to, target in around(axis_a, place_a)
        ]
        yield
        for step, copy in enumerate(copies):
            copy.wait_recv()
            source = lax.rem(place_a + 3 - step, 4)
            piece = full.at[l, pl.ds(pl.multiple_of(source * BAND, 16), BAND), half]
            final.append(post(piece, piece, mate))
        yield
        for copy in final:
            copy.wait_recv()
        dw_ref[l] = full[l]
        yield

    forward_buffers = (s0, s1, s2)
    backward_buffers = (t0, t1, t2)

    spread_rows[...] = x_ref[...].astype(F32).reshape(C * ROWS, LANES)
    for r in range(ROWS):
        row = spread_rows[pl.ds(r, C, stride=ROWS), :]
        s0[C : 2 * C, columns(r)] = (row * mask).astype(BF)

    for l in range(3):
        d = 2**l
        buf = forward_buffers[l]
        waits = send_rims(l, buf, d, True)
        for a in range(3):
            for b in range(3):
                tap = w_ref[l, 3 * a + b]
                wf[l, a, :, b * C : (b + 1) * C] = tap
                wt[l, a, :, (2 - b) * C : (3 - b) * C] = tap.T
        if l > 0:
            v = slope[l - 1]
            s = jax.nn.sigmoid(v)
            slope[l - 1] = s * (1.0 + v * (1.0 - s))
        receive_rims(l, buf, d, waits)
        acc[...] = dot(wf[l, 1], buf[:, 0:CELLS]) + bias_cols[l]
        acc[...] += dot(wf[l, 2], buf[:, d * LANES : CELLS + d * LANES])
        acc[:, d * LANES : CELLS] += dot(wf[l, 0], buf[:, 0 : CELLS - d * LANES])
        v = acc[...]
        slope[l] = v
        after = (
            mask * (buf[C : 2 * C, 0:CELLS].astype(F32) + v * jax.nn.sigmoid(v))
        ).astype(BF)
        if l < 2:
            forward_buffers[l + 1][C : 2 * C, 0:CELLS] = after
        else:
            for r in range(ROWS):
                out_ref[r] = after[:, columns(r)]

    v = slope[2]
    s = jax.nn.sigmoid(v)
    slope[2] = s * (1.0 + v * (1.0 - s))
    spread_rows[...] = ct_ref[...].astype(F32).reshape(C * ROWS, LANES)
    for r in range(ROWS):
        grad[:, columns(r)] = mask * spread_rows[pl.ds(r, C, stride=ROWS), :]

    running = []
    for l in (2, 1, 0):
        d = 2**l
        stored = forward_buffers[l]
        buf = backward_buffers[l]
        delta = (grad[...] * slope[l]).astype(BF)
        buf[C : 2 * C, 0:CELLS] = delta
        waits = send_rims(5 - l, buf, d, False)
        for reduction in running:
            next(reduction)
        partial[l, :, 512:640] = jnp.zeros((C, LANES), F32)
        partial[l, :, 1152:1280] = jnp.zeros((C, LANES), F32)
        partial[l, :, 1792:1920] = jnp.zeros((C, LANES), F32)
        partial[l, :, 0:576] = dot_nt(
            buf[C : 2 * C, d * LANES : CELLS], stored[:, 0 : CELLS - d * LANES]
        )
        partial[l, :, 640:1216] = dot_nt(buf[C : 2 * C, 0:CELLS], stored[:, 0:CELLS])
        partial[l, :, 1280:1856] = dot_nt(
            buf[C : 2 * C, 0:CELLS], stored[:, d * LANES : CELLS + d * LANES]
        )
        partial[l, :, 1920:2048] = jnp.broadcast_to(
            jnp.sum(buf[C : 2 * C, 0:CELLS].astype(F32), axis=1, keepdims=True), (C, LANES)
        )
        reduction = all_reduce(l)
        next(reduction)
        running.append(reduction)
        receive_rims(5 - l, buf, d, waits)
        rest = CELLS - d * LANES
        acc[...] = dot(wt[l, 1], buf[:, 0:CELLS])
        acc[:, d * LANES : CELLS] += dot(wt[l, 2], buf[:, 0:rest])
        acc[:, 0:rest] += dot(wt[l, 0], buf[:, d * LANES : CELLS])
        over = dot(wt[l, 2, :, 0:C], buf[2 * C : 3 * C, CELLS : CELLS + d * LANES])
        over += dot(wt[l, 2, :, C : 2 * C], buf[C : 2 * C, CELLS : CELLS + d * LANES])
        over += dot(wt[l, 2, :, 2 * C : 3 * C], buf[0:C, CELLS : CELLS + d * LANES])
        acc[:, rest:CELLS] += flip_sign * over
        grad[...] = mask * (grad[...] + acc[...])

    for r in range(ROWS):
        fg_ref[r] = grad[:, columns(r)].astype(BF)
    done = object()
    while running:
        running = [reduction for reduction in running if next(reduction, done) is not done]
    for condition, copy in sends:
        if condition is None:
            copy.wait_send()
        else:

            @pl.when(condition)
            def _():
                copy.wait_send()


def finish(rows_a, rows_b, summed, out_a, out_b, kernel_grad, bias_grad, spread_rows, bias_rows):
    l = pl.program_id(0)
    for a in range(3):
        for b in range(3):
            first = a * WIDE + b * C
            kernel_grad[0, 3 * a + b] = summed[0, :, first : first + C].astype(F32)
    bias_rows[pl.ds(l, 1), :] = summed[0, :, 3 * WIDE : TOTAL].astype(F32).T[0:1]
    bias_grad[...] = bias_rows[0:3]
    for step, rows, out in ((0, rows_a, out_a), (1, rows_b, out_b)):

        @pl.when(l == step)
        def _():
            for r in range(ROWS):
                spread_rows[pl.ds(r, C, stride=ROWS), :] = rows[r].astype(F32)
            out[...] = spread_rows[...].reshape(C, ROWS, LANES).astype(BF)


def shards(fields, cotangent, weights, biases, ocean_tiles, velocity_mask):
    n = lax.axis_size("tiles")
    vmem = pl.BlockSpec(memory_space=pltpu.VMEM)
    out, field_grad, summed = pl.pallas_call(
        functools.partial(kernel, n),
        out_shape=(
            jax.ShapeDtypeStruct((ROWS, C, LANES), BF),
            jax.ShapeDtypeStruct((ROWS, C, LANES), BF),
            jax.ShapeDtypeStruct((3, C, TOTAL), BF),
        ),
        in_specs=[vmem] * 4 + [pl.BlockSpec(memory_space=pltpu.SMEM), vmem],
        out_specs=(vmem,) * 3,
        scratch_shapes=[
            pltpu.VMEM((3 * C, CELLS + LANES), BF),
            pltpu.VMEM((3 * C, CELLS + 2 * LANES), BF),
            pltpu.VMEM((3 * C, CELLS + 4 * LANES), BF),
            pltpu.VMEM((3 * C, CELLS + LANES), BF),
            pltpu.VMEM((3 * C, CELLS + 2 * LANES), BF),
            pltpu.VMEM((3 * C, CELLS + 4 * LANES), BF),
            pltpu.VMEM((C * ROWS, LANES), F32),
            pltpu.VMEM((LANES, 2 * LANES), F32),
            pltpu.VMEM((3, C, CELLS), F32),
            pltpu.VMEM((C, CELLS), F32),
            pltpu.VMEM((C, CELLS), F32),
            pltpu.VMEM((3, 3, C, 3 * C), BF),
            pltpu.VMEM((3, 3, C, 3 * C), BF),
            pltpu.VMEM((6, C, LANES), BF),
            pltpu.VMEM((6, C, 4 * LANES), BF),
            pltpu.VMEM((6, 4, C, LANES), BF),
            pltpu.VMEM((3, C, TOTAL), F32),
            pltpu.VMEM((3, C, HALF), BF),
            pltpu.VMEM((3, C, HALF), BF),
            pltpu.VMEM((3, C, HALF), BF),
            pltpu.VMEM((3, 3, BAND, HALF), BF),
            pltpu.VMEM((3, BAND, HALF), BF),
            pltpu.VMEM((3, 3, BAND, PART), BF),
            pltpu.VMEM((3, 4, BAND, PART), BF),
            pltpu.VMEM((3, C, TOTAL), BF),
            pltpu.SemaphoreType.DMA((6, 5)),
            pltpu.SemaphoreType.DMA((6, 5)),
            pltpu.SemaphoreType.DMA((3, 20)),
            pltpu.SemaphoreType.DMA((3, 20)),
        ],
        compiler_params=pltpu.CompilerParams(
            collective_id=0, has_side_effects=True, vmem_limit_bytes=56 * 1024 * 1024
        ),
        cost_estimate=pl.CostEstimate(
            flops=18 * 9 * C * C * CELLS, bytes_accessed=8 * 1024 * 1024, transcendentals=9 * C * CELLS
        ),
    )(fields, cotangent, weights, biases, ocean_tiles, velocity_mask)
    whole = lambda *shape: pl.BlockSpec(shape, lambda l: (0,) * len(shape))
    return pl.pallas_call(
        finish,
        grid=(3,),
        out_shape=(
            jax.ShapeDtypeStruct((C, ROWS, LANES), BF),
            jax.ShapeDtypeStruct((C, ROWS, LANES), BF),
            jax.ShapeDtypeStruct((3, 9, C, C), F32),
            jax.ShapeDtypeStruct((3, C), F32),
        ),
        in_specs=[
            whole(ROWS, C, LANES),
            whole(ROWS, C, LANES),
            pl.BlockSpec((1, C, TOTAL), lambda l: (l, 0, 0)),
        ],
        out_specs=(
            whole(C, ROWS, LANES),
            whole(C, ROWS, LANES),
            pl.BlockSpec((1, 9, C, C), lambda l: (l, 0, 0, 0)),
            whole(3, C),
        ),
        scratch_shapes=[pltpu.VMEM((C * ROWS, LANES), F32), pltpu.VMEM((8, C), F32)],
        compiler_params=pltpu.CompilerParams(vmem_limit_bytes=32 * 1024 * 1024),
    )(out, field_grad, summed)


def solution(mesh):
    placed = (P(None, None, "tiles"), P(None, None, "tiles"), P(), P(), P(None, "tiles"), P())
    return jax.shard_map(
        shards,
        mesh=mesh,
        in_specs=placed,
        out_specs=(P(None, None, "tiles"), P(None, None, "tiles"), P(), P()),
        check_vma=False,
    )
```

```python
import functools

import jax
import jax.numpy as jnp
from jax import lax
from jax.experimental import pallas as pl
from jax.experimental.pallas import tpu as pltpu
from jax.sharding import PartitionSpec as P

C = 192
ROWS = 8
LANES = 128
CELLS = ROWS * LANES
WIDE = 640
TOTAL = 2048
HALF = TOTAL // 2
BAND = C // 4
PART = HALF // 4
BF = jnp.bfloat16
F32 = jnp.float32
MESH = pl.DeviceIdType.MESH

CORE = (1, 2)
Y = (2, 4)
X = (8, 4)
Z = (32, 4)
ORDERS = ((Y, X, Z), (Z, Y, X), (X, Z, Y))


def coordinate(me, axis):
    return lax.rem(lax.div(me, axis[0]), axis[1])


def with_coordinate(me, axis, value):
    return me + (value - coordinate(me, axis)) * axis[0]


def copy_to(src, dst, send_sem, recv_sem, device):
    return pltpu.make_async_remote_copy(
        src_ref=src,
        dst_ref=dst,
        send_sem=send_sem,
        recv_sem=recv_sem,
        device_id=(device,),
        device_id_type=MESH,
    )


def start_if(condition, copy):
    @pl.when(condition)
    def _():
        copy.start()


def dot(a, b):
    return jnp.dot(a, b, preferred_element_type=F32)


def dot_nt(a, b):
    return lax.dot_general(a, b, (((1,), (1,)), ((), ())), preferred_element_type=F32)


def kernel(
    n,
    x_ref,
    ct_ref,
    w_hbm,
    bias_ref,
    ocean_ref,
    velocity_ref,
    out_ref,
    fg_ref,
    dw_ref,
    s0,
    s1,
    s2,
    t0,
    t1,
    t2,
    w_ref,
    spread_rows,
    cols_ref,
    slope,
    acc,
    grad,
    w_side,
    v_mid,
    v_side,
    v_over,
    packed,
    corner,
    turned,
    rims,
    corners,
    partial,
    to_mate,
    from_mate,
    a_out,
    a_in,
    b_out,
    b_in,
    c_in,
    full,
    w_sem,
    ex_send,
    ex_recv,
    ar_send,
    ar_recv,
):
    me = lax.axis_index("tiles")
    east = lax.rem(me + 1, n)
    west = lax.rem(me + n - 1, n)
    mirror = n - 1 - me
    fold_a = lax.rem(n - me, n)
    fold_b = lax.rem(2 * n - 2 - me, n)
    mate = with_coordinate(me, CORE, 1 - coordinate(me, CORE))
    core = coordinate(me, CORE)
    a_away = fold_a != me
    b_away = fold_b != me

    barrier = pltpu.get_barrier_semaphore()
    partners = [east, west, mirror, mate]
    for axis in (Y, X, Z):
        for step in (1, 2, 3):
            partners.append(
                with_coordinate(me, axis, lax.rem(coordinate(me, axis) + step, axis[1]))
            )
    for partner in partners:
        pl.semaphore_signal(barrier, inc=1, device_id=(partner,), device_id_type=MESH)

    @pl.when(a_away)
    def _():
        pl.semaphore_signal(barrier, inc=1, device_id=(fold_a,), device_id_type=MESH)

    @pl.when(b_away)
    def _():
        pl.semaphore_signal(barrier, inc=1, device_id=(fold_b,), device_id_type=MESH)

    loads = [
        pltpu.make_async_copy(w_hbm.at[l], w_ref.at[l], w_sem.at[l]) for l in range(3)
    ]
    for load in loads:
        load.start()

    lane = lax.broadcasted_iota(jnp.int32, (C, LANES), 1)
    flip_matrix = (
        lax.broadcasted_iota(jnp.int32, (LANES, LANES), 0)
        + lax.broadcasted_iota(jnp.int32, (LANES, LANES), 1)
        == LANES - 1
    ).astype(F32).astype(BF)
    cols_ref[...] = jnp.zeros((LANES, 2 * LANES), F32)
    cols_ref[0:3, 0:C] = bias_ref[...]
    cols_ref[3:4, 0:C] = (1 - 2 * velocity_ref[...]).astype(F32).reshape(1, C)
    turned_cols = cols_ref[...].T[0:C]
    bias_cols = [turned_cols[:, l : l + 1] for l in range(3)]
    flip_sign = turned_cols[:, 3:4]
    mask = ocean_ref[0, 0].astype(F32)
    sends = []

    def columns(row, count=1):
        return slice(row * LANES, (row + count) * LANES)

    class Rims:
        def __init__(self, e, buf, d, signed):
            self.e, self.buf, self.d, self.signed = e, buf, d, signed
            self.folds = []

        def turn(self, first, last):
            for k in range(first, last):
                row = dot(self.buf[0:C, columns(ROWS - 1 - k)], flip_matrix)
                if self.signed:
                    row = row * flip_sign
                turned[self.e, :, columns(k)] = row.astype(BF)

        def send_fold(self, first, last):
            slot = 4 + len(self.folds)
            fold = copy_to(
                turned.at[self.e, :, pl.ds(first * LANES, (last - first) * LANES)],
                self.buf.at[pl.ds(0, C), pl.ds(CELLS + first * LANES, (last - first) * LANES)],
                ex_send.at[self.e, slot],
                ex_recv.at[self.e, slot],
                mirror,
            )
            fold.start()
            self.folds.append(fold)
            sends.append((None, fold))

        def pack(self, rows, count):
            d = self.d
            tile = jnp.zeros((C, LANES), F32)
            for r in range(count):
                at = 2 * d * r
                here = jnp.logical_and(lane >= at, lane < at + 2 * d)
                tile = jnp.where(here, pltpu.roll(rows(r).astype(F32), (at + d) % LANES, 1), tile)
            return tile

        def pack_sides(self):
            tile = self.pack(lambda r: self.buf[0:C, columns(r)], ROWS)
            packed[self.e] = tile.astype(BF)

        def pack_corners(self):
            tile = self.pack(lambda k: turned[self.e, :, columns(k)], self.d)
            dense = tile[0:BAND]
            for q in range(1, 4):
                dense = dense + pltpu.roll(tile[q * BAND : (q + 1) * BAND], 32 * q, 1)
            corner[self.e] = dense.astype(BF)

        def send_sides(self):
            self.sides = []
            for slot, target in enumerate((east, west)):
                copy = copy_to(
                    packed.at[self.e],
                    rims.at[self.e, slot],
                    ex_send.at[self.e, slot],
                    ex_recv.at[self.e, slot],
                    target,
                )
                copy.start()
                self.sides.append(copy)
                sends.append((None, copy))

        def send_corners(self):
            self.turns = []
            for slot, target, away in ((0, fold_a, a_away), (1, fold_b, b_away)):
                copy = copy_to(
                    corner.at[self.e],
                    corners.at[self.e, slot],
                    ex_send.at[self.e, 2 + slot],
                    ex_recv.at[self.e, 2 + slot],
                    target,
                )
                start_if(away, copy)
                self.turns.append((away, copy))
                sends.append((away, copy))

        def unpack(self, rim, row, slot):
            buf, d = self.buf, self.d
            center = buf[0:C, columns(row)].astype(F32)
            edge = pltpu.roll(rim, (-(2 * d * slot + d)) % LANES, 1)
            left = pltpu.roll(jnp.where(lane >= LANES - d, edge, center), d, 1)
            right = pltpu.roll(jnp.where(lane < d, edge, center), LANES - d, 1)
            buf[C : 2 * C, columns(row)] = left.astype(BF)
            buf[2 * C : 3 * C, columns(row)] = right.astype(BF)

        def receive_sides(self):
            for copy in self.sides:
                copy.wait_recv()
            low = lax.rem(lane, 2 * self.d) < self.d
            rim = jnp.where(
                low, rims[self.e, 0].astype(F32), rims[self.e, 1].astype(F32)
            )
            for r in range(ROWS):
                self.unpack(rim, r, r)

        def receive_fold(self):
            for slot, (away, copy) in enumerate(self.turns):

                @pl.when(away)
                def _():
                    copy.wait_recv()

                @pl.when(jnp.logical_not(away))
                def _():
                    corners[self.e, slot] = corner[self.e]

            for fold in self.folds:
                fold.wait_recv()
            low = lax.rem(lane, 2 * self.d) < self.d
            tiles = []
            for slot in range(2):
                dense = corners[self.e, slot].astype(F32)
                tiles.append(
                    jnp.concatenate(
                        [dense] + [pltpu.roll(dense, LANES - 32 * q, 1) for q in range(1, 4)],
                        axis=0,
                    )
                )
            rim = jnp.where(low, tiles[0], tiles[1])
            for k in range(self.d):
                self.unpack(rim, ROWS + k, k)

    def all_reduce(l):
        axis_a, axis_b, axis_c = ORDERS[l]
        place_a, place_b, place_c = (coordinate(me, axis) for axis in ORDERS[l])
        half = pl.ds(pl.multiple_of(core * HALF, LANES), HALF)
        other = pl.ds(pl.multiple_of((1 - core) * HALF, LANES), HALF)
        band = pl.ds(pl.multiple_of(place_a * BAND, 16), BAND)
        count = [0]

        def post(src, dst, target):
            number = count[0]
            count[0] += 1
            copy = copy_to(src, dst, ar_send.at[l, number], ar_recv.at[l, number], target)
            copy.start()
            sends.append((None, copy))
            return copy

        def around(axis, place):
            for step in (1, 2, 3):
                to = lax.rem(place + step, 4)
                yield step - 1, to, with_coordinate(me, axis, to)

        to_mate[l] = partial[l, :, other].astype(BF)
        copy = post(to_mate.at[l], from_mate.at[l], mate)
        yield
        copy.wait_recv()
        a_out[l] = (partial[l, :, half] + from_mate[l].astype(F32)).astype(BF)
        copies = [
            post(
                a_out.at[l, pl.ds(pl.multiple_of(to * BAND, 16), BAND)], a_in.at[l, slot], target
            )
            for slot, to, target in around(axis_a, place_a)
        ]
        yield
        for copy in copies:
            copy.wait_recv()
        total = a_out[l, band].astype(F32)
        for slot in range(3):
            total = total + a_in[l, slot].astype(F32)
        b_out[l] = total.astype(BF)
        copies = [
            post(
                b_out.at[l, :, pl.ds(pl.multiple_of(to * PART, LANES), PART)],
                b_in.at[l, slot],
                target,
            )
            for slot, to, target in around(axis_b, place_b)
        ]
        yield
        for copy in copies:
            copy.wait_recv()
        total = b_out[l, :, pl.ds(pl.multiple_of(place_b * PART, LANES), PART)].astype(F32)
        for slot in range(3):
            total = total + b_in[l, slot].astype(F32)
        c_in[l, place_c] = total.astype(BF)
        copies = [
            post(c_in.at[l, place_c], c_in.at[l, place_c], target)
            for slot, to, target in around(axis_c, place_c)
        ]
        yield
        for copy in copies:
            copy.wait_recv()
        total = c_in[l, 0].astype(F32)
        for slot in range(1, 4):
            total = total + c_in[l, slot].astype(F32)
        mine = pl.ds(pl.multiple_of(core * HALF + place_b * PART, LANES), PART)
        full[l, band, mine] = total.astype(BF)
        copies = [
            post(full.at[l, band, mine], full.at[l, band, mine], target)
            for slot, to, target in around(axis_b, place_b)
        ]
        yield
        for copy in copies:
            copy.wait_recv()
        copies = [
            post(full.at[l, band, half], full.at[l, band, half], target)
            for slot, to, target in around(axis_a, place_a)
        ]
        final = [post(full.at[l, band, half], full.at[l, band, half], mate)]
        yield
        for step, copy in enumerate(copies):
            copy.wait_recv()
            source = lax.rem(place_a + 3 - step, 4)
            piece = full.at[l, pl.ds(pl.multiple_of(source * BAND, 16), BAND), half]
            final.append(post(piece, piece, mate))
        yield
        for copy in final:
            copy.wait_recv()
        dw_ref[l] = full[l]
        yield

    def prepare_forward(l):
        for a in range(3):
            w_side[l, a, :, 0:C] = w_ref[l, 3 * a]
            w_side[l, a, :, C : 2 * C] = w_ref[l, 3 * a + 2]

    def prepare_backward(l):
        for a in range(3):
            v_mid[l, a] = w_ref[l, 3 * a + 1].T
            v_side[l, a, :, 0:C] = w_ref[l, 3 * a + 2].T
            v_side[l, a, :, C : 2 * C] = w_ref[l, 3 * a].T
        for place, tap in enumerate((7, 6, 8)):
            v_over[l, :, place * C : (place + 1) * C] = (
                w_ref[l, tap].T.astype(F32) * flip_sign
            ).astype(BF)

    forward_buffers = (s0, s1, s2)
    backward_buffers = (t0, t1, t2)

    spread_rows[...] = x_ref[...].astype(F32).reshape(C * ROWS, LANES)
    for r in range(ROWS):
        row = spread_rows[pl.ds(r, C, stride=ROWS), :]
        s0[0:C, columns(r)] = (row * mask).astype(BF)
    rim = Rims(0, s0, 1, True)
    rim.turn(0, 1)
    rim.pack_sides()
    rim.pack_corners()
    loads[0].wait()
    prepare_forward(0)
    spread_rows[...] = ct_ref[...].astype(F32).reshape(C * ROWS, LANES)
    for r in range(ROWS):
        grad[:, columns(r)] = mask * spread_rows[pl.ds(r, C, stride=ROWS), :]
    loads[1].wait()
    loads[2].wait()
    pl.semaphore_wait(
        barrier, len(partners) + a_away.astype(jnp.int32) + b_away.astype(jnp.int32)
    )
    rim.send_fold(0, 1)
    rim.send_corners()
    rim.send_sides()

    for l in range(3):
        d = 2**l
        rest = CELLS - d * LANES
        buf = forward_buffers[l]
        acc[...] = dot(w_ref[l, 4], buf[0:C, 0:CELLS]) + bias_cols[l]
        acc[:, 0:rest] += dot(w_ref[l, 7], buf[0:C, d * LANES : CELLS])
        acc[:, d * LANES : CELLS] += dot(w_ref[l, 1], buf[0:C, 0:rest])
        if l < 2:
            prepare_forward(l + 1)
        prepare_backward(2 - l)
        rim.receive_sides()
        acc[...] += dot(w_side[l, 1], buf[C : 3 * C, 0:CELLS])
        acc[:, 0:rest] += dot(w_side[l, 2], buf[C : 3 * C, d * LANES : CELLS])
        acc[:, d * LANES : CELLS] += dot(w_side[l, 0], buf[C : 3 * C, 0:rest])

        def activate(first, last):
            v = acc[:, first:last]
            s = jax.nn.sigmoid(v)
            after = mask * (buf[0:C, first:last].astype(F32) + v * s)
            s = s * (1.0 + v * (1.0 - s))
            slope[l, :, first:last] = s
            if l < 2:
                forward_buffers[l + 1][0:C, first:last] = after.astype(BF)
            else:
                for r in range(first // LANES, last // LANES):
                    out_ref[r] = after[:, r * LANES - first : (r + 1) * LANES - first].astype(BF)
                t2[0:C, first:last] = (grad[:, first:last] * s).astype(BF)

        activate(0, rest)
        if l < 2:
            later = Rims(l + 1, forward_buffers[l + 1], 2 * d, True)
            later.turn(d, 2 * d)
            later.send_fold(d, 2 * d)
        else:
            later = Rims(3, t2, d, False)
        rim.receive_fold()
        acc[:, rest:CELLS] += dot(w_ref[l, 7], buf[0:C, CELLS : CELLS + d * LANES]) + dot(
            w_side[l, 2], buf[C : 3 * C, CELLS : CELLS + d * LANES]
        )
        activate(rest, CELLS)
        rim = later
        rim.turn(0, d)
        rim.send_fold(0, d)
        rim.pack_corners()
        rim.send_corners()
        rim.pack_sides()
        rim.send_sides()

    running = []
    for l in (2, 1, 0):
        d = 2**l
        rest = CELLS - d * LANES
        stored = forward_buffers[l]
        buf = backward_buffers[l]
        for reduction in running:
            next(reduction)
        partial[l, :, 512:640] = jnp.zeros((C, LANES), F32)
        partial[l, :, 1152:1280] = jnp.zeros((C, LANES), F32)
        partial[l, :, 1792:1920] = jnp.zeros((C, LANES), F32)
        partial[l, :, 0:576] = dot_nt(buf[0:C, d * LANES : CELLS], stored[:, 0:rest])
        partial[l, :, 640:1216] = dot_nt(buf[0:C, 0:CELLS], stored[:, 0:CELLS])
        partial[l, :, 1280:1856] = dot_nt(
            buf[0:C, 0:CELLS], stored[:, d * LANES : CELLS + d * LANES]
        )
        partial[l, :, 1920:2048] = jnp.broadcast_to(
            jnp.sum(buf[0:C, 0:CELLS].astype(F32), axis=1, keepdims=True), (C, LANES)
        )
        reduction = all_reduce(l)
        next(reduction)
        running.append(reduction)
        acc[...] = dot(v_mid[l, 1], buf[0:C, 0:CELLS])
        acc[:, d * LANES : CELLS] += dot(v_mid[l, 2], buf[0:C, 0:rest])
        acc[:, 0:rest] += dot(v_mid[l, 0], buf[0:C, d * LANES : CELLS])
        rim.receive_sides()
        acc[...] += dot(v_side[l, 1], buf[C : 3 * C, 0:CELLS])
        acc[:, d * LANES : CELLS] += dot(v_side[l, 2], buf[C : 3 * C, 0:rest])
        acc[:, 0:rest] += dot(v_side[l, 0], buf[C : 3 * C, d * LANES : CELLS])

        def descend(first, last):
            g = mask * (grad[:, first:last] + acc[:, first:last])
            if l > 0:
                grad[:, first:last] = g
                backward_buffers[l - 1][0:C, first:last] = (
                    g * slope[l - 1, :, first:last]
                ).astype(BF)
            else:
                for r in range(first // LANES, last // LANES):
                    fg_ref[r] = g[:, r * LANES - first : (r + 1) * LANES - first].astype(BF)

        descend(0, rest)
        for reduction in running:
            next(reduction)
        rim.receive_fold()
        acc[:, rest:CELLS] += dot(v_over[l], buf[:, CELLS : CELLS + d * LANES])
        descend(rest, CELLS)
        if l > 0:
            rim = Rims(6 - l, backward_buffers[l - 1], d // 2, False)
            rim.turn(0, d // 2)
            rim.send_fold(0, d // 2)
            rim.pack_corners()
            rim.send_corners()
            rim.pack_sides()
            rim.send_sides()

    done = object()
    while running:
        running = [reduction for reduction in running if next(reduction, done) is not done]
    for condition, copy in sends:
        if condition is None:
            copy.wait_send()
        else:

            @pl.when(condition)
            def _():
                copy.wait_send()


def finish(rows_a, rows_b, summed, out_a, out_b, kernel_grad, bias_grad, spread_rows, bias_rows):
    l = pl.program_id(0)
    for a in range(3):
        for b in range(3):
            first = a * WIDE + (1, 0, 2)[b] * C
            kernel_grad[0, 3 * a + b] = summed[0, :, first : first + C].astype(F32)
    bias_rows[pl.ds(l, 1), :] = summed[0, :, 3 * WIDE : TOTAL].astype(F32).T[0:1]
    bias_grad[...] = bias_rows[0:3]
    for step, rows, out in ((0, rows_a, out_a), (1, rows_b, out_b)):

        @pl.when(l == step)
        def _():
            for r in range(ROWS):
                spread_rows[pl.ds(r, C, stride=ROWS), :] = rows[r].astype(F32)
            out[...] = spread_rows[...].reshape(C, ROWS, LANES).astype(BF)


def shards(fields, cotangent, weights, biases, ocean_tiles, velocity_mask):
    n = lax.axis_size("tiles")
    vmem = pl.BlockSpec(memory_space=pltpu.VMEM)
    out, field_grad, summed = pl.pallas_call(
        functools.partial(kernel, n),
        out_shape=(
            jax.ShapeDtypeStruct((ROWS, C, LANES), BF),
            jax.ShapeDtypeStruct((ROWS, C, LANES), BF),
            jax.ShapeDtypeStruct((3, C, TOTAL), BF),
        ),
        in_specs=[
            vmem,
            vmem,
            pl.BlockSpec(memory_space=pl.ANY),
            vmem,
            pl.BlockSpec(memory_space=pltpu.SMEM),
            vmem,
        ],
        out_specs=(vmem,) * 3,
        scratch_shapes=[
            pltpu.VMEM((3 * C, CELLS + LANES), BF),
            pltpu.VMEM((3 * C, CELLS + 2 * LANES), BF),
            pltpu.VMEM((3 * C, CELLS + 4 * LANES), BF),
            pltpu.VMEM((3 * C, CELLS + LANES), BF),
            pltpu.VMEM((3 * C, CELLS + 2 * LANES), BF),
            pltpu.VMEM((3 * C, CELLS + 4 * LANES), BF),
            pltpu.VMEM((3, 9, C, C), BF),
            pltpu.VMEM((C * ROWS, LANES), F32),
            pltpu.VMEM((LANES, 2 * LANES), F32),
            pltpu.VMEM((3, C, CELLS), F32),
            pltpu.VMEM((C, CELLS), F32),
            pltpu.VMEM((C, CELLS), F32),
            pltpu.VMEM((3, 3, C, 2 * C), BF),
            pltpu.VMEM((3, 3, C, C), BF),
            pltpu.VMEM((3, 3, C, 2 * C), BF),
            pltpu.VMEM((3, C, 3 * C), BF),
            pltpu.VMEM((6, C, LANES), BF),
            pltpu.VMEM((6, BAND, LANES), BF),
            pltpu.VMEM((6, C, 4 * LANES), BF),
            pltpu.VMEM((6, 2, C, LANES), BF),
            pltpu.VMEM((6, 2, BAND, LANES), BF),
            pltpu.VMEM((3, C, TOTAL), F32),
            pltpu.VMEM((3, C, HALF), BF),
            pltpu.VMEM((3, C, HALF), BF),
            pltpu.VMEM((3, C, HALF), BF),
            pltpu.VMEM((3, 3, BAND, HALF), BF),
            pltpu.VMEM((3, BAND, HALF), BF),
            pltpu.VMEM((3, 3, BAND, PART), BF),
            pltpu.VMEM((3, 4, BAND, PART), BF),
            pltpu.VMEM((3, C, TOTAL), BF),
            pltpu.SemaphoreType.DMA((3,)),
            pltpu.SemaphoreType.DMA((6, 6)),
            pltpu.SemaphoreType.DMA((6, 6)),
            pltpu.SemaphoreType.DMA((3, 20)),
            pltpu.SemaphoreType.DMA((3, 20)),
        ],
        compiler_params=pltpu.CompilerParams(
            collective_id=0, has_side_effects=True, vmem_limit_bytes=48 * 1024 * 1024
        ),
        cost_estimate=pl.CostEstimate(
            flops=18 * 9 * C * C * CELLS, bytes_accessed=8 * 1024 * 1024, transcendentals=9 * C * CELLS
        ),
    )(fields, cotangent, weights, biases, ocean_tiles, velocity_mask)
    whole = lambda *shape: pl.BlockSpec(shape, lambda l: (0,) * len(shape))
    return pl.pallas_call(
        finish,
        grid=(3,),
        out_shape=(
            jax.ShapeDtypeStruct((C, ROWS, LANES), BF),
            jax.ShapeDtypeStruct((C, ROWS, LANES), BF),
            jax.ShapeDtypeStruct((3, 9, C, C), F32),
            jax.ShapeDtypeStruct((3, C), F32),
        ),
        in_specs=[
            whole(ROWS, C, LANES),
            whole(ROWS, C, LANES),
            pl.BlockSpec((1, C, TOTAL), lambda l: (l, 0, 0)),
        ],
        out_specs=(
            whole(C, ROWS, LANES),
            whole(C, ROWS, LANES),
            pl.BlockSpec((1, 9, C, C), lambda l: (l, 0, 0, 0)),
            whole(3, C),
        ),
        scratch_shapes=[pltpu.VMEM((C * ROWS, LANES), F32), pltpu.VMEM((8, C), F32)],
        compiler_params=pltpu.CompilerParams(vmem_limit_bytes=32 * 1024 * 1024),
    )(out, field_grad, summed)


def solution(mesh):
    placed = (P(None, None, "tiles"), P(None, None, "tiles"), P(), P(), P(None, "tiles"), P())
    return jax.shard_map(
        shards,
        mesh=mesh,
        in_specs=placed,
        out_specs=(P(None, None, "tiles"), P(None, None, "tiles"), P(), P()),
        check_vma=False,
    )
```

```python
import functools

import jax
import jax.numpy as jnp
from jax import lax
from jax.experimental import pallas as pl
from jax.experimental.pallas import tpu as pltpu
from jax.sharding import PartitionSpec as P

C = 192
ROWS = 8
LANES = 128
CELLS = ROWS * LANES
WIDE = 640
TOTAL = 2048
HALF = TOTAL // 2
BAND = C // 4
BF = jnp.bfloat16
F32 = jnp.float32
MESH = pl.DeviceIdType.MESH

CORE = (1, 2)
Y = (2, 4)
X = (8, 4)
Z = (32, 4)
PARTS = (
    (pl.ds(0, 384), (Y, X, Z)),
    (pl.ds(384, 384), (Z, Y, X)),
    (pl.ds(768, 256), (X, Z, Y)),
)


def coordinate(me, axis):
    return lax.rem(lax.div(me, axis[0]), axis[1])


def with_coordinate(me, axis, value):
    return me + (value - coordinate(me, axis)) * axis[0]


def copy_to(src, dst, send_sem, recv_sem, device):
    return pltpu.make_async_remote_copy(
        src_ref=src,
        dst_ref=dst,
        send_sem=send_sem,
        recv_sem=recv_sem,
        device_id=(device,),
        device_id_type=MESH,
    )


def start_if(condition, copy):
    @pl.when(condition)
    def _():
        copy.start()


def dot(a, b):
    return jnp.dot(a, b, preferred_element_type=F32)


def dot_nt(a, b):
    return lax.dot_general(a, b, (((1,), (1,)), ((), ())), preferred_element_type=F32)


def kernel(
    n,
    x_hbm,
    ct_hbm,
    w_hbm,
    bias_hbm,
    ocean_ref,
    velocity_hbm,
    out_hbm,
    fg_hbm,
    dw_hbm,
    s0,
    s1,
    s2,
    t0,
    t1,
    t2,
    x_ref,
    ct_ref,
    bias_ref,
    velocity_ref,
    w_ref,
    out_ref,
    fg_ref,
    spread_rows,
    cols_ref,
    slope,
    acc,
    grad,
    w_side,
    v_mid,
    v_side,
    v_over,
    packed,
    corner,
    turned,
    rims,
    corners,
    partial,
    to_mate,
    from_mate,
    a_out,
    a_in,
    b_in,
    c_in,
    full,
    w_sem,
    out_sem,
    ex_send,
    ex_recv,
    ar_send,
    ar_recv,
):
    me = lax.axis_index("tiles")
    east = lax.rem(me + 1, n)
    west = lax.rem(me + n - 1, n)
    mirror = n - 1 - me
    fold_a = lax.rem(n - me, n)
    fold_b = lax.rem(2 * n - 2 - me, n)
    mate = with_coordinate(me, CORE, 1 - coordinate(me, CORE))
    core = coordinate(me, CORE)
    a_away = fold_a != me
    b_away = fold_b != me

    barrier = pltpu.get_barrier_semaphore()
    partners = [east, west, mirror, mate]
    for axis in (Y, X, Z):
        for step in (1, 2, 3):
            partners.append(
                with_coordinate(me, axis, lax.rem(coordinate(me, axis) + step, axis[1]))
            )
    for partner in partners:
        pl.semaphore_signal(barrier, inc=1, device_id=(partner,), device_id_type=MESH)

    @pl.when(a_away)
    def _():
        pl.semaphore_signal(barrier, inc=1, device_id=(fold_a,), device_id_type=MESH)

    @pl.when(b_away)
    def _():
        pl.semaphore_signal(barrier, inc=1, device_id=(fold_b,), device_id_type=MESH)

    small = [
        pltpu.make_async_copy(src, dst, w_sem.at[3 + number])
        for number, (src, dst) in enumerate(
            (
                (bias_hbm, bias_ref),
                (velocity_hbm, velocity_ref),
                (x_hbm, x_ref),
                (ct_hbm, ct_ref),
            )
        )
    ]
    loads = [
        pltpu.make_async_copy(w_hbm.at[l], w_ref.at[l], w_sem.at[l]) for l in range(3)
    ]
    for load in small + loads:
        load.start()

    lane = lax.broadcasted_iota(jnp.int32, (C, LANES), 1)
    flip_matrix = (
        lax.broadcasted_iota(jnp.int32, (LANES, LANES), 0)
        + lax.broadcasted_iota(jnp.int32, (LANES, LANES), 1)
        == LANES - 1
    ).astype(F32).astype(BF)
    cols_ref[...] = jnp.zeros((LANES, 2 * LANES), F32)
    small[0].wait()
    small[1].wait()
    cols_ref[0:3, 0:C] = bias_ref[...]
    cols_ref[3:4, 0:C] = (1 - 2 * velocity_ref[...]).astype(F32).reshape(1, C)
    turned_cols = cols_ref[...].T[0:C]
    bias_cols = [turned_cols[:, l : l + 1] for l in range(3)]
    flip_sign = turned_cols[:, 3:4]
    mask = ocean_ref[0, 0].astype(F32)
    sends = []

    stores = []

    def store(src, dst):
        copy = pltpu.make_async_copy(src, dst, out_sem.at[len(stores)])
        copy.start()
        stores.append(copy)

    def columns(row, count=1):
        return slice(row * LANES, (row + count) * LANES)

    class Rims:
        def __init__(self, e, buf, d, signed):
            self.e, self.buf, self.d, self.signed = e, buf, d, signed
            self.folds = []

        def turn(self, first, last):
            for k in range(first, last):
                row = dot(self.buf[0:C, columns(ROWS - 1 - k)], flip_matrix)
                if self.signed:
                    row = row * flip_sign
                turned[self.e, :, columns(k)] = row.astype(BF)

        def send_fold(self, first, last):
            slot = 4 + len(self.folds)
            fold = copy_to(
                turned.at[self.e, :, pl.ds(first * LANES, (last - first) * LANES)],
                self.buf.at[pl.ds(0, C), pl.ds(CELLS + first * LANES, (last - first) * LANES)],
                ex_send.at[self.e, slot],
                ex_recv.at[self.e, slot],
                mirror,
            )
            fold.start()
            self.folds.append((fold, first, last))
            sends.append((None, fold))

        def pack(self, rows, count):
            d = self.d
            tile = jnp.zeros((C, LANES), F32)
            for r in range(count):
                at = 2 * d * r
                here = jnp.logical_and(lane >= at, lane < at + 2 * d)
                tile = jnp.where(here, pltpu.roll(rows(r).astype(F32), (at + d) % LANES, 1), tile)
            return tile

        def pack_sides(self):
            tile = self.pack(lambda r: self.buf[0:C, columns(r)], ROWS)
            packed[self.e] = tile.astype(BF)

        def pack_corners(self):
            tile = self.pack(lambda k: turned[self.e, :, columns(k)], self.d)
            dense = tile[0:BAND]
            for q in range(1, 4):
                dense = dense + pltpu.roll(tile[q * BAND : (q + 1) * BAND], 32 * q, 1)
            corner[self.e] = dense.astype(BF)

        def send_sides(self):
            self.sides = []
            for slot, target in enumerate((east, west)):
                copy = copy_to(
                    packed.at[self.e],
                    rims.at[self.e, slot],
                    ex_send.at[self.e, slot],
                    ex_recv.at[self.e, slot],
                    target,
                )
                copy.start()
                self.sides.append(copy)
                sends.append((None, copy))

        def send_corners(self):
            self.turns = []
            for slot, target, away in ((0, fold_a, a_away), (1, fold_b, b_away)):
                copy = copy_to(
                    corner.at[self.e],
                    corners.at[self.e, slot],
                    ex_send.at[self.e, 2 + slot],
                    ex_recv.at[self.e, 2 + slot],
                    target,
                )
                start_if(away, copy)
                self.turns.append((away, copy))
                sends.append((away, copy))

        def unpack(self, rim, row, slot):
            buf, d = self.buf, self.d
            center = buf[0:C, columns(row)].astype(F32)
            edge = pltpu.roll(rim, (-(2 * d * slot + d)) % LANES, 1)
            left = pltpu.roll(jnp.where(lane >= LANES - d, edge, center), d, 1)
            right = pltpu.roll(jnp.where(lane < d, edge, center), LANES - d, 1)
            buf[C : 2 * C, columns(row)] = left.astype(BF)
            buf[2 * C : 3 * C, columns(row)] = right.astype(BF)

        def receive_sides(self):
            for copy in self.sides:
                copy.wait_recv()
            low = lax.rem(lane, 2 * self.d) < self.d
            rim = jnp.where(
                low, rims[self.e, 0].astype(F32), rims[self.e, 1].astype(F32)
            )
            for r in range(ROWS):
                self.unpack(rim, r, r)

        def receive_corners(self):
            for slot, (away, copy) in enumerate(self.turns):

                @pl.when(away)
                def _():
                    copy.wait_recv()

                @pl.when(jnp.logical_not(away))
                def _():
                    corners[self.e, slot] = corner[self.e]

            low = lax.rem(lane, 2 * self.d) < self.d
            tiles = []
            for slot in range(2):
                dense = corners[self.e, slot].astype(F32)
                tiles.append(
                    jnp.concatenate(
                        [dense] + [pltpu.roll(dense, LANES - 32 * q, 1) for q in range(1, 4)],
                        axis=0,
                    )
                )
            self.rim = jnp.where(low, tiles[0], tiles[1])

        def receive_fold(self, number):
            fold, first, last = self.folds[number]
            fold.wait_recv()
            for k in range(first, last):
                self.unpack(self.rim, ROWS + k, k)

    def all_reduce(l):
        half = pl.ds(pl.multiple_of(core * HALF, LANES), HALF)
        other = pl.ds(pl.multiple_of((1 - core) * HALF, LANES), HALF)
        count = [0]

        def post(src, dst, target):
            number = count[0]
            count[0] += 1
            copy = copy_to(src, dst, ar_send.at[l, number], ar_recv.at[l, number], target)
            copy.start()
            sends.append((None, copy))
            return copy

        def around(axis):
            for step in (1, 2, 3):
                to = lax.rem(coordinate(me, axis) + step, 4)
                yield step - 1, to, with_coordinate(me, axis, to)

        def exchange(total, landing, axis, lanes):
            mine = coordinate(me, axis)
            landing[mine, :, lanes] = total.astype(BF)
            piece = landing.at[mine, :, lanes]
            return [post(piece, piece, target) for slot, to, target in around(axis)]

        def arrived(landing, copies, lanes):
            for copy in copies:
                copy.wait_recv()
            total = landing[0, :, lanes].astype(F32)
            for slot in range(1, 4):
                total = total + landing[slot, :, lanes].astype(F32)
            return total

        to_mate[l] = partial[l, :, other].astype(BF)
        copy = post(to_mate.at[l], from_mate.at[l], mate)
        yield
        copy.wait_recv()
        a_out[l] = (partial[l, :, half] + from_mate[l].astype(F32)).astype(BF)
        waits = []
        for lanes, axes in PARTS:
            waits.append(
                [
                    post(
                        a_out.at[l, pl.ds(pl.multiple_of(to * BAND, 16), BAND), lanes],
                        a_in.at[l, slot, :, lanes],
                        target,
                    )
                    for slot, to, target in around(axes[0])
                ]
            )
        yield
        for part, (lanes, axes) in enumerate(PARTS):
            for copy in waits[part]:
                copy.wait_recv()
            band = pl.ds(pl.multiple_of(coordinate(me, axes[0]) * BAND, 16), BAND)
            total = a_out[l, band, lanes].astype(F32)
            for slot in range(3):
                total = total + a_in[l, slot, :, lanes].astype(F32)
            waits[part] = exchange(total, b_in.at[l], axes[1], lanes)
        yield
        for part, (lanes, axes) in enumerate(PARTS):
            total = arrived(b_in.at[l], waits[part], lanes)
            waits[part] = exchange(total, c_in.at[l], axes[2], lanes)
        yield
        for part, (lanes, axes) in enumerate(PARTS):
            total = arrived(c_in.at[l], waits[part], lanes)
            band = pl.ds(pl.multiple_of(coordinate(me, axes[0]) * BAND, 16), BAND)
            here = pl.ds(pl.multiple_of(core * HALF + lanes.start, LANES), lanes.size)
            full[l, band, here] = total.astype(BF)
            piece = full.at[l, band, here]
            waits[part] = [post(piece, piece, target) for slot, to, target in around(axes[0])]
        yield
        final = []
        for part, (lanes, axes) in enumerate(PARTS):
            for copy in waits[part]:
                copy.wait_recv()
            here = pl.ds(pl.multiple_of(core * HALF + lanes.start, LANES), lanes.size)
            piece = full.at[l, :, here]
            final.append(post(piece, piece, mate))
        yield
        for copy in final:
            copy.wait_recv()
        store(full.at[l], dw_hbm.at[l])
        yield

    def prepare_forward(l):
        for a in range(3):
            w_side[l, a, :, 0:C] = w_ref[l, 3 * a]
            w_side[l, a, :, C : 2 * C] = w_ref[l, 3 * a + 2]

    def prepare_backward(l):
        for a in range(3):
            v_mid[l, a] = w_ref[l, 3 * a + 1].T
            v_side[l, a, :, 0:C] = w_ref[l, 3 * a + 2].T
            v_side[l, a, :, C : 2 * C] = w_ref[l, 3 * a].T
        for place, tap in enumerate((7, 6, 8)):
            v_over[l, :, place * C : (place + 1) * C] = (
                w_ref[l, tap].T.astype(F32) * flip_sign
            ).astype(BF)

    forward_buffers = (s0, s1, s2)
    backward_buffers = (t0, t1, t2)

    small[2].wait()
    spread_rows[...] = x_ref[...].astype(F32).reshape(C * ROWS, LANES)
    for r in range(ROWS):
        row = spread_rows[pl.ds(r, C, stride=ROWS), :]
        s0[0:C, columns(r)] = (row * mask).astype(BF)
    rim = Rims(0, s0, 1, True)
    rim.turn(0, 1)
    rim.pack_sides()
    rim.pack_corners()
    loads[0].wait()
    prepare_forward(0)
    small[3].wait()
    spread_rows[...] = ct_ref[...].astype(F32).reshape(C * ROWS, LANES)
    for r in range(ROWS):
        grad[:, columns(r)] = mask * spread_rows[pl.ds(r, C, stride=ROWS), :]
    loads[1].wait()
    loads[2].wait()
    pl.semaphore_wait(
        barrier, len(partners) + a_away.astype(jnp.int32) + b_away.astype(jnp.int32)
    )
    rim.send_corners()
    rim.send_fold(0, 1)
    rim.send_sides()

    for l in range(3):
        d = 2**l
        rest = CELLS - d * LANES
        buf = forward_buffers[l]
        acc[...] = dot(w_ref[l, 4], buf[0:C, 0:CELLS]) + bias_cols[l]
        acc[:, 0:rest] += dot(w_ref[l, 7], buf[0:C, d * LANES : CELLS])
        acc[:, d * LANES : CELLS] += dot(w_ref[l, 1], buf[0:C, 0:rest])
        if l < 2:
            prepare_forward(l + 1)
        prepare_backward(2 - l)
        rim.receive_sides()
        acc[...] += dot(w_side[l, 1], buf[C : 3 * C, 0:CELLS])
        acc[:, 0:rest] += dot(w_side[l, 2], buf[C : 3 * C, d * LANES : CELLS])
        acc[:, d * LANES : CELLS] += dot(w_side[l, 0], buf[C : 3 * C, 0:rest])

        def activate(first, last):
            v = acc[:, first:last]
            s = jax.nn.sigmoid(v)
            after = mask * (buf[0:C, first:last].astype(F32) + v * s)
            s = s * (1.0 + v * (1.0 - s))
            slope[l, :, first:last] = s
            if l < 2:
                forward_buffers[l + 1][0:C, first:last] = after.astype(BF)
            else:
                for r in range(first // LANES, last // LANES):
                    out_ref[r] = after[:, r * LANES - first : (r + 1) * LANES - first].astype(BF)
                t2[0:C, first:last] = (grad[:, first:last] * s).astype(BF)

        activate(0, rest)
        if l < 2:
            later = Rims(l + 1, forward_buffers[l + 1], 2 * d, True)
            later.turn(d, 2 * d)
            later.send_fold(d, 2 * d)
        else:
            later = Rims(3, t2, d, False)
        rim.receive_corners()
        for number in range(len(rim.folds)):
            rim.receive_fold(number)
        acc[:, rest:CELLS] += dot(w_ref[l, 7], buf[0:C, CELLS : CELLS + d * LANES]) + dot(
            w_side[l, 2], buf[C : 3 * C, CELLS : CELLS + d * LANES]
        )
        activate(rest, CELLS)
        rim = later
        rim.turn(0, d)
        rim.pack_corners()
        rim.send_corners()
        if l < 2:
            rim.send_fold(0, d)
        else:
            rim.send_fold(d // 2, d)
            rim.send_fold(0, d // 2)
        rim.pack_sides()
        rim.send_sides()

    store(out_ref, out_hbm)
    running = []
    for l in (2, 1, 0):
        d = 2**l
        rest = CELLS - d * LANES
        stored = forward_buffers[l]
        buf = backward_buffers[l]
        for reduction in running:
            next(reduction)
        partial[l, :, 512:640] = jnp.zeros((C, LANES), F32)
        partial[l, :, 1152:1280] = jnp.zeros((C, LANES), F32)
        partial[l, :, 1792:1920] = jnp.zeros((C, LANES), F32)
        partial[l, :, 0:576] = dot_nt(buf[0:C, d * LANES : CELLS], stored[:, 0:rest])
        partial[l, :, 640:1216] = dot_nt(buf[0:C, 0:CELLS], stored[:, 0:CELLS])
        partial[l, :, 1280:1856] = dot_nt(
            buf[0:C, 0:CELLS], stored[:, d * LANES : CELLS + d * LANES]
        )
        partial[l, :, 1920:2048] = jnp.broadcast_to(
            jnp.sum(buf[0:C, 0:CELLS].astype(F32), axis=1, keepdims=True), (C, LANES)
        )
        reduction = all_reduce(l)
        next(reduction)
        running.append(reduction)
        acc[...] = dot(v_mid[l, 1], buf[0:C, 0:CELLS])
        acc[:, d * LANES : CELLS] += dot(v_mid[l, 2], buf[0:C, 0:rest])
        acc[:, 0:rest] += dot(v_mid[l, 0], buf[0:C, d * LANES : CELLS])
        rim.receive_sides()
        acc[...] += dot(v_side[l, 1], buf[C : 3 * C, 0:CELLS])
        acc[:, d * LANES : CELLS] += dot(v_side[l, 2], buf[C : 3 * C, 0:rest])
        acc[:, 0:rest] += dot(v_side[l, 0], buf[C : 3 * C, d * LANES : CELLS])

        def descend(first, last):
            g = mask * (grad[:, first:last] + acc[:, first:last])
            if l > 0:
                grad[:, first:last] = g
                backward_buffers[l - 1][0:C, first:last] = (
                    g * slope[l - 1, :, first:last]
                ).astype(BF)
            else:
                for r in range(first // LANES, last // LANES):
                    fg_ref[r] = g[:, r * LANES - first : (r + 1) * LANES - first].astype(BF)

        descend(0, rest)
        for reduction in running:
            next(reduction)
        rim.receive_corners()
        middle = d // 2
        for number, (fold, first, last) in enumerate(rim.folds):
            rim.receive_fold(number)
            top = slice(rest + first * LANES, rest + last * LANES)
            acc[:, top] += dot(
                v_over[l], buf[:, CELLS + first * LANES : CELLS + last * LANES]
            )
            descend(top.start, top.stop)
            if l > 0 and number == 0:
                later = Rims(6 - l, backward_buffers[l - 1], middle, False)
                later.turn(0, middle)
                later.pack_corners()
                later.send_corners()
                if middle > 1:
                    later.send_fold(middle // 2, middle)
                    later.send_fold(0, middle // 2)
                else:
                    later.send_fold(0, 1)
        if l > 0:
            rim = later
            rim.pack_sides()
            rim.send_sides()

    store(fg_ref, fg_hbm)
    done = object()
    while running:
        running = [reduction for reduction in running if next(reduction, done) is not done]
    for condition, copy in sends:
        if condition is None:
            copy.wait_send()
        else:

            @pl.when(condition)
            def _():
                copy.wait_send()

    for copy in stores:
        copy.wait()


def finish(rows_a, rows_b, summed, out_a, out_b, kernel_grad, bias_grad, spread_rows, bias_rows):
    l = pl.program_id(0)
    for a in range(3):
        for b in range(3):
            first = a * WIDE + (1, 0, 2)[b] * C
            kernel_grad[0, 3 * a + b] = summed[0, :, first : first + C].astype(F32)
    bias_rows[pl.ds(l, 1), :] = summed[0, :, 3 * WIDE : TOTAL].astype(F32).T[0:1]
    bias_grad[...] = bias_rows[0:3]
    for step, rows, out in ((0, rows_a, out_a), (1, rows_b, out_b)):

        @pl.when(l == step)
        def _():
            for r in range(ROWS):
                spread_rows[pl.ds(r, C, stride=ROWS), :] = rows[r].astype(F32)
            out[...] = spread_rows[...].reshape(C, ROWS, LANES).astype(BF)


def shards(fields, cotangent, weights, biases, ocean_tiles, velocity_mask):
    n = lax.axis_size("tiles")
    hbm = pl.BlockSpec(memory_space=pltpu.HBM)
    out, field_grad, summed = pl.pallas_call(
        functools.partial(kernel, n),
        out_shape=(
            jax.ShapeDtypeStruct((ROWS, C, LANES), BF),
            jax.ShapeDtypeStruct((ROWS, C, LANES), BF),
            jax.ShapeDtypeStruct((3, C, TOTAL), BF),
        ),
        in_specs=[
            hbm,
            hbm,
            hbm,
            hbm,
            pl.BlockSpec(memory_space=pltpu.SMEM),
            hbm,
        ],
        out_specs=(hbm,) * 3,
        scratch_shapes=[
            pltpu.VMEM((3 * C, CELLS + LANES), BF),
            pltpu.VMEM((3 * C, CELLS + 2 * LANES), BF),
            pltpu.VMEM((3 * C, CELLS + 4 * LANES), BF),
            pltpu.VMEM((3 * C, CELLS + LANES), BF),
            pltpu.VMEM((3 * C, CELLS + 2 * LANES), BF),
            pltpu.VMEM((3 * C, CELLS + 4 * LANES), BF),
            pltpu.VMEM((C, ROWS, LANES), BF),
            pltpu.VMEM((C, ROWS, LANES), BF),
            pltpu.VMEM((3, C), F32),
            pltpu.VMEM((C,), jnp.int32),
            pltpu.VMEM((3, 9, C, C), BF),
            pltpu.VMEM((ROWS, C, LANES), BF),
            pltpu.VMEM((ROWS, C, LANES), BF),
            pltpu.VMEM((C * ROWS, LANES), F32),
            pltpu.VMEM((LANES, 2 * LANES), F32),
            pltpu.VMEM((3, C, CELLS), F32),
            pltpu.VMEM((C, CELLS), F32),
            pltpu.VMEM((C, CELLS), F32),
            pltpu.VMEM((3, 3, C, 2 * C), BF),
            pltpu.VMEM((3, 3, C, C), BF),
            pltpu.VMEM((3, 3, C, 2 * C), BF),
            pltpu.VMEM((3, C, 3 * C), BF),
            pltpu.VMEM((6, C, LANES), BF),
            pltpu.VMEM((6, BAND, LANES), BF),
            pltpu.VMEM((6, C, 4 * LANES), BF),
            pltpu.VMEM((6, 2, C, LANES), BF),
            pltpu.VMEM((6, 2, BAND, LANES), BF),
            pltpu.VMEM((3, C, TOTAL), F32),
            pltpu.VMEM((3, C, HALF), BF),
            pltpu.VMEM((3, C, HALF), BF),
            pltpu.VMEM((3, C, HALF), BF),
            pltpu.VMEM((3, 3, BAND, HALF), BF),
            pltpu.VMEM((3, 4, BAND, HALF), BF),
            pltpu.VMEM((3, 4, BAND, HALF), BF),
            pltpu.VMEM((3, C, TOTAL), BF),
            pltpu.SemaphoreType.DMA((7,)),
            pltpu.SemaphoreType.DMA((5,)),
            pltpu.SemaphoreType.DMA((6, 6)),
            pltpu.SemaphoreType.DMA((6, 6)),
            pltpu.SemaphoreType.DMA((3, 40)),
            pltpu.SemaphoreType.DMA((3, 40)),
        ],
        compiler_params=pltpu.CompilerParams(
            collective_id=0, has_side_effects=True, vmem_limit_bytes=62 * 1024 * 1024
        ),
        cost_estimate=pl.CostEstimate(
            flops=18 * 9 * C * C * CELLS, bytes_accessed=8 * 1024 * 1024, transcendentals=9 * C * CELLS
        ),
    )(fields, cotangent, weights, biases, ocean_tiles, velocity_mask)
    whole = lambda *shape: pl.BlockSpec(shape, lambda l: (0,) * len(shape))
    return pl.pallas_call(
        finish,
        grid=(3,),
        out_shape=(
            jax.ShapeDtypeStruct((C, ROWS, LANES), BF),
            jax.ShapeDtypeStruct((C, ROWS, LANES), BF),
            jax.ShapeDtypeStruct((3, 9, C, C), F32),
            jax.ShapeDtypeStruct((3, C), F32),
        ),
        in_specs=[
            whole(ROWS, C, LANES),
            whole(ROWS, C, LANES),
            pl.BlockSpec((1, C, TOTAL), lambda l: (l, 0, 0)),
        ],
        out_specs=(
            whole(C, ROWS, LANES),
            whole(C, ROWS, LANES),
            pl.BlockSpec((1, 9, C, C), lambda l: (l, 0, 0, 0)),
            whole(3, C),
        ),
        scratch_shapes=[pltpu.VMEM((C * ROWS, LANES), F32), pltpu.VMEM((8, C), F32)],
        compiler_params=pltpu.CompilerParams(vmem_limit_bytes=62 * 1024 * 1024),
    )(out, field_grad, summed)


def solution(mesh):
    placed = (P(None, None, "tiles"), P(None, None, "tiles"), P(), P(), P(None, "tiles"), P())
    return jax.shard_map(
        shards,
        mesh=mesh,
        in_specs=placed,
        out_specs=(P(None, None, "tiles"), P(None, None, "tiles"), P(), P()),
        check_vma=False,
    )
```

```python
import functools

import jax
import jax.numpy as jnp
from jax import lax
from jax.experimental import pallas as pl
from jax.experimental.pallas import tpu as pltpu
from jax.sharding import PartitionSpec as P

C = 192
ROWS = 8
LANES = 128
CELLS = ROWS * LANES
WIDE = 640
TOTAL = 2048
HALF = TOTAL // 2
BAND = C // 4
BLOCK = 32
BF = jnp.bfloat16
F32 = jnp.float32
MESH = pl.DeviceIdType.MESH

CORE = (1, 2)
Y = (2, 4)
X = (8, 4)
Z = (32, 4)
PARTS = (
    (pl.ds(0, 384), (Y, X, Z)),
    (pl.ds(384, 384), (Z, Y, X)),
    (pl.ds(768, 256), (X, Z, Y)),
)


def coordinate(me, axis):
    return lax.rem(lax.div(me, axis[0]), axis[1])


def with_coordinate(me, axis, value):
    return me + (value - coordinate(me, axis)) * axis[0]


def copy_to(src, dst, send_sem, recv_sem, device):
    return pltpu.make_async_remote_copy(
        src_ref=src,
        dst_ref=dst,
        send_sem=send_sem,
        recv_sem=recv_sem,
        device_id=(device,),
        device_id_type=MESH,
    )


def start_if(condition, copy):
    @pl.when(condition)
    def _():
        copy.start()


def dot(a, b):
    return jnp.dot(a, b, preferred_element_type=F32)


def dot_nt(a, b):
    return lax.dot_general(a, b, (((1,), (1,)), ((), ())), preferred_element_type=F32)


def kernel(
    n,
    x_hbm,
    ct_hbm,
    w_hbm,
    bias_hbm,
    ocean_ref,
    velocity_hbm,
    out_hbm,
    fg_hbm,
    dw_hbm,
    s0,
    s1,
    s2,
    t0,
    t1,
    t2,
    x_ref,
    ct_ref,
    bias_ref,
    velocity_ref,
    w_ref,
    out_ref,
    fg_ref,
    spread_rows,
    cols_ref,
    slope,
    acc,
    grad,
    w_side,
    v_mid,
    v_side,
    v_over,
    packed,
    side_tile,
    corner,
    turned,
    rims,
    corners,
    partial,
    to_mate,
    from_mate,
    a_out,
    a_in,
    b_in,
    c_in,
    full,
    w_sem,
    out_sem,
    ex_send,
    ex_recv,
    ar_send,
    ar_recv,
):
    me = lax.axis_index("tiles")
    east = lax.rem(me + 1, n)
    west = lax.rem(me + n - 1, n)
    mirror = n - 1 - me
    fold_a = lax.rem(n - me, n)
    fold_b = lax.rem(2 * n - 2 - me, n)
    mate = with_coordinate(me, CORE, 1 - coordinate(me, CORE))
    core = coordinate(me, CORE)
    a_away = fold_a != me
    b_away = fold_b != me

    barrier = pltpu.get_barrier_semaphore()
    partners = [east, west, mirror, mate]
    for axis in (Y, X, Z):
        for step in (1, 2, 3):
            partners.append(
                with_coordinate(me, axis, lax.rem(coordinate(me, axis) + step, axis[1]))
            )
    for partner in partners:
        pl.semaphore_signal(barrier, inc=1, device_id=(partner,), device_id_type=MESH)

    @pl.when(a_away)
    def _():
        pl.semaphore_signal(barrier, inc=1, device_id=(fold_a,), device_id_type=MESH)

    @pl.when(b_away)
    def _():
        pl.semaphore_signal(barrier, inc=1, device_id=(fold_b,), device_id_type=MESH)

    small = [
        pltpu.make_async_copy(src, dst, w_sem.at[3 + number])
        for number, (src, dst) in enumerate(
            (
                (bias_hbm, bias_ref),
                (velocity_hbm, velocity_ref),
                (x_hbm, x_ref),
                (ct_hbm, ct_ref),
            )
        )
    ]
    loads = [
        pltpu.make_async_copy(w_hbm.at[l], w_ref.at[l], w_sem.at[l]) for l in range(3)
    ]
    for load in small + loads:
        load.start()

    lane = lax.broadcasted_iota(jnp.int32, (C, LANES), 1)
    flip_matrix = (
        lax.broadcasted_iota(jnp.int32, (LANES, LANES), 0)
        + lax.broadcasted_iota(jnp.int32, (LANES, LANES), 1)
        == LANES - 1
    ).astype(F32).astype(BF)
    cols_ref[...] = jnp.zeros((LANES, 2 * LANES), F32)
    small[0].wait()
    small[1].wait()
    cols_ref[0:3, 0:C] = bias_ref[...]
    cols_ref[3:4, 0:C] = (1 - 2 * velocity_ref[...]).astype(F32).reshape(1, C)
    turned_cols = cols_ref[...].T[0:C]
    bias_cols = [turned_cols[:, l : l + 1] for l in range(3)]
    flip_sign = turned_cols[:, 3:4]
    mask = ocean_ref[0, 0].astype(F32)
    sends = []

    stores = []

    def store(src, dst):
        copy = pltpu.make_async_copy(src, dst, out_sem.at[len(stores)])
        copy.start()
        stores.append(copy)

    def columns(row, count=1):
        return slice(row * LANES, (row + count) * LANES)

    class Rims:
        def __init__(self, e, buf, d, signed):
            self.e, self.buf, self.d, self.signed = e, buf, d, signed
            self.folds = []
            self.groups = 4 if d <= 2 else 2

        def turn(self, first, last):
            for k in range(first, last):
                row = dot(self.buf[0:C, columns(ROWS - 1 - k)], flip_matrix)
                if self.signed:
                    row = row * flip_sign
                turned[self.e, :, columns(k)] = row.astype(BF)

        def send_fold(self, first, last):
            slot = 4 + len(self.folds)
            fold = copy_to(
                turned.at[self.e, :, pl.ds(first * LANES, (last - first) * LANES)],
                self.buf.at[pl.ds(0, C), pl.ds(CELLS + first * LANES, (last - first) * LANES)],
                ex_send.at[self.e, slot],
                ex_recv.at[self.e, slot],
                mirror,
            )
            fold.start()
            self.folds.append((fold, first, last))
            sends.append((None, fold))

        def pack(self, tile, rows, first, last):
            d = self.d
            for r in range(first, last):
                at = 2 * d * r
                here = jnp.logical_and(lane >= at, lane < at + 2 * d)
                tile = jnp.where(here, pltpu.roll(rows(r).astype(F32), (at + d) % LANES, 1), tile)
            return tile

        def dense(self, tile, groups):
            size = C // groups
            total = tile[0:size]
            for q in range(1, groups):
                piece = tile[q * size : (q + 1) * size]
                total = total + pltpu.roll(piece, q * LANES // groups, 1)
            return total.astype(BF)

        def loose(self, total, groups):
            total = total.astype(F32)
            return jnp.concatenate(
                [total]
                + [pltpu.roll(total, LANES - q * LANES // groups, 1) for q in range(1, groups)],
                axis=0,
            )

        def pack_sides(self, first, last):
            tile = jnp.zeros((C, LANES), F32) if first == 0 else side_tile[...]
            side_tile[...] = self.pack(
                tile, lambda r: self.buf[0:C, columns(r)], first, last
            )
            if last == ROWS:
                packed[self.e, 0 : C // self.groups] = self.dense(side_tile[...], self.groups)

        def pack_corners(self):
            tile = self.pack(
                jnp.zeros((C, LANES), F32), lambda k: turned[self.e, :, columns(k)], 0, self.d
            )
            corner[self.e] = self.dense(tile, 4)

        def send_sides(self):
            self.sides = []
            for slot, target in enumerate((east, west)):
                copy = copy_to(
                    packed.at[self.e, pl.ds(0, C // self.groups)],
                    rims.at[self.e, slot, pl.ds(0, C // self.groups)],
                    ex_send.at[self.e, slot],
                    ex_recv.at[self.e, slot],
                    target,
                )
                copy.start()
                self.sides.append(copy)
                sends.append((None, copy))

        def send_corners(self):
            self.turns = []
            for slot, target, away in ((0, fold_a, a_away), (1, fold_b, b_away)):
                copy = copy_to(
                    corner.at[self.e],
                    corners.at[self.e, slot],
                    ex_send.at[self.e, 2 + slot],
                    ex_recv.at[self.e, 2 + slot],
                    target,
                )
                start_if(away, copy)
                self.turns.append((away, copy))
                sends.append((away, copy))

        def unpack(self, rim, row, slot):
            buf, d = self.buf, self.d
            center = buf[0:C, columns(row)].astype(F32)
            edge = pltpu.roll(rim, (-(2 * d * slot + d)) % LANES, 1)
            left = pltpu.roll(jnp.where(lane >= LANES - d, edge, center), d, 1)
            right = pltpu.roll(jnp.where(lane < d, edge, center), LANES - d, 1)
            buf[C : 2 * C, columns(row)] = left.astype(BF)
            buf[2 * C : 3 * C, columns(row)] = right.astype(BF)

        def roll_sides(self):
            buf, d = self.buf, self.d
            for r in range(ROWS):
                center = buf[0:C, columns(r)].astype(F32)
                buf[C : 2 * C, columns(r)] = pltpu.roll(center, d, 1).astype(BF)
                buf[2 * C : 3 * C, columns(r)] = pltpu.roll(center, LANES - d, 1).astype(BF)

        def receive_sides(self):
            buf, d = self.buf, self.d
            for copy in self.sides:
                copy.wait_recv()
            size = C // self.groups
            low = lax.rem(lane, 2 * d) < d
            rim = jnp.where(
                low,
                self.loose(rims[self.e, 0, 0:size], self.groups),
                self.loose(rims[self.e, 1, 0:size], self.groups),
            )
            for r in range(ROWS + 1):
                edge = pltpu.roll(rim, (-2 * d * r) % LANES, 1) if r > 0 else rim
                if r < ROWS:
                    old = buf[C : 2 * C, columns(r)].astype(F32)
                    buf[C : 2 * C, columns(r)] = jnp.where(lane < d, edge, old).astype(BF)
                if r > 0:
                    old = buf[2 * C : 3 * C, columns(r - 1)].astype(F32)
                    buf[2 * C : 3 * C, columns(r - 1)] = jnp.where(
                        lane >= LANES - d, edge, old
                    ).astype(BF)

        def receive_corners(self):
            for slot, (away, copy) in enumerate(self.turns):

                @pl.when(away)
                def _():
                    copy.wait_recv()

                @pl.when(jnp.logical_not(away))
                def _():
                    corners[self.e, slot] = corner[self.e]

            low = lax.rem(lane, 2 * self.d) < self.d
            tiles = [self.loose(corners[self.e, slot], 4) for slot in range(2)]
            self.rim = jnp.where(low, tiles[0], tiles[1])

        def receive_fold(self, number):
            fold, first, last = self.folds[number]
            fold.wait_recv()
            for k in range(first, last):
                self.unpack(self.rim, ROWS + k, k)

    def all_reduce(l):
        half = pl.ds(pl.multiple_of(core * HALF, LANES), HALF)
        other = pl.ds(pl.multiple_of((1 - core) * HALF, LANES), HALF)
        count = [0]

        def post(src, dst, target):
            number = count[0]
            count[0] += 1
            copy = copy_to(src, dst, ar_send.at[l, number], ar_recv.at[l, number], target)
            copy.start()
            sends.append((None, copy))
            return copy

        def around(axis):
            for step in (1, 2, 3):
                to = lax.rem(coordinate(me, axis) + step, 4)
                yield step - 1, to, with_coordinate(me, axis, to)

        def exchange(total, landing, axis, lanes):
            mine = coordinate(me, axis)
            landing[mine, :, lanes] = total.astype(BF)
            piece = landing.at[mine, :, lanes]
            return [post(piece, piece, target) for slot, to, target in around(axis)]

        def arrived(landing, copies, lanes):
            for copy in copies:
                copy.wait_recv()
            total = landing[0, :, lanes].astype(F32)
            for slot in range(1, 4):
                total = total + landing[slot, :, lanes].astype(F32)
            return total

        to_mate[l] = partial[l, :, other].astype(BF)
        copy = post(to_mate.at[l], from_mate.at[l], mate)
        yield
        copy.wait_recv()
        a_out[l] = (partial[l, :, half] + from_mate[l].astype(F32)).astype(BF)
        waits = []
        for lanes, axes in PARTS:
            waits.append(
                [
                    post(
                        a_out.at[l, pl.ds(pl.multiple_of(to * BAND, 16), BAND), lanes],
                        a_in.at[l, slot, :, lanes],
                        target,
                    )
                    for slot, to, target in around(axes[0])
                ]
            )
        yield
        for part, (lanes, axes) in enumerate(PARTS):
            for copy in waits[part]:
                copy.wait_recv()
            band = pl.ds(pl.multiple_of(coordinate(me, axes[0]) * BAND, 16), BAND)
            total = a_out[l, band, lanes].astype(F32)
            for slot in range(3):
                total = total + a_in[l, slot, :, lanes].astype(F32)
            waits[part] = exchange(total, b_in.at[l], axes[1], lanes)
        yield
        for part, (lanes, axes) in enumerate(PARTS):
            total = arrived(b_in.at[l], waits[part], lanes)
            waits[part] = exchange(total, c_in.at[l], axes[2], lanes)
        yield
        for part, (lanes, axes) in enumerate(PARTS):
            total = arrived(c_in.at[l], waits[part], lanes)
            band = pl.ds(pl.multiple_of(coordinate(me, axes[0]) * BAND, 16), BAND)
            here = pl.ds(pl.multiple_of(core * HALF + lanes.start, LANES), lanes.size)
            full[l, band, here] = total.astype(BF)
            piece = full.at[l, band, here]
            waits[part] = [post(piece, piece, target) for slot, to, target in around(axes[0])]
        yield
        final = []
        for part, (lanes, axes) in enumerate(PARTS):
            for copy in waits[part]:
                copy.wait_recv()
            here = pl.ds(pl.multiple_of(core * HALF + lanes.start, LANES), lanes.size)
            piece = full.at[l, :, here]
            final.append(post(piece, piece, mate))
        yield
        for copy in final:
            copy.wait_recv()
        store(full.at[l], dw_hbm.at[l])
        yield

    def weight_sums(l, delta, stored):
        d = 2**l
        rest = CELLS - d * LANES
        for a in range(3):
            partial[l, :, a * WIDE + 512 : (a + 1) * WIDE] = jnp.zeros((C, LANES), F32)
        partial[l, :, 0:576] = dot_nt(delta[0:C, d * LANES : CELLS], stored[:, 0:rest])
        partial[l, :, 640:1216] = dot_nt(delta[0:C, 0:CELLS], stored[:, 0:CELLS])
        partial[l, :, 1280:1856] = dot_nt(
            delta[0:C, 0:CELLS], stored[:, d * LANES : CELLS + d * LANES]
        )
        partial[l, :, 1920:2048] = jnp.broadcast_to(
            jnp.sum(delta[0:C, 0:CELLS].astype(F32), axis=1, keepdims=True), (C, LANES)
        )
        reduction = all_reduce(l)
        next(reduction)
        return reduction

    def prepare_forward(l):
        for a in range(3):
            w_side[l, a, :, 0:C] = w_ref[l, 3 * a]
            w_side[l, a, :, C : 2 * C] = w_ref[l, 3 * a + 2]

    def prepare_backward(l):
        for a in range(3):
            v_mid[l, a] = w_ref[l, 3 * a + 1].T
            v_side[l, a, :, 0:C] = w_ref[l, 3 * a + 2].T
            v_side[l, a, :, C : 2 * C] = w_ref[l, 3 * a].T
        for place, tap in enumerate((7, 6, 8)):
            v_over[l, :, place * C : (place + 1) * C] = (
                w_ref[l, tap].T.astype(F32) * flip_sign
            ).astype(BF)

    forward_buffers = (s0, s1, s2)
    backward_buffers = (t0, t1, t2)

    small[2].wait()
    spread_rows[...] = x_ref[...].astype(F32).reshape(C * ROWS, LANES)
    for r in range(ROWS):
        row = spread_rows[pl.ds(r, C, stride=ROWS), :]
        s0[0:C, columns(r)] = (row * mask).astype(BF)
    rim = Rims(0, s0, 1, True)
    rim.turn(0, 1)
    rim.pack_sides(0, ROWS)
    rim.pack_corners()
    loads[0].wait()
    prepare_forward(0)
    small[3].wait()
    spread_rows[...] = ct_ref[...].astype(F32).reshape(C * ROWS, LANES)
    for r in range(ROWS):
        grad[:, columns(r)] = mask * spread_rows[pl.ds(r, C, stride=ROWS), :]
    loads[1].wait()
    loads[2].wait()
    pl.semaphore_wait(
        barrier, len(partners) + a_away.astype(jnp.int32) + b_away.astype(jnp.int32)
    )
    rim.send_corners()
    rim.send_fold(0, 1)
    rim.send_sides()

    for l in range(3):
        d = 2**l
        rest = CELLS - d * LANES
        buf = forward_buffers[l]
        acc[...] = dot(w_ref[l, 4], buf[0:C, 0:CELLS]) + bias_cols[l]
        acc[:, 0:rest] += dot(w_ref[l, 7], buf[0:C, d * LANES : CELLS])
        acc[:, d * LANES : CELLS] += dot(w_ref[l, 1], buf[0:C, 0:rest])
        if l < 2:
            prepare_forward(l + 1)
        rim.roll_sides()
        prepare_backward(2 - l)
        rim.receive_sides()
        acc[...] += dot(w_side[l, 1], buf[C : 3 * C, 0:CELLS])
        acc[:, 0:rest] += dot(w_side[l, 2], buf[C : 3 * C, d * LANES : CELLS])
        acc[:, d * LANES : CELLS] += dot(w_side[l, 0], buf[C : 3 * C, 0:rest])

        def activate(first, last):
            v = acc[:, first:last]
            s = jax.nn.sigmoid(v)
            after = mask * (buf[0:C, first:last].astype(F32) + v * s)
            s = s * (1.0 + v * (1.0 - s))
            slope[l, :, first:last] = s
            if l < 2:
                forward_buffers[l + 1][0:C, first:last] = after.astype(BF)
            else:
                for r in range(first // LANES, last // LANES):
                    out_ref[r] = after[:, r * LANES - first : (r + 1) * LANES - first].astype(BF)
                t2[0:C, first:last] = (grad[:, first:last] * s).astype(BF)

        activate(0, rest)
        if l < 2:
            later = Rims(l + 1, forward_buffers[l + 1], 2 * d, True)
            later.turn(d, 2 * d)
            later.send_fold(d, 2 * d)
        else:
            later = Rims(3, t2, d, False)
        later.pack_sides(0, ROWS - d)
        rim.receive_corners()
        for number in range(len(rim.folds)):
            rim.receive_fold(number)
        acc[:, rest:CELLS] += dot(w_ref[l, 7], buf[0:C, CELLS : CELLS + d * LANES]) + dot(
            w_side[l, 2], buf[C : 3 * C, CELLS : CELLS + d * LANES]
        )
        activate(rest, CELLS)
        rim = later
        rim.turn(0, d)
        rim.pack_corners()
        rim.send_corners()
        if l < 2:
            rim.send_fold(0, d)
        else:
            rim.send_fold(d // 2, d)
            rim.send_fold(0, d // 2)
        rim.pack_sides(ROWS - d, ROWS)
        rim.send_sides()

    store(out_ref, out_hbm)
    reductions = {}
    for l in (2, 1, 0):
        d = 2**l
        rest = CELLS - d * LANES
        stored = forward_buffers[l]
        buf = backward_buffers[l]
        if l == 0:
            reductions[0] = weight_sums(0, buf, stored)
            rim.pack_sides(0, ROWS)
            rim.send_sides()
            for older in (0, 1, 2):
                next(reductions[older])
        else:
            reductions[l] = weight_sums(l, buf, stored)
            for older in range(l + 1, 3):
                next(reductions[older])
        acc[...] = dot(v_mid[l, 1], buf[0:C, 0:CELLS])
        acc[:, d * LANES : CELLS] += dot(v_mid[l, 2], buf[0:C, 0:rest])
        acc[:, 0:rest] += dot(v_mid[l, 0], buf[0:C, d * LANES : CELLS])
        rim.roll_sides()
        rim.receive_sides()
        if l == 0:
            for older in (0, 1, 2):
                next(reductions[older])
        acc[...] += dot(v_side[l, 1], buf[C : 3 * C, 0:CELLS])
        acc[:, d * LANES : CELLS] += dot(v_side[l, 2], buf[C : 3 * C, 0:rest])
        acc[:, 0:rest] += dot(v_side[l, 0], buf[C : 3 * C, d * LANES : CELLS])

        def descend(first, last):
            g = mask * (grad[:, first:last] + acc[:, first:last])
            if l > 0:
                grad[:, first:last] = g
                backward_buffers[l - 1][0:C, first:last] = (
                    g * slope[l - 1, :, first:last]
                ).astype(BF)
            else:
                for r in range(first // LANES, last // LANES):
                    fg_ref[r] = g[:, r * LANES - first : (r + 1) * LANES - first].astype(BF)

        descend(0, rest)
        if l > 0:
            for older in range(l, 3):
                next(reductions[older])
        rim.receive_corners()
        middle = d // 2
        for number, (fold, first, last) in enumerate(rim.folds):
            rim.receive_fold(number)
            top = slice(rest + first * LANES, rest + last * LANES)
            acc[:, top] += dot(
                v_over[l], buf[:, CELLS + first * LANES : CELLS + last * LANES]
            )
            descend(top.start, top.stop)
            if l > 0 and number == 0:
                later = Rims(6 - l, backward_buffers[l - 1], middle, False)
                later.turn(0, middle)
                later.pack_corners()
                later.send_corners()
                if middle > 1:
                    later.send_fold(middle // 2, middle)
                    later.send_fold(0, middle // 2)
                else:
                    later.send_fold(0, 1)
        if l > 0:
            rim = later
        if l > 1:
            rim.pack_sides(0, ROWS)
            rim.send_sides()

    store(fg_ref, fg_hbm)
    done = object()
    running = [reductions[l] for l in range(3)]
    while running:
        running = [reduction for reduction in running if next(reduction, done) is not done]
    for condition, copy in sends:
        if condition is None:
            copy.wait_send()
        else:

            @pl.when(condition)
            def _():
                copy.wait_send()

    for copy in stores:
        copy.wait()


def finish(
    rows_a, rows_b, summed, last, out_a, out_b, kernel_grad, bias_grad, spread_rows
):
    for l in range(3):
        for a in range(3):
            for b in range(3):
                first = a * WIDE + (1, 0, 2)[b] * C
                kernel_grad[l, 3 * a + b] = summed[l, :, first : first + C].astype(F32)
    for rows, out in ((rows_a, out_a), (rows_b, out_b)):
        for r in range(ROWS):
            spread_rows[pl.ds(r, BLOCK, stride=ROWS), :] = rows[r].astype(F32)
        out[...] = spread_rows[...].reshape(BLOCK, ROWS, LANES).astype(BF)

    @pl.when(pl.program_id(0) == 0)
    def _():
        for l in range(3):
            bias_grad[l : l + 1, :] = last[l].astype(F32).T[0:1]


def shards(fields, cotangent, weights, biases, ocean_tiles, velocity_mask):
    n = lax.axis_size("tiles")
    hbm = pl.BlockSpec(memory_space=pltpu.HBM)
    out, field_grad, summed = pl.pallas_call(
        functools.partial(kernel, n),
        out_shape=(
            jax.ShapeDtypeStruct((ROWS, C, LANES), BF),
            jax.ShapeDtypeStruct((ROWS, C, LANES), BF),
            jax.ShapeDtypeStruct((3, C, TOTAL), BF),
        ),
        in_specs=[
            hbm,
            hbm,
            hbm,
            hbm,
            pl.BlockSpec(memory_space=pltpu.SMEM),
            hbm,
        ],
        out_specs=(hbm,) * 3,
        scratch_shapes=[
            pltpu.VMEM((3 * C, CELLS + LANES), BF),
            pltpu.VMEM((3 * C, CELLS + 2 * LANES), BF),
            pltpu.VMEM((3 * C, CELLS + 4 * LANES), BF),
            pltpu.VMEM((3 * C, CELLS + LANES), BF),
            pltpu.VMEM((3 * C, CELLS + 2 * LANES), BF),
            pltpu.VMEM((3 * C, CELLS + 4 * LANES), BF),
            pltpu.VMEM((C, ROWS, LANES), BF),
            pltpu.VMEM((C, ROWS, LANES), BF),
            pltpu.VMEM((3, C), F32),
            pltpu.VMEM((C,), jnp.int32),
            pltpu.VMEM((3, 9, C, C), BF),
            pltpu.VMEM((ROWS, C, LANES), BF),
            pltpu.VMEM((ROWS, C, LANES), BF),
            pltpu.VMEM((C * ROWS, LANES), F32),
            pltpu.VMEM((LANES, 2 * LANES), F32),
            pltpu.VMEM((3, C, CELLS), F32),
            pltpu.VMEM((C, CELLS), F32),
            pltpu.VMEM((C, CELLS), F32),
            pltpu.VMEM((3, 3, C, 2 * C), BF),
            pltpu.VMEM((3, 3, C, C), BF),
            pltpu.VMEM((3, 3, C, 2 * C), BF),
            pltpu.VMEM((3, C, 3 * C), BF),
            pltpu.VMEM((6, C, LANES), BF),
            pltpu.VMEM((C, LANES), F32),
            pltpu.VMEM((6, BAND, LANES), BF),
            pltpu.VMEM((6, C, 4 * LANES), BF),
            pltpu.VMEM((6, 2, C, LANES), BF),
            pltpu.VMEM((6, 2, BAND, LANES), BF),
            pltpu.VMEM((3, C, TOTAL), F32),
            pltpu.VMEM((3, C, HALF), BF),
            pltpu.VMEM((3, C, HALF), BF),
            pltpu.VMEM((3, C, HALF), BF),
            pltpu.VMEM((3, 3, BAND, HALF), BF),
            pltpu.VMEM((3, 4, BAND, HALF), BF),
            pltpu.VMEM((3, 4, BAND, HALF), BF),
            pltpu.VMEM((3, C, TOTAL), BF),
            pltpu.SemaphoreType.DMA((7,)),
            pltpu.SemaphoreType.DMA((5,)),
            pltpu.SemaphoreType.DMA((6, 6)),
            pltpu.SemaphoreType.DMA((6, 6)),
            pltpu.SemaphoreType.DMA((3, 40)),
            pltpu.SemaphoreType.DMA((3, 40)),
        ],
        compiler_params=pltpu.CompilerParams(
            collective_id=0, has_side_effects=True, vmem_limit_bytes=62 * 1024 * 1024
        ),
        cost_estimate=pl.CostEstimate(
            flops=18 * 9 * C * C * CELLS, bytes_accessed=8 * 1024 * 1024, transcendentals=9 * C * CELLS
        ),
    )(fields, cotangent, weights, biases, ocean_tiles, velocity_mask)
    return pl.pallas_call(
        finish,
        grid=(C // BLOCK,),
        out_shape=(
            jax.ShapeDtypeStruct((C, ROWS, LANES), BF),
            jax.ShapeDtypeStruct((C, ROWS, LANES), BF),
            jax.ShapeDtypeStruct((3, 9, C, C), F32),
            jax.ShapeDtypeStruct((3, C), F32),
        ),
        in_specs=[
            pl.BlockSpec((ROWS, BLOCK, LANES), lambda i: (0, i, 0)),
            pl.BlockSpec((ROWS, BLOCK, LANES), lambda i: (0, i, 0)),
            pl.BlockSpec((3, BLOCK, TOTAL), lambda i: (0, i, 0)),
            pl.BlockSpec((3, C, LANES), lambda i: (0, 0, TOTAL // LANES - 1)),
        ],
        out_specs=(
            pl.BlockSpec((BLOCK, ROWS, LANES), lambda i: (i, 0, 0)),
            pl.BlockSpec((BLOCK, ROWS, LANES), lambda i: (i, 0, 0)),
            pl.BlockSpec((3, 9, BLOCK, C), lambda i: (0, 0, i, 0)),
            pl.BlockSpec((3, C), lambda i: (0, 0)),
        ),
        scratch_shapes=[pltpu.VMEM((BLOCK * ROWS, LANES), F32)],
        compiler_params=pltpu.CompilerParams(vmem_limit_bytes=62 * 1024 * 1024),
    )(out, field_grad, summed, summed)


def solution(mesh):
    placed = (P(None, None, "tiles"), P(None, None, "tiles"), P(), P(), P(None, "tiles"), P())
    return jax.shard_map(
        shards,
        mesh=mesh,
        in_specs=placed,
        out_specs=(P(None, None, "tiles"), P(None, None, "tiles"), P(), P()),
        check_vma=False,
    )
```

```python
import functools

import jax
import jax.numpy as jnp
from jax import lax
from jax.experimental import pallas as pl
from jax.experimental.pallas import tpu as pltpu
from jax.sharding import PartitionSpec as P

C = 192
ROWS = 8
LANES = 128
CELLS = ROWS * LANES
WIDE = 640
TOTAL = 2048
HALF = TOTAL // 2
BAND = C // 4
BF = jnp.bfloat16
F32 = jnp.float32
MESH = pl.DeviceIdType.MESH

CORE = (1, 2)
Y = (2, 4)
X = (8, 4)
Z = (32, 4)
PARTS = (
    (pl.ds(0, 384), (Y, X, Z)),
    (pl.ds(384, 384), (Z, Y, X)),
    (pl.ds(768, 256), (X, Z, Y)),
)


def coordinate(me, axis):
    return lax.rem(lax.div(me, axis[0]), axis[1])


def with_coordinate(me, axis, value):
    return me + (value - coordinate(me, axis)) * axis[0]


def copy_to(src, dst, send_sem, recv_sem, device):
    return pltpu.make_async_remote_copy(
        src_ref=src,
        dst_ref=dst,
        send_sem=send_sem,
        recv_sem=recv_sem,
        device_id=(device,),
        device_id_type=MESH,
    )


def start_if(condition, copy):
    @pl.when(condition)
    def _():
        copy.start()


def dot(a, b):
    return jnp.dot(a, b, preferred_element_type=F32)


def dot_nt(a, b):
    return lax.dot_general(a, b, (((1,), (1,)), ((), ())), preferred_element_type=F32)


def kernel(
    n,
    x_hbm,
    ct_hbm,
    w_hbm,
    bias_hbm,
    ocean_ref,
    velocity_hbm,
    out_hbm,
    fg_hbm,
    dw_hbm,
    s0,
    s1,
    s2,
    t0,
    t1,
    t2,
    x_ref,
    ct_ref,
    bias_ref,
    velocity_ref,
    w_ref,
    out_ref,
    fg_ref,
    spread_rows,
    cols_ref,
    slope,
    acc,
    grad,
    w_side,
    v_mid,
    v_side,
    v_over,
    packed,
    side_tile,
    corner,
    turned,
    rims,
    corners,
    partial,
    to_mate,
    from_mate,
    a_out,
    a_in,
    b_in,
    c_in,
    full,
    w_sem,
    out_sem,
    ex_send,
    ex_recv,
    ar_send,
    ar_recv,
):
    me = lax.axis_index("tiles")
    east = lax.rem(me + 1, n)
    west = lax.rem(me + n - 1, n)
    mirror = n - 1 - me
    fold_a = lax.rem(n - me, n)
    fold_b = lax.rem(2 * n - 2 - me, n)
    mate = with_coordinate(me, CORE, 1 - coordinate(me, CORE))
    core = coordinate(me, CORE)
    a_away = fold_a != me
    b_away = fold_b != me

    barrier = pltpu.get_barrier_semaphore()
    partners = [east, west, mirror, mate]
    for axis in (Y, X, Z):
        for step in (1, 2, 3):
            partners.append(
                with_coordinate(me, axis, lax.rem(coordinate(me, axis) + step, axis[1]))
            )
    for partner in partners:
        pl.semaphore_signal(barrier, inc=1, device_id=(partner,), device_id_type=MESH)

    @pl.when(a_away)
    def _():
        pl.semaphore_signal(barrier, inc=1, device_id=(fold_a,), device_id_type=MESH)

    @pl.when(b_away)
    def _():
        pl.semaphore_signal(barrier, inc=1, device_id=(fold_b,), device_id_type=MESH)

    small = [
        pltpu.make_async_copy(src, dst, w_sem.at[3 + number])
        for number, (src, dst) in enumerate(
            (
                (bias_hbm, bias_ref),
                (velocity_hbm, velocity_ref),
                (x_hbm, x_ref),
                (ct_hbm, ct_ref),
            )
        )
    ]
    loads = [
        pltpu.make_async_copy(w_hbm.at[l], w_ref.at[l], w_sem.at[l]) for l in range(3)
    ]
    for load in small + loads:
        load.start()

    lane = lax.broadcasted_iota(jnp.int32, (C, LANES), 1)
    flip_matrix = (
        lax.broadcasted_iota(jnp.int32, (LANES, LANES), 0)
        + lax.broadcasted_iota(jnp.int32, (LANES, LANES), 1)
        == LANES - 1
    ).astype(F32).astype(BF)
    cols_ref[...] = jnp.zeros((LANES, 2 * LANES), F32)
    small[0].wait()
    small[1].wait()
    cols_ref[0:3, 0:C] = bias_ref[...]
    cols_ref[3:4, 0:C] = (1 - 2 * velocity_ref[...]).astype(F32).reshape(1, C)
    turned_cols = cols_ref[...].T[0:C]
    bias_cols = [turned_cols[:, l : l + 1] for l in range(3)]
    flip_sign = turned_cols[:, 3:4]
    mask = ocean_ref[0, 0].astype(F32)
    sends = []

    stores = []

    def store(src, dst):
        copy = pltpu.make_async_copy(src, dst, out_sem.at[len(stores)])
        copy.start()
        stores.append(copy)

    def columns(row, count=1):
        return slice(row * LANES, (row + count) * LANES)

    class Rims:
        def __init__(self, e, buf, d, signed):
            self.e, self.buf, self.d, self.signed = e, buf, d, signed
            self.folds = []
            self.groups = 4 if d <= 2 else 2

        def turn(self, first, last):
            for k in range(first, last):
                row = dot(self.buf[0:C, columns(ROWS - 1 - k)], flip_matrix)
                if self.signed:
                    row = row * flip_sign
                turned[self.e, :, columns(k)] = row.astype(BF)

        def send_fold(self, first, last):
            slot = 4 + len(self.folds)
            fold = copy_to(
                turned.at[self.e, :, pl.ds(first * LANES, (last - first) * LANES)],
                self.buf.at[pl.ds(0, C), pl.ds(CELLS + first * LANES, (last - first) * LANES)],
                ex_send.at[self.e, slot],
                ex_recv.at[self.e, slot],
                mirror,
            )
            fold.start()
            self.folds.append((fold, first, last))
            sends.append((None, fold))

        def pack(self, tile, rows, first, last):
            d = self.d
            for r in range(first, last):
                at = 2 * d * r
                here = jnp.logical_and(lane >= at, lane < at + 2 * d)
                tile = jnp.where(here, pltpu.roll(rows(r).astype(F32), (at + d) % LANES, 1), tile)
            return tile

        def dense(self, tile, groups):
            size = C // groups
            total = tile[0:size]
            for q in range(1, groups):
                piece = tile[q * size : (q + 1) * size]
                total = total + pltpu.roll(piece, q * LANES // groups, 1)
            return total.astype(BF)

        def loose(self, total, groups):
            total = total.astype(F32)
            return jnp.concatenate(
                [total]
                + [pltpu.roll(total, LANES - q * LANES // groups, 1) for q in range(1, groups)],
                axis=0,
            )

        def pack_sides(self, first, last):
            tile = jnp.zeros((C, LANES), F32) if first == 0 else side_tile[...]
            side_tile[...] = self.pack(
                tile, lambda r: self.buf[0:C, columns(r)], first, last
            )
            if last == ROWS:
                packed[self.e, 0 : C // self.groups] = self.dense(side_tile[...], self.groups)

        def pack_corners(self):
            tile = self.pack(
                jnp.zeros((C, LANES), F32), lambda k: turned[self.e, :, columns(k)], 0, self.d
            )
            corner[self.e] = self.dense(tile, 4)

        def send_sides(self):
            self.sides = []
            for slot, target in enumerate((east, west)):
                copy = copy_to(
                    packed.at[self.e, pl.ds(0, C // self.groups)],
                    rims.at[self.e, slot, pl.ds(0, C // self.groups)],
                    ex_send.at[self.e, slot],
                    ex_recv.at[self.e, slot],
                    target,
                )
                copy.start()
                self.sides.append(copy)
                sends.append((None, copy))

        def send_corners(self):
            self.turns = []
            for slot, target, away in ((0, fold_a, a_away), (1, fold_b, b_away)):
                copy = copy_to(
                    corner.at[self.e],
                    corners.at[self.e, slot],
                    ex_send.at[self.e, 2 + slot],
                    ex_recv.at[self.e, 2 + slot],
                    target,
                )
                start_if(away, copy)
                self.turns.append((away, copy))
                sends.append((away, copy))

        def unpack(self, rim, row, slot):
            buf, d = self.buf, self.d
            center = buf[0:C, columns(row)].astype(F32)
            edge = pltpu.roll(rim, (-(2 * d * slot + d)) % LANES, 1)
            left = pltpu.roll(jnp.where(lane >= LANES - d, edge, center), d, 1)
            right = pltpu.roll(jnp.where(lane < d, edge, center), LANES - d, 1)
            buf[C : 2 * C, columns(row)] = left.astype(BF)
            buf[2 * C : 3 * C, columns(row)] = right.astype(BF)

        def roll_sides(self):
            buf, d = self.buf, self.d
            for r in range(ROWS):
                center = buf[0:C, columns(r)].astype(F32)
                buf[C : 2 * C, columns(r)] = pltpu.roll(center, d, 1).astype(BF)
                buf[2 * C : 3 * C, columns(r)] = pltpu.roll(center, LANES - d, 1).astype(BF)

        def receive_sides(self):
            buf, d = self.buf, self.d
            for copy in self.sides:
                copy.wait_recv()
            size = C // self.groups
            low = lax.rem(lane, 2 * d) < d
            rim = jnp.where(
                low,
                self.loose(rims[self.e, 0, 0:size], self.groups),
                self.loose(rims[self.e, 1, 0:size], self.groups),
            )
            for r in range(ROWS + 1):
                edge = pltpu.roll(rim, (-2 * d * r) % LANES, 1) if r > 0 else rim
                if r < ROWS:
                    old = buf[C : 2 * C, columns(r)].astype(F32)
                    buf[C : 2 * C, columns(r)] = jnp.where(lane < d, edge, old).astype(BF)
                if r > 0:
                    old = buf[2 * C : 3 * C, columns(r - 1)].astype(F32)
                    buf[2 * C : 3 * C, columns(r - 1)] = jnp.where(
                        lane >= LANES - d, edge, old
                    ).astype(BF)

        def receive_corners(self):
            for slot, (away, copy) in enumerate(self.turns):

                @pl.when(away)
                def _():
                    copy.wait_recv()

                @pl.when(jnp.logical_not(away))
                def _():
                    corners[self.e, slot] = corner[self.e]

            low = lax.rem(lane, 2 * self.d) < self.d
            tiles = [self.loose(corners[self.e, slot], 4) for slot in range(2)]
            self.rim = jnp.where(low, tiles[0], tiles[1])

        def receive_fold(self, number):
            fold, first, last = self.folds[number]
            fold.wait_recv()
            for k in range(first, last):
                self.unpack(self.rim, ROWS + k, k)

    def all_reduce(l):
        half = pl.ds(pl.multiple_of(core * HALF, LANES), HALF)
        other = pl.ds(pl.multiple_of((1 - core) * HALF, LANES), HALF)
        count = [0]

        def post(src, dst, target):
            number = count[0]
            count[0] += 1
            copy = copy_to(src, dst, ar_send.at[l, number], ar_recv.at[l, number], target)
            copy.start()
            sends.append((None, copy))
            return copy

        def around(axis):
            for step in (1, 2, 3):
                to = lax.rem(coordinate(me, axis) + step, 4)
                yield step - 1, to, with_coordinate(me, axis, to)

        def exchange(total, landing, axis, lanes):
            mine = coordinate(me, axis)
            landing[mine, :, lanes] = total.astype(BF)
            piece = landing.at[mine, :, lanes]
            return [post(piece, piece, target) for slot, to, target in around(axis)]

        def arrived(landing, copies, lanes):
            for copy in copies:
                copy.wait_recv()
            total = landing[0, :, lanes].astype(F32)
            for slot in range(1, 4):
                total = total + landing[slot, :, lanes].astype(F32)
            return total

        to_mate[l] = partial[l, :, other].astype(BF)
        copy = post(to_mate.at[l], from_mate.at[l], mate)
        yield
        copy.wait_recv()
        a_out[l] = (partial[l, :, half] + from_mate[l].astype(F32)).astype(BF)
        waits = []
        for lanes, axes in PARTS:
            waits.append(
                [
                    post(
                        a_out.at[l, pl.ds(pl.multiple_of(to * BAND, 16), BAND), lanes],
                        a_in.at[l, slot, :, lanes],
                        target,
                    )
                    for slot, to, target in around(axes[0])
                ]
            )
        yield
        for part, (lanes, axes) in enumerate(PARTS):
            for copy in waits[part]:
                copy.wait_recv()
            band = pl.ds(pl.multiple_of(coordinate(me, axes[0]) * BAND, 16), BAND)
            total = a_out[l, band, lanes].astype(F32)
            for slot in range(3):
                total = total + a_in[l, slot, :, lanes].astype(F32)
            waits[part] = exchange(total, b_in.at[l], axes[1], lanes)
        yield
        for part, (lanes, axes) in enumerate(PARTS):
            total = arrived(b_in.at[l], waits[part], lanes)
            waits[part] = exchange(total, c_in.at[l], axes[2], lanes)
        yield
        for part, (lanes, axes) in enumerate(PARTS):
            total = arrived(c_in.at[l], waits[part], lanes)
            band = pl.ds(pl.multiple_of(coordinate(me, axes[0]) * BAND, 16), BAND)
            here = pl.ds(pl.multiple_of(core * HALF + lanes.start, LANES), lanes.size)
            full[l, band, here] = total.astype(BF)
            piece = full.at[l, band, here]
            waits[part] = [post(piece, piece, target) for slot, to, target in around(axes[0])]
        yield
        final = []
        for part, (lanes, axes) in enumerate(PARTS):
            for copy in waits[part]:
                copy.wait_recv()
            here = pl.ds(pl.multiple_of(core * HALF + lanes.start, LANES), lanes.size)
            piece = full.at[l, :, here]
            final.append(post(piece, piece, mate))
        yield
        for copy in final:
            copy.wait_recv()
        store(full.at[l], dw_hbm.at[l])
        yield

    def weight_sums(l, delta, stored):
        d = 2**l
        rest = CELLS - d * LANES
        for a in range(3):
            partial[l, :, a * WIDE + 512 : (a + 1) * WIDE] = jnp.zeros((C, LANES), F32)
        partial[l, :, 0:576] = dot_nt(delta[0:C, d * LANES : CELLS], stored[:, 0:rest])
        partial[l, :, 640:1216] = dot_nt(delta[0:C, 0:CELLS], stored[:, 0:CELLS])
        partial[l, :, 1280:1856] = dot_nt(
            delta[0:C, 0:CELLS], stored[:, d * LANES : CELLS + d * LANES]
        )
        partial[l, :, 1920:2048] = jnp.broadcast_to(
            jnp.sum(delta[0:C, 0:CELLS].astype(F32), axis=1, keepdims=True), (C, LANES)
        )
        reduction = all_reduce(l)
        next(reduction)
        return reduction

    def prepare_forward(l):
        for a in range(3):
            w_side[l, a, :, 0:C] = w_ref[l, 3 * a]
            w_side[l, a, :, C : 2 * C] = w_ref[l, 3 * a + 2]

    def prepare_backward(l):
        for a in range(3):
            v_mid[l, a] = w_ref[l, 3 * a + 1].T
            v_side[l, a, :, 0:C] = w_ref[l, 3 * a + 2].T
            v_side[l, a, :, C : 2 * C] = w_ref[l, 3 * a].T
        for place, tap in enumerate((7, 6, 8)):
            v_over[l, :, place * C : (place + 1) * C] = (
                w_ref[l, tap].T.astype(F32) * flip_sign
            ).astype(BF)

    forward_buffers = (s0, s1, s2)
    backward_buffers = (t0, t1, t2)

    small[2].wait()
    spread_rows[...] = x_ref[...].astype(F32).reshape(C * ROWS, LANES)
    for r in range(ROWS):
        row = spread_rows[pl.ds(r, C, stride=ROWS), :]
        s0[0:C, columns(r)] = (row * mask).astype(BF)
    rim = Rims(0, s0, 1, True)
    rim.turn(0, 1)
    rim.pack_sides(0, ROWS)
    rim.pack_corners()
    loads[0].wait()
    prepare_forward(0)
    small[3].wait()
    spread_rows[...] = ct_ref[...].astype(F32).reshape(C * ROWS, LANES)
    for r in range(ROWS):
        grad[:, columns(r)] = mask * spread_rows[pl.ds(r, C, stride=ROWS), :]
    loads[1].wait()
    loads[2].wait()
    pl.semaphore_wait(
        barrier, len(partners) + a_away.astype(jnp.int32) + b_away.astype(jnp.int32)
    )
    rim.send_corners()
    rim.send_fold(0, 1)
    rim.send_sides()

    for l in range(3):
        d = 2**l
        rest = CELLS - d * LANES
        buf = forward_buffers[l]
        acc[...] = dot(w_ref[l, 4], buf[0:C, 0:CELLS]) + bias_cols[l]
        acc[:, 0:rest] += dot(w_ref[l, 7], buf[0:C, d * LANES : CELLS])
        acc[:, d * LANES : CELLS] += dot(w_ref[l, 1], buf[0:C, 0:rest])
        if l < 2:
            prepare_forward(l + 1)
        rim.roll_sides()
        prepare_backward(2 - l)
        rim.receive_sides()
        acc[...] += dot(w_side[l, 1], buf[C : 3 * C, 0:CELLS])
        acc[:, 0:rest] += dot(w_side[l, 2], buf[C : 3 * C, d * LANES : CELLS])
        acc[:, d * LANES : CELLS] += dot(w_side[l, 0], buf[C : 3 * C, 0:rest])

        def activate(first, last):
            v = acc[:, first:last]
            s = jax.nn.sigmoid(v)
            after = mask * (buf[0:C, first:last].astype(F32) + v * s)
            s = s * (1.0 + v * (1.0 - s))
            slope[l, :, first:last] = s
            if l < 2:
                forward_buffers[l + 1][0:C, first:last] = after.astype(BF)
            else:
                for r in range(first // LANES, last // LANES):
                    out_ref[r] = after[:, r * LANES - first : (r + 1) * LANES - first].astype(BF)
                t2[0:C, first:last] = (grad[:, first:last] * s).astype(BF)

        activate(0, rest)
        if l < 2:
            later = Rims(l + 1, forward_buffers[l + 1], 2 * d, True)
            later.turn(d, 2 * d)
            later.send_fold(d, 2 * d)
        else:
            later = Rims(3, t2, d, False)
        later.pack_sides(0, ROWS - d)
        rim.receive_corners()
        for number in range(len(rim.folds)):
            rim.receive_fold(number)
        acc[:, rest:CELLS] += dot(w_ref[l, 7], buf[0:C, CELLS : CELLS + d * LANES]) + dot(
            w_side[l, 2], buf[C : 3 * C, CELLS : CELLS + d * LANES]
        )
        activate(rest, CELLS)
        rim = later
        rim.turn(0, d)
        rim.pack_corners()
        rim.send_corners()
        if l < 2:
            rim.send_fold(0, d)
        else:
            rim.send_fold(d // 2, d)
            rim.send_fold(0, d // 2)
        rim.pack_sides(ROWS - d, ROWS)
        rim.send_sides()

    store(out_ref, out_hbm)
    reductions = {}
    for l in (2, 1, 0):
        d = 2**l
        rest = CELLS - d * LANES
        stored = forward_buffers[l]
        buf = backward_buffers[l]
        if l == 0:
            reductions[0] = weight_sums(0, buf, stored)
            rim.pack_sides(0, ROWS)
            rim.send_sides()
            for older in (0, 1, 2):
                next(reductions[older])
        else:
            reductions[l] = weight_sums(l, buf, stored)
            for older in range(l + 1, 3):
                next(reductions[older])
        acc[...] = dot(v_mid[l, 1], buf[0:C, 0:CELLS])
        acc[:, d * LANES : CELLS] += dot(v_mid[l, 2], buf[0:C, 0:rest])
        acc[:, 0:rest] += dot(v_mid[l, 0], buf[0:C, d * LANES : CELLS])
        rim.roll_sides()
        rim.receive_sides()
        if l == 0:
            for older in (0, 1, 2):
                next(reductions[older])
        acc[...] += dot(v_side[l, 1], buf[C : 3 * C, 0:CELLS])
        acc[:, d * LANES : CELLS] += dot(v_side[l, 2], buf[C : 3 * C, 0:rest])
        acc[:, 0:rest] += dot(v_side[l, 0], buf[C : 3 * C, d * LANES : CELLS])

        def descend(first, last):
            g = mask * (grad[:, first:last] + acc[:, first:last])
            if l > 0:
                grad[:, first:last] = g
                backward_buffers[l - 1][0:C, first:last] = (
                    g * slope[l - 1, :, first:last]
                ).astype(BF)
            else:
                for r in range(first // LANES, last // LANES):
                    fg_ref[r] = g[:, r * LANES - first : (r + 1) * LANES - first].astype(BF)

        descend(0, rest)
        if l > 0:
            for older in range(l, 3):
                next(reductions[older])
        rim.receive_corners()
        middle = d // 2
        for number, (fold, first, last) in enumerate(rim.folds):
            rim.receive_fold(number)
            top = slice(rest + first * LANES, rest + last * LANES)
            acc[:, top] += dot(
                v_over[l], buf[:, CELLS + first * LANES : CELLS + last * LANES]
            )
            descend(top.start, top.stop)
            if l > 0 and number == 0:
                later = Rims(6 - l, backward_buffers[l - 1], middle, False)
                later.turn(0, middle)
                later.pack_corners()
                later.send_corners()
                if middle > 1:
                    later.send_fold(middle // 2, middle)
                    later.send_fold(0, middle // 2)
                else:
                    later.send_fold(0, 1)
        if l > 0:
            rim = later
        if l > 1:
            rim.pack_sides(0, ROWS)
            rim.send_sides()

    store(fg_ref, fg_hbm)
    done = object()
    running = [reductions[l] for l in range(3)]
    while running:
        running = [reduction for reduction in running if next(reduction, done) is not done]
    for condition, copy in sends:
        if condition is None:
            copy.wait_send()
        else:

            @pl.when(condition)
            def _():
                copy.wait_send()

    for copy in stores:
        copy.wait()


def finish(
    rows_a,
    rows_b,
    summed,
    out_a,
    out_b,
    kernel_grad,
    bias_grad,
    rows,
    sums,
    spread_rows,
    cells,
    kernels,
    bias_rows,
    in_sem,
    out_sem,
):
    loads = [pltpu.make_async_copy(summed.at[l], sums.at[l], in_sem.at[l]) for l in range(3)]
    for number, src in enumerate((rows_a, rows_b)):
        loads.append(pltpu.make_async_copy(src, rows.at[number], in_sem.at[3 + number]))
    for load in loads:
        load.start()
    stores = []

    def store(src, dst):
        copy = pltpu.make_async_copy(src, dst, out_sem.at[len(stores)])
        copy.start()
        stores.append(copy)

    for l in range(3):
        loads[l].wait()
        for a in range(3):
            for b in range(3):
                first = a * WIDE + (1, 0, 2)[b] * C
                kernels[l, 3 * a + b] = sums[l, :, first : first + C].astype(F32)
            taps = pl.ds(3 * a, 3)
            store(kernels.at[l, taps], kernel_grad.at[l, taps])
        bias_rows[l : l + 1, :] = sums[l, :, 3 * WIDE : TOTAL].astype(F32).T[0:1]
    store(bias_rows, bias_grad)
    for number, dst in enumerate((out_a, out_b)):
        loads[3 + number].wait()
        for r in range(ROWS):
            spread_rows[pl.ds(r, C, stride=ROWS), :] = rows[number, r].astype(F32)
        cells[number] = spread_rows[...].reshape(C, ROWS, LANES).astype(BF)
        store(cells.at[number], dst)
    for copy in stores:
        copy.wait()


def shards(fields, cotangent, weights, biases, ocean_tiles, velocity_mask):
    n = lax.axis_size("tiles")
    hbm = pl.BlockSpec(memory_space=pltpu.HBM)
    out, field_grad, summed = pl.pallas_call(
        functools.partial(kernel, n),
        out_shape=(
            jax.ShapeDtypeStruct((ROWS, C, LANES), BF),
            jax.ShapeDtypeStruct((ROWS, C, LANES), BF),
            jax.ShapeDtypeStruct((3, C, TOTAL), BF),
        ),
        in_specs=[
            hbm,
            hbm,
            hbm,
            hbm,
            pl.BlockSpec(memory_space=pltpu.SMEM),
            hbm,
        ],
        out_specs=(hbm,) * 3,
        scratch_shapes=[
            pltpu.VMEM((3 * C, CELLS + LANES), BF),
            pltpu.VMEM((3 * C, CELLS + 2 * LANES), BF),
            pltpu.VMEM((3 * C, CELLS + 4 * LANES), BF),
            pltpu.VMEM((3 * C, CELLS + LANES), BF),
            pltpu.VMEM((3 * C, CELLS + 2 * LANES), BF),
            pltpu.VMEM((3 * C, CELLS + 4 * LANES), BF),
            pltpu.VMEM((C, ROWS, LANES), BF),
            pltpu.VMEM((C, ROWS, LANES), BF),
            pltpu.VMEM((3, C), F32),
            pltpu.VMEM((C,), jnp.int32),
            pltpu.VMEM((3, 9, C, C), BF),
            pltpu.VMEM((ROWS, C, LANES), BF),
            pltpu.VMEM((ROWS, C, LANES), BF),
            pltpu.VMEM((C * ROWS, LANES), F32),
            pltpu.VMEM((LANES, 2 * LANES), F32),
            pltpu.VMEM((3, C, CELLS), F32),
            pltpu.VMEM((C, CELLS), F32),
            pltpu.VMEM((C, CELLS), F32),
            pltpu.VMEM((3, 3, C, 2 * C), BF),
            pltpu.VMEM((3, 3, C, C), BF),
            pltpu.VMEM((3, 3, C, 2 * C), BF),
            pltpu.VMEM((3, C, 3 * C), BF),
            pltpu.VMEM((6, C, LANES), BF),
            pltpu.VMEM((C, LANES), F32),
            pltpu.VMEM((6, BAND, LANES), BF),
            pltpu.VMEM((6, C, 4 * LANES), BF),
            pltpu.VMEM((6, 2, C, LANES), BF),
            pltpu.VMEM((6, 2, BAND, LANES), BF),
            pltpu.VMEM((3, C, TOTAL), F32),
            pltpu.VMEM((3, C, HALF), BF),
            pltpu.VMEM((3, C, HALF), BF),
            pltpu.VMEM((3, C, HALF), BF),
            pltpu.VMEM((3, 3, BAND, HALF), BF),
            pltpu.VMEM((3, 4, BAND, HALF), BF),
            pltpu.VMEM((3, 4, BAND, HALF), BF),
            pltpu.VMEM((3, C, TOTAL), BF),
            pltpu.SemaphoreType.DMA((7,)),
            pltpu.SemaphoreType.DMA((5,)),
            pltpu.SemaphoreType.DMA((6, 6)),
            pltpu.SemaphoreType.DMA((6, 6)),
            pltpu.SemaphoreType.DMA((3, 40)),
            pltpu.SemaphoreType.DMA((3, 40)),
        ],
        compiler_params=pltpu.CompilerParams(
            collective_id=0, has_side_effects=True, vmem_limit_bytes=62 * 1024 * 1024
        ),
        cost_estimate=pl.CostEstimate(
            flops=18 * 9 * C * C * CELLS, bytes_accessed=8 * 1024 * 1024, transcendentals=9 * C * CELLS
        ),
    )(fields, cotangent, weights, biases, ocean_tiles, velocity_mask)
    return pl.pallas_call(
        finish,
        out_shape=(
            jax.ShapeDtypeStruct((C, ROWS, LANES), BF),
            jax.ShapeDtypeStruct((C, ROWS, LANES), BF),
            jax.ShapeDtypeStruct((3, 9, C, C), F32),
            jax.ShapeDtypeStruct((3, C), F32),
        ),
        in_specs=[hbm] * 3,
        out_specs=(hbm,) * 4,
        scratch_shapes=[
            pltpu.VMEM((2, ROWS, C, LANES), BF),
            pltpu.VMEM((3, C, TOTAL), BF),
            pltpu.VMEM((C * ROWS, LANES), F32),
            pltpu.VMEM((2, C, ROWS, LANES), BF),
            pltpu.VMEM((3, 9, C, C), F32),
            pltpu.VMEM((3, C), F32),
            pltpu.SemaphoreType.DMA((5,)),
            pltpu.SemaphoreType.DMA((12,)),
        ],
        compiler_params=pltpu.CompilerParams(vmem_limit_bytes=62 * 1024 * 1024),
    )(out, field_grad, summed)


def solution(mesh):
    placed = (P(None, None, "tiles"), P(None, None, "tiles"), P(), P(), P(None, "tiles"), P())
    return jax.shard_map(
        shards,
        mesh=mesh,
        in_specs=placed,
        out_specs=(P(None, None, "tiles"), P(None, None, "tiles"), P(), P()),
        check_vma=False,
    )
```

```python
import functools

import jax
import jax.numpy as jnp
from jax import lax
from jax.experimental import pallas as pl
from jax.experimental.pallas import tpu as pltpu
from jax.sharding import PartitionSpec as P

C = 192
ROWS = 8
LANES = 128
CELLS = ROWS * LANES
WIDE = 640
TOTAL = 2048
HALF = TOTAL // 2
BAND = C // 4
BF = jnp.bfloat16
F32 = jnp.float32
MESH = pl.DeviceIdType.MESH

CORE = (1, 2)
Y = (2, 4)
X = (8, 4)
Z = (32, 4)
PARTS = (
    (pl.ds(0, 384), (Y, X, Z)),
    (pl.ds(384, 384), (Z, Y, X)),
    (pl.ds(768, 256), (X, Z, Y)),
)


def coordinate(me, axis):
    return lax.rem(lax.div(me, axis[0]), axis[1])


def with_coordinate(me, axis, value):
    return me + (value - coordinate(me, axis)) * axis[0]


def copy_to(src, dst, send_sem, recv_sem, device):
    return pltpu.make_async_remote_copy(
        src_ref=src,
        dst_ref=dst,
        send_sem=send_sem,
        recv_sem=recv_sem,
        device_id=(device,),
        device_id_type=MESH,
    )


def start_if(condition, copy):
    @pl.when(condition)
    def _():
        copy.start()


def dot(a, b):
    return jnp.dot(a, b, preferred_element_type=F32)


def dot_nt(a, b):
    return lax.dot_general(a, b, (((1,), (1,)), ((), ())), preferred_element_type=F32)


def kernel(
    n,
    x_hbm,
    ct_hbm,
    w_hbm,
    bias_hbm,
    ocean_ref,
    velocity_hbm,
    out_hbm,
    fg_hbm,
    dw_hbm,
    s0,
    s1,
    s2,
    t0,
    t1,
    t2,
    x_ref,
    ct_ref,
    bias_ref,
    velocity_ref,
    w_ref,
    out_ref,
    fg_ref,
    spread_rows,
    cols_ref,
    slope,
    acc,
    grad,
    w_side,
    v_mid,
    v_side,
    v_over,
    packed,
    side_tile,
    own_tile,
    strip_cols,
    w_own,
    w_turn,
    corner,
    turned,
    rims,
    corners,
    partial,
    to_mate,
    from_mate,
    a_out,
    a_in,
    b_in,
    c_in,
    full,
    w_sem,
    out_sem,
    ex_send,
    ex_recv,
    ar_send,
    ar_recv,
):
    me = lax.axis_index("tiles")
    east = lax.rem(me + 1, n)
    west = lax.rem(me + n - 1, n)
    mirror = n - 1 - me
    fold_a = lax.rem(n - me, n)
    fold_b = lax.rem(2 * n - 2 - me, n)
    mate = with_coordinate(me, CORE, 1 - coordinate(me, CORE))
    core = coordinate(me, CORE)
    a_away = fold_a != me
    b_away = fold_b != me

    barrier = pltpu.get_barrier_semaphore()
    partners = [east, west, mirror, mate]
    for axis in (Y, X, Z):
        for step in (1, 2, 3):
            partners.append(
                with_coordinate(me, axis, lax.rem(coordinate(me, axis) + step, axis[1]))
            )
    for partner in partners:
        pl.semaphore_signal(barrier, inc=1, device_id=(partner,), device_id_type=MESH)

    @pl.when(a_away)
    def _():
        pl.semaphore_signal(barrier, inc=1, device_id=(fold_a,), device_id_type=MESH)

    @pl.when(b_away)
    def _():
        pl.semaphore_signal(barrier, inc=1, device_id=(fold_b,), device_id_type=MESH)

    small = [
        pltpu.make_async_copy(src, dst, w_sem.at[3 + number])
        for number, (src, dst) in enumerate(
            (
                (bias_hbm, bias_ref),
                (velocity_hbm, velocity_ref),
                (x_hbm, x_ref),
                (ct_hbm, ct_ref),
            )
        )
    ]
    loads = [
        pltpu.make_async_copy(w_hbm.at[l], w_ref.at[l], w_sem.at[l]) for l in range(3)
    ]
    for load in small + loads:
        load.start()

    lane = lax.broadcasted_iota(jnp.int32, (C, LANES), 1)
    flip_matrix = (
        lax.broadcasted_iota(jnp.int32, (LANES, LANES), 0)
        + lax.broadcasted_iota(jnp.int32, (LANES, LANES), 1)
        == LANES - 1
    ).astype(F32).astype(BF)
    cols_ref[...] = jnp.zeros((LANES, 2 * LANES), F32)
    small[0].wait()
    small[1].wait()
    cols_ref[0:3, 0:C] = bias_ref[...]
    cols_ref[3:4, 0:C] = (1 - 2 * velocity_ref[...]).astype(F32).reshape(1, C)
    turned_cols = cols_ref[...].T[0:C]
    bias_cols = [turned_cols[:, l : l + 1] for l in range(3)]
    flip_sign = turned_cols[:, 3:4]
    mask = ocean_ref[0, 0].astype(F32)
    sends = []

    stores = []

    def store(src, dst):
        copy = pltpu.make_async_copy(src, dst, out_sem.at[len(stores)])
        copy.start()
        stores.append(copy)

    def columns(row, count=1):
        return slice(row * LANES, (row + count) * LANES)

    def dense(tile, groups):
        size = C // groups
        total = tile[0:size]
        for q in range(1, groups):
            piece = tile[q * size : (q + 1) * size]
            total = total + pltpu.roll(piece, q * LANES // groups, 1)
        return total.astype(BF)

    def loose(total, groups):
        total = total.astype(F32)
        return jnp.concatenate(
            [total]
            + [pltpu.roll(total, LANES - q * LANES // groups, 1) for q in range(1, groups)],
            axis=0,
        )

    def slots(rows, count):
        tile = jnp.zeros((C, LANES), F32)
        for r in range(count):
            here = jnp.logical_and(lane >= 8 * r, lane < 8 * r + 8)
            tile = jnp.where(here, pltpu.roll(rows(r).astype(F32), (8 * r + 4) % LANES, 1), tile)
        return tile

    def widen(buf, rim, row, d):
        center = buf[0:C, columns(row)].astype(F32)
        left = pltpu.roll(rim, (-(8 * row + 4 - d)) % LANES, 1)
        right = pltpu.roll(rim, (-(8 * row + 4 + d)) % LANES, 1)
        buf[C : 2 * C, columns(row)] = jnp.where(
            lane < d, left, pltpu.roll(center, d, 1)
        ).astype(BF)
        buf[2 * C : 3 * C, columns(row)] = jnp.where(
            lane >= LANES - d, right, pltpu.roll(center, LANES - d, 1)
        ).astype(BF)

    class Rims:
        def __init__(self, e, buf, d, signed):
            self.e, self.buf, self.d, self.signed = e, buf, d, signed
            self.folds = []
            self.groups = 4 if d <= 2 else 2

        def turn(self, first, last):
            for k in range(first, last):
                row = dot(self.buf[0:C, columns(ROWS - 1 - k)], flip_matrix)
                if self.signed:
                    row = row * flip_sign
                turned[self.e, :, columns(k)] = row.astype(BF)

        def send_fold(self, first, last):
            slot = 4 + len(self.folds)
            fold = copy_to(
                turned.at[self.e, :, pl.ds(first * LANES, (last - first) * LANES)],
                self.buf.at[pl.ds(0, C), pl.ds(CELLS + first * LANES, (last - first) * LANES)],
                ex_send.at[self.e, slot],
                ex_recv.at[self.e, slot],
                mirror,
            )
            fold.start()
            self.folds.append((fold, first, last))
            sends.append((None, fold))

        def pack(self, tile, rows, first, last):
            d = self.d
            for r in range(first, last):
                at = 2 * d * r
                here = jnp.logical_and(lane >= at, lane < at + 2 * d)
                tile = jnp.where(here, pltpu.roll(rows(r).astype(F32), (at + d) % LANES, 1), tile)
            return tile

        def pack_sides(self, first, last):
            tile = jnp.zeros((C, LANES), F32) if first == 0 else side_tile[...]
            side_tile[...] = self.pack(
                tile, lambda r: self.buf[0:C, columns(r)], first, last
            )
            if last == ROWS:
                packed[self.e, 0 : C // self.groups] = dense(side_tile[...], self.groups)

        def pack_corners(self):
            tile = self.pack(
                jnp.zeros((C, LANES), F32), lambda k: turned[self.e, :, columns(k)], 0, self.d
            )
            corner[self.e] = dense(tile, 4)

        def send_sides(self):
            self.sides = []
            for slot, target in enumerate((east, west)):
                copy = copy_to(
                    packed.at[self.e, pl.ds(0, C // self.groups)],
                    rims.at[self.e, slot, pl.ds(0, C // self.groups)],
                    ex_send.at[self.e, slot],
                    ex_recv.at[self.e, slot],
                    target,
                )
                copy.start()
                self.sides.append(copy)
                sends.append((None, copy))

        def send_corners(self):
            self.turns = []
            for slot, target, away in ((0, fold_a, a_away), (1, fold_b, b_away)):
                copy = copy_to(
                    corner.at[self.e],
                    corners.at[self.e, slot],
                    ex_send.at[self.e, 2 + slot],
                    ex_recv.at[self.e, 2 + slot],
                    target,
                )
                start_if(away, copy)
                self.turns.append((away, copy))
                sends.append((away, copy))

        def unpack(self, rim, row, slot):
            buf, d = self.buf, self.d
            center = buf[0:C, columns(row)].astype(F32)
            edge = pltpu.roll(rim, (-(2 * d * slot + d)) % LANES, 1)
            left = pltpu.roll(jnp.where(lane >= LANES - d, edge, center), d, 1)
            right = pltpu.roll(jnp.where(lane < d, edge, center), LANES - d, 1)
            buf[C : 2 * C, columns(row)] = left.astype(BF)
            buf[2 * C : 3 * C, columns(row)] = right.astype(BF)

        def roll_sides(self):
            buf, d = self.buf, self.d
            for r in range(ROWS):
                center = buf[0:C, columns(r)].astype(F32)
                buf[C : 2 * C, columns(r)] = pltpu.roll(center, d, 1).astype(BF)
                buf[2 * C : 3 * C, columns(r)] = pltpu.roll(center, LANES - d, 1).astype(BF)

        def receive_sides(self):
            buf, d = self.buf, self.d
            for copy in self.sides:
                copy.wait_recv()
            size = C // self.groups
            low = lax.rem(lane, 2 * d) < d
            rim = jnp.where(
                low,
                loose(rims[self.e, 0, 0:size], self.groups),
                loose(rims[self.e, 1, 0:size], self.groups),
            )
            for r in range(ROWS + 1):
                edge = pltpu.roll(rim, (-2 * d * r) % LANES, 1) if r > 0 else rim
                if r < ROWS:
                    old = buf[C : 2 * C, columns(r)].astype(F32)
                    buf[C : 2 * C, columns(r)] = jnp.where(lane < d, edge, old).astype(BF)
                if r > 0:
                    old = buf[2 * C : 3 * C, columns(r - 1)].astype(F32)
                    buf[2 * C : 3 * C, columns(r - 1)] = jnp.where(
                        lane >= LANES - d, edge, old
                    ).astype(BF)

        def receive_corners(self):
            for slot, (away, copy) in enumerate(self.turns):

                @pl.when(away)
                def _():
                    copy.wait_recv()

                @pl.when(jnp.logical_not(away))
                def _():
                    corners[self.e, slot] = corner[self.e]

            low = lax.rem(lane, 2 * self.d) < self.d
            tiles = [loose(corners[self.e, slot], 4) for slot in range(2)]
            self.rim = jnp.where(low, tiles[0], tiles[1])

        def receive_fold(self, number):
            fold, first, last = self.folds[number]
            fold.wait_recv()
            for k in range(first, last):
                self.unpack(self.rim, ROWS + k, k)

    def all_reduce(l):
        half = pl.ds(pl.multiple_of(core * HALF, LANES), HALF)
        other = pl.ds(pl.multiple_of((1 - core) * HALF, LANES), HALF)
        count = [0]

        def post(src, dst, target):
            number = count[0]
            count[0] += 1
            copy = copy_to(src, dst, ar_send.at[l, number], ar_recv.at[l, number], target)
            copy.start()
            sends.append((None, copy))
            return copy

        def around(axis):
            for step in (1, 2, 3):
                to = lax.rem(coordinate(me, axis) + step, 4)
                yield step - 1, to, with_coordinate(me, axis, to)

        def exchange(total, landing, axis, lanes):
            mine = coordinate(me, axis)
            landing[mine, :, lanes] = total.astype(BF)
            piece = landing.at[mine, :, lanes]
            return [post(piece, piece, target) for slot, to, target in around(axis)]

        def arrived(landing, copies, lanes):
            for copy in copies:
                copy.wait_recv()
            total = landing[0, :, lanes].astype(F32)
            for slot in range(1, 4):
                total = total + landing[slot, :, lanes].astype(F32)
            return total

        to_mate[l] = partial[l, :, other].astype(BF)
        copy = post(to_mate.at[l], from_mate.at[l], mate)
        yield
        copy.wait_recv()
        a_out[l] = (partial[l, :, half] + from_mate[l].astype(F32)).astype(BF)
        waits = []
        for lanes, axes in PARTS:
            waits.append(
                [
                    post(
                        a_out.at[l, pl.ds(pl.multiple_of(to * BAND, 16), BAND), lanes],
                        a_in.at[l, slot, :, lanes],
                        target,
                    )
                    for slot, to, target in around(axes[0])
                ]
            )
        yield
        for part, (lanes, axes) in enumerate(PARTS):
            for copy in waits[part]:
                copy.wait_recv()
            band = pl.ds(pl.multiple_of(coordinate(me, axes[0]) * BAND, 16), BAND)
            total = a_out[l, band, lanes].astype(F32)
            for slot in range(3):
                total = total + a_in[l, slot, :, lanes].astype(F32)
            waits[part] = exchange(total, b_in.at[l], axes[1], lanes)
        yield
        for part, (lanes, axes) in enumerate(PARTS):
            total = arrived(b_in.at[l], waits[part], lanes)
            waits[part] = exchange(total, c_in.at[l], axes[2], lanes)
        yield
        for part, (lanes, axes) in enumerate(PARTS):
            total = arrived(c_in.at[l], waits[part], lanes)
            band = pl.ds(pl.multiple_of(coordinate(me, axes[0]) * BAND, 16), BAND)
            here = pl.ds(pl.multiple_of(core * HALF + lanes.start, LANES), lanes.size)
            full[l, band, here] = total.astype(BF)
            piece = full.at[l, band, here]
            waits[part] = [post(piece, piece, target) for slot, to, target in around(axes[0])]
        yield
        final = []
        for part, (lanes, axes) in enumerate(PARTS):
            for copy in waits[part]:
                copy.wait_recv()
            here = pl.ds(pl.multiple_of(core * HALF + lanes.start, LANES), lanes.size)
            piece = full.at[l, :, here]
            final.append(post(piece, piece, mate))
        yield
        for copy in final:
            copy.wait_recv()
        store(full.at[l], dw_hbm.at[l])
        yield

    def weight_sums(l, delta, stored):
        d = 2**l
        rest = CELLS - d * LANES
        for a in range(3):
            partial[l, :, a * WIDE + 512 : (a + 1) * WIDE] = jnp.zeros((C, LANES), F32)
        partial[l, :, 0:576] = dot_nt(delta[0:C, d * LANES : CELLS], stored[:, 0:rest])
        partial[l, :, 640:1216] = dot_nt(delta[0:C, 0:CELLS], stored[:, 0:CELLS])
        partial[l, :, 1280:1856] = dot_nt(
            delta[0:C, 0:CELLS], stored[:, d * LANES : CELLS + d * LANES]
        )
        partial[l, :, 1920:2048] = jnp.broadcast_to(
            jnp.sum(delta[0:C, 0:CELLS].astype(F32), axis=1, keepdims=True), (C, LANES)
        )
        reduction = all_reduce(l)
        next(reduction)
        return reduction

    def prepare_forward(l):
        for a in range(3):
            w_side[l, a, :, 0:C] = w_ref[l, 3 * a]
            w_side[l, a, :, C : 2 * C] = w_ref[l, 3 * a + 2]

    def prepare_backward(l):
        for a in range(3):
            v_mid[l, a] = w_ref[l, 3 * a + 1].T
            v_side[l, a, :, 0:C] = w_ref[l, 3 * a + 2].T
            v_side[l, a, :, C : 2 * C] = w_ref[l, 3 * a].T
        for place, tap in enumerate((7, 6, 8)):
            v_over[l, :, place * C : (place + 1) * C] = (
                w_ref[l, tap].T.astype(F32) * flip_sign
            ).astype(BF)

    forward_buffers = (s0, s1, s2)
    backward_buffers = (t0, t1, t2)

    small[2].wait()
    spread_rows[...] = x_ref[...].astype(F32).reshape(C * ROWS, LANES)
    for r in range(ROWS):
        row = spread_rows[pl.ds(r, C, stride=ROWS), :]
        s0[0:C, columns(r)] = (row * mask).astype(BF)
    rim = Rims(0, s0, 1, True)
    rim.turn(0, 3)
    own_tile[...] = slots(lambda r: s0[0:C, columns(r)], ROWS)
    packed[0, 0 : C // 2] = dense(own_tile[...], 2)
    packed[0, C // 2 : C // 2 + 16] = jnp.full((16, LANES), mask, F32).astype(BF)
    tile = slots(lambda k: turned[0, :, columns(k)], 3)
    tile = jnp.where(jnp.logical_and(lane >= 24, lane < 32), mask, tile)
    corner[0] = dense(tile, 4)
    loads[0].wait()
    prepare_forward(0)
    for a in range(3):
        for place, b in enumerate((1, 0, 2)):
            part = slice(place * C, (place + 1) * C)
            w_own[a, :, part] = w_ref[0, 3 * a + b]
            w_turn[a, :, part] = (w_ref[0, 8 - 3 * a - b].astype(F32) * cols_ref[3:4, 0:C]).astype(
                BF
            )
    small[3].wait()
    spread_rows[...] = ct_ref[...].astype(F32).reshape(C * ROWS, LANES)
    for r in range(ROWS):
        grad[:, columns(r)] = mask * spread_rows[pl.ds(r, C, stride=ROWS), :]
    loads[1].wait()
    loads[2].wait()
    pl.semaphore_wait(
        barrier, len(partners) + a_away.astype(jnp.int32) + b_away.astype(jnp.int32)
    )
    sides = [
        copy_to(
            packed.at[0, pl.ds(0, C // 2 + 16)],
            rims.at[0, slot, pl.ds(0, C // 2 + 16)],
            ex_send.at[0, slot],
            ex_recv.at[0, slot],
            target,
        )
        for slot, target in enumerate((east, west))
    ]
    over = copy_to(
        corner.at[0], corners.at[0, 2], ex_send.at[0, 5], ex_recv.at[0, 5], mirror
    )
    for copy in sides + [over]:
        copy.start()
        sends.append((None, copy))
    rim.send_corners()
    rim.send_fold(0, 3)

    def activate(l, buf, first, last):
        v = acc[:, first:last]
        s = jax.nn.sigmoid(v)
        after = mask * (buf[0:C, first:last].astype(F32) + v * s)
        s = s * (1.0 + v * (1.0 - s))
        slope[l, :, first:last] = s
        if l < 2:
            forward_buffers[l + 1][0:C, first:last] = after.astype(BF)
        else:
            for r in range(first // LANES, last // LANES):
                out_ref[r] = after[:, r * LANES - first : (r + 1) * LANES - first].astype(BF)
            t2[0:C, first:last] = (grad[:, first:last] * s).astype(BF)

    rest = CELLS - LANES
    acc[...] = dot(w_ref[0, 4], s0[0:C, 0:CELLS]) + bias_cols[0]
    acc[:, 0:rest] += dot(w_ref[0, 7], s0[0:C, LANES:CELLS])
    acc[:, LANES:CELLS] += dot(w_ref[0, 1], s0[0:C, 0:rest])
    prepare_forward(1)
    prepare_backward(2)
    for copy in sides:
        copy.wait_recv()
    low = lax.rem(lane, 8) < 4
    west_tile = loose(rims[0, 0, 0 : C // 2], 2)
    east_tile = loose(rims[0, 1, 0 : C // 2], 2)
    rim_tile = jnp.where(low, west_tile, east_tile)
    for r in range(ROWS):
        widen(s0, rim_tile, r, 1)
    acc[...] += dot(w_side[0, 1], s0[C : 3 * C, 0:CELLS])
    acc[:, 0:rest] += dot(w_side[0, 2], s0[C : 3 * C, LANES:CELLS])
    acc[:, LANES:CELLS] += dot(w_side[0, 0], s0[C : 3 * C, 0:rest])
    activate(0, s0, 0, rest)

    for slot, (away, copy) in enumerate(rim.turns):

        @pl.when(away)
        def _():
            copy.wait_recv()

        @pl.when(jnp.logical_not(away))
        def _():
            corners[0, slot] = corner[0]

    over.wait_recv()
    far_a, far_b, far = (pltpu.roll(loose(corners[0, slot], 4), 64, 1) for slot in range(3))
    inside = lane < 64
    beyond = lane < 88
    strips = [
        jnp.where(
            inside,
            jnp.where(low, west_tile, own_tile[...]),
            jnp.where(beyond, jnp.where(low, far_a, far), 0.0),
        ),
        jnp.where(
            inside,
            jnp.where(low, own_tile[...], east_tile),
            jnp.where(beyond, jnp.where(low, far, far_b), 0.0),
        ),
    ]
    rim_tile = jnp.where(low, strips[0], strips[1])
    for a in range(3):
        for place, b in enumerate((0, -1, 1)):
            shift = (-(8 * (a - 1) + b)) % LANES
            for side in range(2):
                moved = pltpu.roll(strips[side], shift, 1) if shift else strips[side]
                strip_cols[
                    (3 * a + place) * C : (3 * a + place + 1) * C, columns(side)
                ] = moved.astype(BF)
    own_sum = bias_cols[0]
    far_sum = bias_cols[0]
    for a in range(3):
        taps = strip_cols[3 * C * a : 3 * C * (a + 1), :]
        own_sum = own_sum + dot(w_own[a], taps)
        far_sum = far_sum + dot(w_turn[a], taps)
    after = []
    for side in range(2):
        v = jnp.where(inside, own_sum[:, columns(side)], far_sum[:, columns(side)])
        v = v * jax.nn.sigmoid(v)
        v = jnp.where(inside, v, v * flip_sign)
        near_mask = rims[0, side, C // 2 : C // 2 + 1, 0:1].astype(F32)
        far_mask = corners[0, side, 0:1, 24:25].astype(F32)
        side_mask = jnp.where(inside[0:1], near_mask, far_mask)
        after.append((side_mask * (strips[side] + v)).astype(BF).astype(F32))
    next_tile = jnp.where(low, after[0], after[1])
    for r in range(ROWS - 1):
        widen(s1, next_tile, r, 2)

    def second(first, last):
        step = 2 * LANES
        acc[:, first:last] = (
            dot(w_ref[1, 4], s1[0:C, first:last])
            + dot(w_side[1, 1], s1[C : 3 * C, first:last])
            + bias_cols[1]
        )
        acc[:, first:last] += dot(w_ref[1, 7], s1[0:C, first + step : last + step]) + dot(
            w_side[1, 2], s1[C : 3 * C, first + step : last + step]
        )
        low_row = max(first, step)
        acc[:, low_row:last] += dot(w_ref[1, 1], s1[0:C, low_row - step : last - step]) + dot(
            w_side[1, 0], s1[C : 3 * C, low_row - step : last - step]
        )
        activate(1, s1, first, last)

    second(0, 4 * LANES)
    later = Rims(2, s2, 4, True)
    later.pack_sides(0, 4)
    prepare_forward(2)

    rim.folds[0][0].wait_recv()
    for k in range(3):
        widen(s0, rim_tile, ROWS + k, 1)
    acc[:, rest:CELLS] += dot(w_ref[0, 7], s0[0:C, CELLS : CELLS + LANES]) + dot(
        w_side[0, 2], s0[C : 3 * C, CELLS : CELLS + LANES]
    )
    activate(0, s0, rest, CELLS)
    v = bias_cols[0]
    for a in range(3):
        v = v + dot(w_turn[a], s0[:, columns(7 + a, 2)])
    v = v * jax.nn.sigmoid(v) * flip_sign
    far_mask = corners[0, 2, 0:1, 24:25].astype(F32)
    s1[0:C, columns(ROWS, 2)] = (far_mask * (s0[0:C, columns(ROWS, 2)].astype(F32) + v)).astype(BF)
    for r in range(ROWS - 1, ROWS + 2):
        widen(s1, next_tile, r, 2)
    second(4 * LANES, CELLS)
    rim = later
    rim.turn(0, 4)
    rim.pack_corners()
    rim.send_corners()
    rim.send_fold(0, 2)
    rim.send_fold(2, 4)
    rim.pack_sides(4, ROWS)
    rim.send_sides()

    d = 4
    rest = CELLS - d * LANES
    acc[...] = dot(w_ref[2, 4], s2[0:C, 0:CELLS]) + bias_cols[2]
    acc[:, 0:rest] += dot(w_ref[2, 7], s2[0:C, d * LANES : CELLS])
    acc[:, d * LANES : CELLS] += dot(w_ref[2, 1], s2[0:C, 0:rest])
    rim.roll_sides()
    prepare_backward(1)
    prepare_backward(0)
    rim.receive_sides()
    acc[...] += dot(w_side[2, 1], s2[C : 3 * C, 0:CELLS])
    acc[:, 0:rest] += dot(w_side[2, 2], s2[C : 3 * C, d * LANES : CELLS])
    acc[:, d * LANES : CELLS] += dot(w_side[2, 0], s2[C : 3 * C, 0:rest])
    activate(2, s2, 0, rest)
    later = Rims(3, t2, d, False)
    later.pack_sides(0, ROWS - d)
    rim.receive_corners()
    for number, (fold, first, last) in enumerate(rim.folds):
        rim.receive_fold(number)
        top = slice(rest + first * LANES, rest + last * LANES)
        over = slice(CELLS + first * LANES, CELLS + last * LANES)
        acc[:, top] += dot(w_ref[2, 7], s2[0:C, over]) + dot(w_side[2, 2], s2[C : 3 * C, over])
        activate(2, s2, top.start, top.stop)
        later.turn(d - last, d - first)
        if number == 0:
            later.send_fold(d - last, d - first)
    rim = later
    rim.pack_corners()
    rim.send_corners()
    rim.send_fold(0, d // 2)
    rim.pack_sides(ROWS - d, ROWS)
    rim.send_sides()

    store(out_ref, out_hbm)
    reductions = {}
    for l in (2, 1, 0):
        d = 2**l
        rest = CELLS - d * LANES
        stored = forward_buffers[l]
        buf = backward_buffers[l]
        if l == 0:
            reductions[0] = weight_sums(0, buf, stored)
            rim.pack_sides(0, ROWS)
            rim.send_sides()
            for older in (0, 1, 2):
                next(reductions[older])
        else:
            reductions[l] = weight_sums(l, buf, stored)
            for older in range(l + 1, 3):
                next(reductions[older])
        acc[...] = dot(v_mid[l, 1], buf[0:C, 0:CELLS])
        acc[:, d * LANES : CELLS] += dot(v_mid[l, 2], buf[0:C, 0:rest])
        acc[:, 0:rest] += dot(v_mid[l, 0], buf[0:C, d * LANES : CELLS])
        rim.roll_sides()
        rim.receive_sides()
        if l == 0:
            for older in (0, 1, 2):
                next(reductions[older])
        acc[...] += dot(v_side[l, 1], buf[C : 3 * C, 0:CELLS])
        acc[:, d * LANES : CELLS] += dot(v_side[l, 2], buf[C : 3 * C, 0:rest])
        acc[:, 0:rest] += dot(v_side[l, 0], buf[C : 3 * C, d * LANES : CELLS])

        def descend(first, last):
            g = mask * (grad[:, first:last] + acc[:, first:last])
            if l > 0:
                grad[:, first:last] = g
                backward_buffers[l - 1][0:C, first:last] = (
                    g * slope[l - 1, :, first:last]
                ).astype(BF)
            else:
                for r in range(first // LANES, last // LANES):
                    fg_ref[r] = g[:, r * LANES - first : (r + 1) * LANES - first].astype(BF)

        descend(0, rest)
        if l > 0:
            next(reductions[l])
        rim.receive_corners()
        middle = d // 2
        for number, (fold, first, last) in enumerate(rim.folds):
            rim.receive_fold(number)
            top = slice(rest + first * LANES, rest + last * LANES)
            acc[:, top] += dot(
                v_over[l], buf[:, CELLS + first * LANES : CELLS + last * LANES]
            )
            descend(top.start, top.stop)
            if l > 0 and number == 0:
                later = Rims(6 - l, backward_buffers[l - 1], middle, False)
                later.turn(0, middle)
                later.pack_corners()
                later.send_corners()
                if middle > 1:
                    later.send_fold(middle // 2, middle)
                    later.send_fold(0, middle // 2)
                else:
                    later.send_fold(0, 1)
        if l > 0:
            rim = later
        if l > 1:
            rim.pack_sides(0, ROWS)
            rim.send_sides()

    store(fg_ref, fg_hbm)
    done = object()
    running = [reductions[l] for l in range(3)]
    while running:
        running = [reduction for reduction in running if next(reduction, done) is not done]
    for condition, copy in sends:
        if condition is None:
            copy.wait_send()
        else:

            @pl.when(condition)
            def _():
                copy.wait_send()

    for copy in stores:
        copy.wait()


def finish(
    rows_a,
    rows_b,
    summed,
    out_a,
    out_b,
    kernel_grad,
    bias_grad,
    rows,
    sums,
    spread_rows,
    cells,
    kernels,
    bias_rows,
    in_sem,
    out_sem,
):
    loads = [pltpu.make_async_copy(summed.at[l], sums.at[l], in_sem.at[l]) for l in range(3)]
    for number, src in enumerate((rows_a, rows_b)):
        loads.append(pltpu.make_async_copy(src, rows.at[number], in_sem.at[3 + number]))
    for load in loads:
        load.start()
    stores = []

    def store(src, dst):
        copy = pltpu.make_async_copy(src, dst, out_sem.at[len(stores)])
        copy.start()
        stores.append(copy)

    for l in range(3):
        loads[l].wait()
        for a in range(3):
            for b in range(3):
                first = a * WIDE + (1, 0, 2)[b] * C
                kernels[l, 3 * a + b] = sums[l, :, first : first + C].astype(F32)
            taps = pl.ds(3 * a, 3)
            store(kernels.at[l, taps], kernel_grad.at[l, taps])
        bias_rows[l : l + 1, :] = sums[l, :, 3 * WIDE : TOTAL].astype(F32).T[0:1]
    store(bias_rows, bias_grad)
    for number, dst in enumerate((out_a, out_b)):
        loads[3 + number].wait()
        for r in range(ROWS):
            spread_rows[pl.ds(r, C, stride=ROWS), :] = rows[number, r].astype(F32)
        cells[number] = spread_rows[...].reshape(C, ROWS, LANES).astype(BF)
        store(cells.at[number], dst)
    for copy in stores:
        copy.wait()


def shards(fields, cotangent, weights, biases, ocean_tiles, velocity_mask):
    n = lax.axis_size("tiles")
    hbm = pl.BlockSpec(memory_space=pltpu.HBM)
    out, field_grad, summed = pl.pallas_call(
        functools.partial(kernel, n),
        out_shape=(
            jax.ShapeDtypeStruct((ROWS, C, LANES), BF),
            jax.ShapeDtypeStruct((ROWS, C, LANES), BF),
            jax.ShapeDtypeStruct((3, C, TOTAL), BF),
        ),
        in_specs=[
            hbm,
            hbm,
            hbm,
            hbm,
            pl.BlockSpec(memory_space=pltpu.SMEM),
            hbm,
        ],
        out_specs=(hbm,) * 3,
        scratch_shapes=[
            pltpu.VMEM((3 * C, CELLS + 3 * LANES), BF),
            pltpu.VMEM((3 * C, CELLS + 2 * LANES), BF),
            pltpu.VMEM((3 * C, CELLS + 4 * LANES), BF),
            pltpu.VMEM((3 * C, CELLS + LANES), BF),
            pltpu.VMEM((3 * C, CELLS + 2 * LANES), BF),
            pltpu.VMEM((3 * C, CELLS + 4 * LANES), BF),
            pltpu.VMEM((C, ROWS, LANES), BF),
            pltpu.VMEM((C, ROWS, LANES), BF),
            pltpu.VMEM((3, C), F32),
            pltpu.VMEM((C,), jnp.int32),
            pltpu.VMEM((3, 9, C, C), BF),
            pltpu.VMEM((ROWS, C, LANES), BF),
            pltpu.VMEM((ROWS, C, LANES), BF),
            pltpu.VMEM((C * ROWS, LANES), F32),
            pltpu.VMEM((LANES, 2 * LANES), F32),
            pltpu.VMEM((3, C, CELLS), F32),
            pltpu.VMEM((C, CELLS), F32),
            pltpu.VMEM((C, CELLS), F32),
            pltpu.VMEM((3, 3, C, 2 * C), BF),
            pltpu.VMEM((3, 3, C, C), BF),
            pltpu.VMEM((3, 3, C, 2 * C), BF),
            pltpu.VMEM((3, C, 3 * C), BF),
            pltpu.VMEM((6, C, LANES), BF),
            pltpu.VMEM((C, LANES), F32),
            pltpu.VMEM((C, LANES), F32),
            pltpu.VMEM((9 * C, 2 * LANES), BF),
            pltpu.VMEM((3, C, 3 * C), BF),
            pltpu.VMEM((3, C, 3 * C), BF),
            pltpu.VMEM((6, BAND, LANES), BF),
            pltpu.VMEM((6, C, 4 * LANES), BF),
            pltpu.VMEM((6, 2, C, LANES), BF),
            pltpu.VMEM((6, 3, BAND, LANES), BF),
            pltpu.VMEM((3, C, TOTAL), F32),
            pltpu.VMEM((3, C, HALF), BF),
            pltpu.VMEM((3, C, HALF), BF),
            pltpu.VMEM((3, C, HALF), BF),
            pltpu.VMEM((3, 3, BAND, HALF), BF),
            pltpu.VMEM((3, 4, BAND, HALF), BF),
            pltpu.VMEM((3, 4, BAND, HALF), BF),
            pltpu.VMEM((3, C, TOTAL), BF),
            pltpu.SemaphoreType.DMA((7,)),
            pltpu.SemaphoreType.DMA((5,)),
            pltpu.SemaphoreType.DMA((6, 6)),
            pltpu.SemaphoreType.DMA((6, 6)),
            pltpu.SemaphoreType.DMA((3, 40)),
            pltpu.SemaphoreType.DMA((3, 40)),
        ],
        compiler_params=pltpu.CompilerParams(
            collective_id=0, has_side_effects=True, vmem_limit_bytes=62 * 1024 * 1024
        ),
        cost_estimate=pl.CostEstimate(
            flops=18 * 9 * C * C * CELLS, bytes_accessed=8 * 1024 * 1024, transcendentals=9 * C * CELLS
        ),
    )(fields, cotangent, weights, biases, ocean_tiles, velocity_mask)
    return pl.pallas_call(
        finish,
        out_shape=(
            jax.ShapeDtypeStruct((C, ROWS, LANES), BF),
            jax.ShapeDtypeStruct((C, ROWS, LANES), BF),
            jax.ShapeDtypeStruct((3, 9, C, C), F32),
            jax.ShapeDtypeStruct((3, C), F32),
        ),
        in_specs=[hbm] * 3,
        out_specs=(hbm,) * 4,
        scratch_shapes=[
            pltpu.VMEM((2, ROWS, C, LANES), BF),
            pltpu.VMEM((3, C, TOTAL), BF),
            pltpu.VMEM((C * ROWS, LANES), F32),
            pltpu.VMEM((2, C, ROWS, LANES), BF),
            pltpu.VMEM((3, 9, C, C), F32),
            pltpu.VMEM((3, C), F32),
            pltpu.SemaphoreType.DMA((5,)),
            pltpu.SemaphoreType.DMA((12,)),
        ],
        compiler_params=pltpu.CompilerParams(vmem_limit_bytes=62 * 1024 * 1024),
    )(out, field_grad, summed)


def solution(mesh):
    placed = (P(None, None, "tiles"), P(None, None, "tiles"), P(), P(), P(None, "tiles"), P())
    return jax.shard_map(
        shards,
        mesh=mesh,
        in_specs=placed,
        out_specs=(P(None, None, "tiles"), P(None, None, "tiles"), P(), P()),
        check_vma=False,
    )
```

```python
import functools

import jax
import jax.numpy as jnp
from jax import lax
from jax.experimental import pallas as pl
from jax.experimental.pallas import tpu as pltpu
from jax.sharding import PartitionSpec as P

C = 192
ROWS = 8
LANES = 128
CELLS = ROWS * LANES
WIDE = 640
TOTAL = 2048
HALF = TOTAL // 2
BAND = C // 4
BF = jnp.bfloat16
F32 = jnp.float32
MESH = pl.DeviceIdType.MESH

CORE = (1, 2)
Y = (2, 4)
X = (8, 4)
Z = (32, 4)
PARTS = (
    (pl.ds(0, 384), (Y, X, Z)),
    (pl.ds(384, 384), (Z, Y, X)),
    (pl.ds(768, 256), (X, Z, Y)),
)


def coordinate(me, axis):
    return lax.rem(lax.div(me, axis[0]), axis[1])


def with_coordinate(me, axis, value):
    return me + (value - coordinate(me, axis)) * axis[0]


def copy_to(src, dst, send_sem, recv_sem, device):
    return pltpu.make_async_remote_copy(
        src_ref=src,
        dst_ref=dst,
        send_sem=send_sem,
        recv_sem=recv_sem,
        device_id=(device,),
        device_id_type=MESH,
    )


def start_if(condition, copy):
    @pl.when(condition)
    def _():
        copy.start()


def dot(a, b):
    return jnp.dot(a, b, preferred_element_type=F32)


def dot_nt(a, b):
    return lax.dot_general(a, b, (((1,), (1,)), ((), ())), preferred_element_type=F32)


def kernel(
    n,
    x_hbm,
    ct_hbm,
    w_hbm,
    bias_hbm,
    ocean_ref,
    velocity_hbm,
    out_hbm,
    fg_hbm,
    dw_hbm,
    s0,
    s1,
    s2,
    t0,
    t1,
    t2,
    x_ref,
    ct_ref,
    bias_ref,
    velocity_ref,
    w_ref,
    out_ref,
    fg_ref,
    spread_rows,
    cols_ref,
    slope,
    acc,
    grad,
    w_side,
    v_mid,
    v_side,
    v_over,
    packed,
    side_tile,
    own_tile,
    strip_cols,
    w_own,
    w_turn,
    corner,
    turned,
    rims,
    corners,
    partial,
    to_mate,
    from_mate,
    a_out,
    a_in,
    b_in,
    c_in,
    full,
    w_sem,
    out_sem,
    ex_send,
    ex_recv,
    ar_send,
    ar_recv,
):
    me = lax.axis_index("tiles")
    east = lax.rem(me + 1, n)
    west = lax.rem(me + n - 1, n)
    mirror = n - 1 - me
    fold_a = lax.rem(n - me, n)
    fold_b = lax.rem(2 * n - 2 - me, n)
    mate = with_coordinate(me, CORE, 1 - coordinate(me, CORE))
    core = coordinate(me, CORE)
    a_away = fold_a != me
    b_away = fold_b != me

    barrier = pltpu.get_barrier_semaphore()
    partners = [east, west, mirror, mate]
    for axis in (Y, X, Z):
        for step in (1, 2, 3):
            partners.append(
                with_coordinate(me, axis, lax.rem(coordinate(me, axis) + step, axis[1]))
            )
    for partner in partners:
        pl.semaphore_signal(barrier, inc=1, device_id=(partner,), device_id_type=MESH)

    @pl.when(a_away)
    def _():
        pl.semaphore_signal(barrier, inc=1, device_id=(fold_a,), device_id_type=MESH)

    @pl.when(b_away)
    def _():
        pl.semaphore_signal(barrier, inc=1, device_id=(fold_b,), device_id_type=MESH)

    small = [
        pltpu.make_async_copy(src, dst, w_sem.at[3 + number])
        for number, (src, dst) in enumerate(
            (
                (bias_hbm, bias_ref),
                (velocity_hbm, velocity_ref),
                (x_hbm, x_ref),
                (ct_hbm, ct_ref),
            )
        )
    ]
    loads = [
        pltpu.make_async_copy(w_hbm.at[l], w_ref.at[l], w_sem.at[l]) for l in range(3)
    ]
    for load in small + loads:
        load.start()

    lane = lax.broadcasted_iota(jnp.int32, (C, LANES), 1)
    flip_matrix = (
        lax.broadcasted_iota(jnp.int32, (LANES, LANES), 0)
        + lax.broadcasted_iota(jnp.int32, (LANES, LANES), 1)
        == LANES - 1
    ).astype(F32).astype(BF)
    cols_ref[...] = jnp.zeros((LANES, 2 * LANES), F32)
    small[0].wait()
    small[1].wait()
    cols_ref[0:3, 0:C] = bias_ref[...]
    cols_ref[3:4, 0:C] = (1 - 2 * velocity_ref[...]).astype(F32).reshape(1, C)
    turned_cols = cols_ref[...].T[0:C]
    bias_cols = [turned_cols[:, l : l + 1] for l in range(3)]
    flip_sign = turned_cols[:, 3:4]
    mask = ocean_ref[0, 0].astype(F32)
    sends = []

    stores = []

    def store(src, dst):
        copy = pltpu.make_async_copy(src, dst, out_sem.at[len(stores)])
        copy.start()
        stores.append(copy)

    def columns(row, count=1):
        return slice(row * LANES, (row + count) * LANES)

    def dense(tile, groups):
        size = C // groups
        total = tile[0:size]
        for q in range(1, groups):
            piece = tile[q * size : (q + 1) * size]
            total = total + pltpu.roll(piece, q * LANES // groups, 1)
        return total.astype(BF)

    def loose(total, groups):
        total = total.astype(F32)
        return jnp.concatenate(
            [total]
            + [pltpu.roll(total, LANES - q * LANES // groups, 1) for q in range(1, groups)],
            axis=0,
        )

    def slots(rows, count):
        tile = jnp.zeros((C, LANES), F32)
        for r in range(count):
            here = jnp.logical_and(lane >= 8 * r, lane < 8 * r + 8)
            tile = jnp.where(here, pltpu.roll(rows(r).astype(F32), (8 * r + 4) % LANES, 1), tile)
        return tile

    def widen(buf, rim, row, d):
        center = buf[0:C, columns(row)].astype(F32)
        left = pltpu.roll(rim, (-(8 * row + 4 - d)) % LANES, 1)
        right = pltpu.roll(rim, (-(8 * row + 4 + d)) % LANES, 1)
        buf[C : 2 * C, columns(row)] = jnp.where(
            lane < d, left, pltpu.roll(center, d, 1)
        ).astype(BF)
        buf[2 * C : 3 * C, columns(row)] = jnp.where(
            lane >= LANES - d, right, pltpu.roll(center, LANES - d, 1)
        ).astype(BF)

    class Rims:
        def __init__(self, e, buf, d, signed):
            self.e, self.buf, self.d, self.signed = e, buf, d, signed
            self.folds = []
            self.groups = 4 if d <= 2 else 2

        def turn(self, first, last):
            for k in range(first, last):
                row = dot(self.buf[0:C, columns(ROWS - 1 - k)], flip_matrix)
                if self.signed:
                    row = row * flip_sign
                turned[self.e, :, columns(k)] = row.astype(BF)

        def send_fold(self, first, last):
            slot = 4 + len(self.folds)
            fold = copy_to(
                turned.at[self.e, :, pl.ds(first * LANES, (last - first) * LANES)],
                self.buf.at[pl.ds(0, C), pl.ds(CELLS + first * LANES, (last - first) * LANES)],
                ex_send.at[self.e, slot],
                ex_recv.at[self.e, slot],
                mirror,
            )
            fold.start()
            self.folds.append((fold, first, last))
            sends.append((None, fold))

        def pack(self, tile, rows, first, last):
            d = self.d
            for r in range(first, last):
                at = 2 * d * r
                here = jnp.logical_and(lane >= at, lane < at + 2 * d)
                tile = jnp.where(here, pltpu.roll(rows(r).astype(F32), (at + d) % LANES, 1), tile)
            return tile

        def pack_sides(self, first, last):
            tile = jnp.zeros((C, LANES), F32) if first == 0 else side_tile[...]
            side_tile[...] = self.pack(
                tile, lambda r: self.buf[0:C, columns(r)], first, last
            )
            if last == ROWS:
                packed[self.e, 0 : C // self.groups] = dense(side_tile[...], self.groups)

        def pack_corners(self):
            tile = self.pack(
                jnp.zeros((C, LANES), F32), lambda k: turned[self.e, :, columns(k)], 0, self.d
            )
            corner[self.e] = dense(tile, 4)

        def send_sides(self):
            self.sides = []
            for slot, target in enumerate((east, west)):
                copy = copy_to(
                    packed.at[self.e, pl.ds(0, C // self.groups)],
                    rims.at[self.e, slot, pl.ds(0, C // self.groups)],
                    ex_send.at[self.e, slot],
                    ex_recv.at[self.e, slot],
                    target,
                )
                copy.start()
                self.sides.append(copy)
                sends.append((None, copy))

        def send_corners(self):
            self.turns = []
            for slot, target, away in ((0, fold_a, a_away), (1, fold_b, b_away)):
                copy = copy_to(
                    corner.at[self.e],
                    corners.at[self.e, slot],
                    ex_send.at[self.e, 2 + slot],
                    ex_recv.at[self.e, 2 + slot],
                    target,
                )
                start_if(away, copy)
                self.turns.append((away, copy))
                sends.append((away, copy))

        def unpack(self, rim, row, slot):
            buf, d = self.buf, self.d
            center = buf[0:C, columns(row)].astype(F32)
            edge = pltpu.roll(rim, (-(2 * d * slot + d)) % LANES, 1)
            left = pltpu.roll(jnp.where(lane >= LANES - d, edge, center), d, 1)
            right = pltpu.roll(jnp.where(lane < d, edge, center), LANES - d, 1)
            buf[C : 2 * C, columns(row)] = left.astype(BF)
            buf[2 * C : 3 * C, columns(row)] = right.astype(BF)

        def roll_sides(self):
            buf, d = self.buf, self.d
            for r in range(ROWS):
                center = buf[0:C, columns(r)].astype(F32)
                left = jnp.where(lane < d, 0.0, pltpu.roll(center, d, 1))
                right = jnp.where(lane >= LANES - d, 0.0, pltpu.roll(center, LANES - d, 1))
                buf[C : 2 * C, columns(r)] = left.astype(BF)
                buf[2 * C : 3 * C, columns(r)] = right.astype(BF)

        def receive_sides(self):
            buf, d = self.buf, self.d
            for copy in self.sides:
                copy.wait_recv()
            size = C // self.groups
            low = lax.rem(lane, 2 * d) < d
            rim = jnp.where(
                low,
                loose(rims[self.e, 0, 0:size], self.groups),
                loose(rims[self.e, 1, 0:size], self.groups),
            )
            for r in range(ROWS + 1):
                edge = pltpu.roll(rim, (-2 * d * r) % LANES, 1) if r > 0 else rim
                if r < ROWS:
                    old = buf[C : 2 * C, columns(r)].astype(F32)
                    buf[C : 2 * C, columns(r)] = jnp.where(lane < d, edge, old).astype(BF)
                if r > 0:
                    old = buf[2 * C : 3 * C, columns(r - 1)].astype(F32)
                    buf[2 * C : 3 * C, columns(r - 1)] = jnp.where(
                        lane >= LANES - d, edge, old
                    ).astype(BF)

        def receive_edges(self, l):
            d = self.d
            for copy in self.sides:
                copy.wait_recv()
            size = C // self.groups
            low = lax.rem(lane, 2 * d) < d
            rim = jnp.where(
                low,
                loose(rims[self.e, 0, 0:size], self.groups),
                loose(rims[self.e, 1, 0:size], self.groups),
            )
            rim = jnp.where(lane < 2 * d * ROWS, rim, 0.0)
            left = right = 0.0
            for a, shift in ((1, 0), (2, 2 * d * d), (0, LANES - 2 * d * d)):
                moved = (pltpu.roll(rim, shift, 1) if shift else rim).astype(BF)
                left = left + dot(v_side[l, a, :, 0:C], moved)
                right = right + dot(v_side[l, a, :, C : 2 * C], moved)
            both = jnp.where(low, left, right)
            edge = both
            for r in range(ROWS):
                after = pltpu.roll(both, (-2 * d * (r + 1)) % LANES, 1)
                acc[:, columns(r)] += jnp.where(
                    lane < d, edge, jnp.where(lane >= LANES - d, after, 0.0)
                )
                edge = after

        def receive_corners(self):
            for slot, (away, copy) in enumerate(self.turns):

                @pl.when(away)
                def _():
                    copy.wait_recv()

                @pl.when(jnp.logical_not(away))
                def _():
                    corners[self.e, slot] = corner[self.e]

            low = lax.rem(lane, 2 * self.d) < self.d
            tiles = [loose(corners[self.e, slot], 4) for slot in range(2)]
            self.rim = jnp.where(low, tiles[0], tiles[1])

        def receive_fold(self, number):
            fold, first, last = self.folds[number]
            fold.wait_recv()
            for k in range(first, last):
                self.unpack(self.rim, ROWS + k, k)

    def all_reduce(l):
        half = pl.ds(pl.multiple_of(core * HALF, LANES), HALF)
        other = pl.ds(pl.multiple_of((1 - core) * HALF, LANES), HALF)
        count = [0]

        def post(src, dst, target):
            number = count[0]
            count[0] += 1
            copy = copy_to(src, dst, ar_send.at[l, number], ar_recv.at[l, number], target)
            copy.start()
            sends.append((None, copy))
            return copy

        def around(axis):
            for step in (2, 1, 3):
                to = lax.rem(coordinate(me, axis) + step, 4)
                yield step - 1, to, with_coordinate(me, axis, to)

        def exchange(total, landing, axis, lanes):
            mine = coordinate(me, axis)
            landing[mine, :, lanes] = total.astype(BF)
            piece = landing.at[mine, :, lanes]
            return [post(piece, piece, target) for slot, to, target in around(axis)]

        def arrived(landing, copies, lanes):
            for copy in copies:
                copy.wait_recv()
            total = landing[0, :, lanes].astype(F32)
            for slot in range(1, 4):
                total = total + landing[slot, :, lanes].astype(F32)
            return total

        to_mate[l] = partial[l, :, other].astype(BF)
        copy = post(to_mate.at[l], from_mate.at[l], mate)
        yield
        copy.wait_recv()
        a_out[l] = (partial[l, :, half] + from_mate[l].astype(F32)).astype(BF)
        waits = []
        for lanes, axes in PARTS:
            waits.append(
                [
                    post(
                        a_out.at[l, pl.ds(pl.multiple_of(to * BAND, 16), BAND), lanes],
                        a_in.at[l, slot, :, lanes],
                        target,
                    )
                    for slot, to, target in around(axes[0])
                ]
            )
        yield
        for part, (lanes, axes) in enumerate(PARTS):
            for copy in waits[part]:
                copy.wait_recv()
            band = pl.ds(pl.multiple_of(coordinate(me, axes[0]) * BAND, 16), BAND)
            total = a_out[l, band, lanes].astype(F32)
            for slot in range(3):
                total = total + a_in[l, slot, :, lanes].astype(F32)
            waits[part] = exchange(total, b_in.at[l], axes[1], lanes)
        yield
        for part, (lanes, axes) in enumerate(PARTS):
            total = arrived(b_in.at[l], waits[part], lanes)
            waits[part] = exchange(total, c_in.at[l], axes[2], lanes)
        yield
        for part, (lanes, axes) in enumerate(PARTS):
            total = arrived(c_in.at[l], waits[part], lanes)
            band = pl.ds(pl.multiple_of(coordinate(me, axes[0]) * BAND, 16), BAND)
            here = pl.ds(pl.multiple_of(core * HALF + lanes.start, LANES), lanes.size)
            full[l, band, here] = total.astype(BF)
            piece = full.at[l, band, here]
            waits[part] = [post(piece, piece, target) for slot, to, target in around(axes[0])]
        yield
        final = []
        for part, (lanes, axes) in enumerate(PARTS):
            for copy in waits[part]:
                copy.wait_recv()
            here = pl.ds(pl.multiple_of(core * HALF + lanes.start, LANES), lanes.size)
            piece = full.at[l, :, here]
            final.append(post(piece, piece, mate))
        yield
        for copy in final:
            copy.wait_recv()
        store(full.at[l], dw_hbm.at[l])
        yield

    def block_sums(l, first, last):
        delta, stored = backward_buffers[l], forward_buffers[l]
        for a in range(3):
            shift = (a - 1) * 2**l * LANES
            low = max(first, -shift)
            block = dot_nt(delta[0:C, low:last], stored[:, low + shift : last + shift])
            if first == 0:
                partial[l, :, a * WIDE + 512 : (a + 1) * WIDE] = jnp.zeros((C, LANES), F32)
                partial[l, :, a * WIDE : a * WIDE + 3 * C] = block
            else:
                partial[l, :, a * WIDE : a * WIDE + 3 * C] += block

    def weight_sums(l):
        block_sums(l, 0 if l > 0 else 6 * LANES, CELLS)
        delta = backward_buffers[l]
        partial[l, :, 3 * WIDE : TOTAL] = jnp.broadcast_to(
            jnp.sum(delta[0:C, 0:CELLS].astype(F32), axis=1, keepdims=True), (C, LANES)
        )
        reduction = all_reduce(l)
        next(reduction)
        return reduction

    def cells_first(rows, cells):
        for r in range(ROWS):
            spread_rows[pl.ds(r, C, stride=ROWS), :] = rows[r].astype(F32)
        cells[...] = spread_rows[...].reshape(C, ROWS, LANES).astype(BF)

    def prepare_forward(l):
        for a in range(3):
            w_side[l, a, :, 0:C] = w_ref[l, 3 * a]
            w_side[l, a, :, C : 2 * C] = w_ref[l, 3 * a + 2]

    def prepare_backward(l):
        for a in range(3):
            v_mid[l, a] = w_ref[l, 3 * a + 1].T
            v_side[l, a, :, 0:C] = w_ref[l, 3 * a + 2].T
            v_side[l, a, :, C : 2 * C] = w_ref[l, 3 * a].T
        for place, tap in enumerate((7, 6, 8)):
            v_over[l, :, place * C : (place + 1) * C] = (
                w_ref[l, tap].T.astype(F32) * flip_sign
            ).astype(BF)

    forward_buffers = (s0, s1, s2)
    backward_buffers = (t0, t1, t2)

    small[2].wait()
    spread_rows[...] = x_ref[...].astype(F32).reshape(C * ROWS, LANES)
    for r in range(ROWS):
        row = spread_rows[pl.ds(r, C, stride=ROWS), :]
        s0[0:C, columns(r)] = (row * mask).astype(BF)
    rim = Rims(0, s0, 1, True)
    rim.turn(0, 3)
    own_tile[...] = slots(lambda r: s0[0:C, columns(r)], ROWS)
    packed[0, 0 : C // 2] = dense(own_tile[...], 2)
    packed[0, C // 2 : C // 2 + 16] = jnp.full((16, LANES), mask, F32).astype(BF)
    tile = slots(lambda k: turned[0, :, columns(k)], 3)
    tile = jnp.where(jnp.logical_and(lane >= 24, lane < 32), mask, tile)
    corner[0] = dense(tile, 4)
    loads[0].wait()
    prepare_forward(0)
    for a in range(3):
        for place, b in enumerate((1, 0, 2)):
            part = slice(place * C, (place + 1) * C)
            w_own[a, :, part] = w_ref[0, 3 * a + b]
            w_turn[a, :, part] = (w_ref[0, 8 - 3 * a - b].astype(F32) * cols_ref[3:4, 0:C]).astype(
                BF
            )
    small[3].wait()
    spread_rows[...] = ct_ref[...].astype(F32).reshape(C * ROWS, LANES)
    for r in range(ROWS):
        grad[:, columns(r)] = mask * spread_rows[pl.ds(r, C, stride=ROWS), :]
    loads[1].wait()
    loads[2].wait()
    pl.semaphore_wait(
        barrier, len(partners) + a_away.astype(jnp.int32) + b_away.astype(jnp.int32)
    )
    sides = [
        copy_to(
            packed.at[0, pl.ds(0, C // 2 + 16)],
            rims.at[0, slot, pl.ds(0, C // 2 + 16)],
            ex_send.at[0, slot],
            ex_recv.at[0, slot],
            target,
        )
        for slot, target in enumerate((east, west))
    ]
    over = copy_to(
        corner.at[0], corners.at[0, 2], ex_send.at[0, 5], ex_recv.at[0, 5], mirror
    )
    for copy in sides + [over]:
        copy.start()
        sends.append((None, copy))
    rim.send_corners()
    rim.send_fold(0, 3)

    def activate(l, buf, first, last):
        v = acc[:, first:last]
        s = jax.nn.sigmoid(v)
        after = mask * (buf[0:C, first:last].astype(F32) + v * s)
        s = s * (1.0 + v * (1.0 - s))
        slope[l, :, first:last] = s
        if l < 2:
            forward_buffers[l + 1][0:C, first:last] = after.astype(BF)
        else:
            for r in range(first // LANES, last // LANES):
                out_ref[r] = after[:, r * LANES - first : (r + 1) * LANES - first].astype(BF)
            t2[0:C, first:last] = (grad[:, first:last] * s).astype(BF)

    rest = CELLS - LANES
    acc[...] = dot(w_ref[0, 4], s0[0:C, 0:CELLS]) + bias_cols[0]
    acc[:, 0:rest] += dot(w_ref[0, 7], s0[0:C, LANES:CELLS])
    acc[:, LANES:CELLS] += dot(w_ref[0, 1], s0[0:C, 0:rest])
    prepare_forward(1)
    prepare_backward(2)
    for copy in sides:
        copy.wait_recv()
    low = lax.rem(lane, 8) < 4
    west_tile = loose(rims[0, 0, 0 : C // 2], 2)
    east_tile = loose(rims[0, 1, 0 : C // 2], 2)
    rim_tile = jnp.where(low, west_tile, east_tile)
    for r in range(ROWS):
        widen(s0, rim_tile, r, 1)
    acc[...] += dot(w_side[0, 1], s0[C : 3 * C, 0:CELLS])
    acc[:, 0:rest] += dot(w_side[0, 2], s0[C : 3 * C, LANES:CELLS])
    acc[:, LANES:CELLS] += dot(w_side[0, 0], s0[C : 3 * C, 0:rest])
    activate(0, s0, 0, rest)

    for slot, (away, copy) in enumerate(rim.turns):

        @pl.when(away)
        def _():
            copy.wait_recv()

        @pl.when(jnp.logical_not(away))
        def _():
            corners[0, slot] = corner[0]

    over.wait_recv()
    far_a, far_b, far = (pltpu.roll(loose(corners[0, slot], 4), 64, 1) for slot in range(3))
    inside = lane < 64
    beyond = lane < 88
    strips = [
        jnp.where(
            inside,
            jnp.where(low, west_tile, own_tile[...]),
            jnp.where(beyond, jnp.where(low, far_a, far), 0.0),
        ),
        jnp.where(
            inside,
            jnp.where(low, own_tile[...], east_tile),
            jnp.where(beyond, jnp.where(low, far, far_b), 0.0),
        ),
    ]
    rim_tile = jnp.where(low, strips[0], strips[1])
    for a in range(3):
        for place, b in enumerate((0, -1, 1)):
            shift = (-(8 * (a - 1) + b)) % LANES
            for side in range(2):
                moved = pltpu.roll(strips[side], shift, 1) if shift else strips[side]
                strip_cols[
                    (3 * a + place) * C : (3 * a + place + 1) * C, columns(side)
                ] = moved.astype(BF)
    own_sum = bias_cols[0]
    far_sum = bias_cols[0]
    for a in range(3):
        taps = strip_cols[3 * C * a : 3 * C * (a + 1), :]
        own_sum = own_sum + dot(w_own[a], taps)
        far_sum = far_sum + dot(w_turn[a], taps)
    after = []
    for side in range(2):
        v = jnp.where(inside, own_sum[:, columns(side)], far_sum[:, columns(side)])
        v = v * jax.nn.sigmoid(v)
        v = jnp.where(inside, v, v * flip_sign)
        near_mask = rims[0, side, C // 2 : C // 2 + 1, 0:1].astype(F32)
        far_mask = corners[0, side, 0:1, 24:25].astype(F32)
        side_mask = jnp.where(inside[0:1], near_mask, far_mask)
        after.append((side_mask * (strips[side] + v)).astype(BF).astype(F32))
    next_tile = jnp.where(low, after[0], after[1])
    for r in range(ROWS - 1):
        widen(s1, next_tile, r, 2)

    def second(first, last):
        step = 2 * LANES
        acc[:, first:last] = (
            dot(w_ref[1, 4], s1[0:C, first:last])
            + dot(w_side[1, 1], s1[C : 3 * C, first:last])
            + bias_cols[1]
        )
        acc[:, first:last] += dot(w_ref[1, 7], s1[0:C, first + step : last + step]) + dot(
            w_side[1, 2], s1[C : 3 * C, first + step : last + step]
        )
        low_row = max(first, step)
        acc[:, low_row:last] += dot(w_ref[1, 1], s1[0:C, low_row - step : last - step]) + dot(
            w_side[1, 0], s1[C : 3 * C, low_row - step : last - step]
        )
        activate(1, s1, first, last)

    second(0, 4 * LANES)
    later = Rims(2, s2, 4, True)
    later.pack_sides(0, 4)
    prepare_forward(2)

    rim.folds[0][0].wait_recv()
    for k in range(3):
        widen(s0, rim_tile, ROWS + k, 1)
    acc[:, rest:CELLS] += dot(w_ref[0, 7], s0[0:C, CELLS : CELLS + LANES]) + dot(
        w_side[0, 2], s0[C : 3 * C, CELLS : CELLS + LANES]
    )
    activate(0, s0, rest, CELLS)
    v = bias_cols[0]
    for a in range(3):
        v = v + dot(w_turn[a], s0[:, columns(7 + a, 2)])
    v = v * jax.nn.sigmoid(v) * flip_sign
    far_mask = corners[0, 2, 0:1, 24:25].astype(F32)
    s1[0:C, columns(ROWS, 2)] = (far_mask * (s0[0:C, columns(ROWS, 2)].astype(F32) + v)).astype(BF)
    for r in range(ROWS - 1, ROWS + 2):
        widen(s1, next_tile, r, 2)
    second(4 * LANES, CELLS)
    rim = later
    rim.turn(0, 4)
    rim.pack_corners()
    rim.send_corners()
    rim.send_fold(0, 2)
    rim.send_fold(2, 4)
    rim.pack_sides(4, ROWS)
    rim.send_sides()

    d = 4
    rest = CELLS - d * LANES
    acc[...] = dot(w_ref[2, 4], s2[0:C, 0:CELLS]) + bias_cols[2]
    acc[:, 0:rest] += dot(w_ref[2, 7], s2[0:C, d * LANES : CELLS])
    acc[:, d * LANES : CELLS] += dot(w_ref[2, 1], s2[0:C, 0:rest])
    rim.roll_sides()
    prepare_backward(1)
    prepare_backward(0)
    rim.receive_sides()
    acc[...] += dot(w_side[2, 1], s2[C : 3 * C, 0:CELLS])
    acc[:, 0:rest] += dot(w_side[2, 2], s2[C : 3 * C, d * LANES : CELLS])
    acc[:, d * LANES : CELLS] += dot(w_side[2, 0], s2[C : 3 * C, 0:rest])
    activate(2, s2, 0, rest)
    later = Rims(3, t2, d, False)
    later.pack_sides(0, ROWS - d)
    rim.receive_corners()
    for number, (fold, first, last) in enumerate(rim.folds):
        rim.receive_fold(number)
        top = slice(rest + first * LANES, rest + last * LANES)
        over = slice(CELLS + first * LANES, CELLS + last * LANES)
        acc[:, top] += dot(w_ref[2, 7], s2[0:C, over]) + dot(w_side[2, 2], s2[C : 3 * C, over])
        activate(2, s2, top.start, top.stop)
        later.turn(d - last, d - first)
        if number == 0:
            later.send_fold(d - last, d - first)
    rim = later
    rim.pack_corners()
    rim.send_corners()
    rim.send_fold(0, d // 2)
    rim.pack_sides(ROWS - d, ROWS)
    rim.send_sides()

    reductions = {}
    for l in (2, 1, 0):
        d = 2**l
        rest = CELLS - d * LANES
        buf = backward_buffers[l]
        if l == 0:
            reductions[0] = weight_sums(0)
            rim.pack_sides(0, ROWS)
            rim.send_sides()
            for older in (0, 1, 2):
                next(reductions[older])
        else:
            reductions[l] = weight_sums(l)
            for older in range(l + 1, 3):
                next(reductions[older])
        acc[...] = dot(v_mid[l, 1], buf[0:C, 0:CELLS])
        acc[:, d * LANES : CELLS] += dot(v_mid[l, 2], buf[0:C, 0:rest])
        acc[:, 0:rest] += dot(v_mid[l, 0], buf[0:C, d * LANES : CELLS])
        rim.roll_sides()
        acc[...] += dot(v_side[l, 1], buf[C : 3 * C, 0:CELLS])
        acc[:, d * LANES : CELLS] += dot(v_side[l, 2], buf[C : 3 * C, 0:rest])
        acc[:, 0:rest] += dot(v_side[l, 0], buf[C : 3 * C, d * LANES : CELLS])
        if l == 2:
            cells_first(out_ref, x_ref)
            store(x_ref, out_hbm)
        rim.receive_edges(l)
        if l == 0:
            for older in (0, 1, 2):
                next(reductions[older])

        def descend(first, last):
            g = mask * (grad[:, first:last] + acc[:, first:last])
            if l > 0:
                grad[:, first:last] = g
                backward_buffers[l - 1][0:C, first:last] = (
                    g * slope[l - 1, :, first:last]
                ).astype(BF)
            else:
                for r in range(first // LANES, last // LANES):
                    fg_ref[r] = g[:, r * LANES - first : (r + 1) * LANES - first].astype(BF)

        descend(0, rest)
        if l > 0:
            next(reductions[l])
        if l == 1:
            block_sums(0, 0, 6 * LANES)
        rim.receive_corners()
        middle = d // 2
        for number, (fold, first, last) in enumerate(rim.folds):
            rim.receive_fold(number)
            top = slice(rest + first * LANES, rest + last * LANES)
            acc[:, top] += dot(
                v_over[l], buf[:, CELLS + first * LANES : CELLS + last * LANES]
            )
            descend(top.start, top.stop)
            if l > 0 and number == 0:
                later = Rims(6 - l, backward_buffers[l - 1], middle, False)
                later.turn(0, middle)
                later.pack_corners()
                later.send_corners()
                if middle > 1:
                    later.send_fold(middle // 2, middle)
                    later.send_fold(0, middle // 2)
                else:
                    later.send_fold(0, 1)
        if l > 0:
            rim = later
        if l > 1:
            rim.pack_sides(0, ROWS)
            rim.send_sides()

    cells_first(fg_ref, ct_ref)
    store(ct_ref, fg_hbm)
    done = object()
    running = [reductions[l] for l in range(3)]
    while running:
        running = [reduction for reduction in running if next(reduction, done) is not done]
    for condition, copy in sends:
        if condition is None:
            copy.wait_send()
        else:

            @pl.when(condition)
            def _():
                copy.wait_send()

    for copy in stores:
        copy.wait()


def finish(
    cells_a,
    cells_b,
    summed,
    out_a,
    out_b,
    kernel_grad,
    bias_grad,
    sums,
    cells,
    kernels,
    bias_rows,
    in_sem,
    out_sem,
):
    loads = [pltpu.make_async_copy(summed.at[l], sums.at[l], in_sem.at[l]) for l in range(3)]
    for number, src in enumerate((cells_a, cells_b)):
        loads.append(pltpu.make_async_copy(src, cells.at[number], in_sem.at[3 + number]))
    for load in loads:
        load.start()
    stores = []

    def store(src, dst):
        copy = pltpu.make_async_copy(src, dst, out_sem.at[len(stores)])
        copy.start()
        stores.append(copy)

    for l in range(3):
        loads[l].wait()
        if l > 0:
            loads[2 + l].wait()
            store(cells.at[l - 1], (out_a, out_b)[l - 1])
        for a in range(3):
            for b in range(3):
                first = a * WIDE + (1, 0, 2)[b] * C
                kernels[l, 3 * a + b] = sums[l, :, first : first + C].astype(F32)
            taps = pl.ds(3 * a, 3)
            store(kernels.at[l, taps], kernel_grad.at[l, taps])
        bias_rows[l : l + 1, :] = sums[l, :, 3 * WIDE : TOTAL].astype(F32).T[0:1]
    store(bias_rows, bias_grad)
    for copy in stores:
        copy.wait()


def shards(fields, cotangent, weights, biases, ocean_tiles, velocity_mask):
    n = lax.axis_size("tiles")
    hbm = pl.BlockSpec(memory_space=pltpu.HBM)
    out, field_grad, summed = pl.pallas_call(
        functools.partial(kernel, n),
        out_shape=(
            jax.ShapeDtypeStruct((C, ROWS, LANES), BF),
            jax.ShapeDtypeStruct((C, ROWS, LANES), BF),
            jax.ShapeDtypeStruct((3, C, TOTAL), BF),
        ),
        in_specs=[
            hbm,
            hbm,
            hbm,
            hbm,
            pl.BlockSpec(memory_space=pltpu.SMEM),
            hbm,
        ],
        out_specs=(hbm,) * 3,
        scratch_shapes=[
            pltpu.VMEM((3 * C, CELLS + 3 * LANES), BF),
            pltpu.VMEM((3 * C, CELLS + 2 * LANES), BF),
            pltpu.VMEM((3 * C, CELLS + 4 * LANES), BF),
            pltpu.VMEM((3 * C, CELLS + LANES), BF),
            pltpu.VMEM((3 * C, CELLS + 2 * LANES), BF),
            pltpu.VMEM((3 * C, CELLS + 4 * LANES), BF),
            pltpu.VMEM((C, ROWS, LANES), BF),
            pltpu.VMEM((C, ROWS, LANES), BF),
            pltpu.VMEM((3, C), F32),
            pltpu.VMEM((C,), jnp.int32),
            pltpu.VMEM((3, 9, C, C), BF),
            pltpu.VMEM((ROWS, C, LANES), BF),
            pltpu.VMEM((ROWS, C, LANES), BF),
            pltpu.VMEM((C * ROWS, LANES), F32),
            pltpu.VMEM((LANES, 2 * LANES), F32),
            pltpu.VMEM((3, C, CELLS), F32),
            pltpu.VMEM((C, CELLS), F32),
            pltpu.VMEM((C, CELLS), F32),
            pltpu.VMEM((3, 3, C, 2 * C), BF),
            pltpu.VMEM((3, 3, C, C), BF),
            pltpu.VMEM((3, 3, C, 2 * C), BF),
            pltpu.VMEM((3, C, 3 * C), BF),
            pltpu.VMEM((6, C, LANES), BF),
            pltpu.VMEM((C, LANES), F32),
            pltpu.VMEM((C, LANES), F32),
            pltpu.VMEM((9 * C, 2 * LANES), BF),
            pltpu.VMEM((3, C, 3 * C), BF),
            pltpu.VMEM((3, C, 3 * C), BF),
            pltpu.VMEM((6, BAND, LANES), BF),
            pltpu.VMEM((6, C, 4 * LANES), BF),
            pltpu.VMEM((6, 2, C, LANES), BF),
            pltpu.VMEM((6, 3, BAND, LANES), BF),
            pltpu.VMEM((3, C, TOTAL), F32),
            pltpu.VMEM((3, C, HALF), BF),
            pltpu.VMEM((3, C, HALF), BF),
            pltpu.VMEM((3, C, HALF), BF),
            pltpu.VMEM((3, 3, BAND, HALF), BF),
            pltpu.VMEM((3, 4, BAND, HALF), BF),
            pltpu.VMEM((3, 4, BAND, HALF), BF),
            pltpu.VMEM((3, C, TOTAL), BF),
            pltpu.SemaphoreType.DMA((7,)),
            pltpu.SemaphoreType.DMA((5,)),
            pltpu.SemaphoreType.DMA((6, 6)),
            pltpu.SemaphoreType.DMA((6, 6)),
            pltpu.SemaphoreType.DMA((3, 40)),
            pltpu.SemaphoreType.DMA((3, 40)),
        ],
        compiler_params=pltpu.CompilerParams(
            collective_id=0, has_side_effects=True, vmem_limit_bytes=62 * 1024 * 1024
        ),
        cost_estimate=pl.CostEstimate(
            flops=18 * 9 * C * C * CELLS, bytes_accessed=8 * 1024 * 1024, transcendentals=9 * C * CELLS
        ),
    )(fields, cotangent, weights, biases, ocean_tiles, velocity_mask)
    return pl.pallas_call(
        finish,
        out_shape=(
            jax.ShapeDtypeStruct((C, ROWS, LANES), BF),
            jax.ShapeDtypeStruct((C, ROWS, LANES), BF),
            jax.ShapeDtypeStruct((3, 9, C, C), F32),
            jax.ShapeDtypeStruct((3, C), F32),
        ),
        in_specs=[hbm] * 3,
        out_specs=(hbm,) * 4,
        scratch_shapes=[
            pltpu.VMEM((3, C, TOTAL), BF),
            pltpu.VMEM((2, C, ROWS, LANES), BF),
            pltpu.VMEM((3, 9, C, C), F32),
            pltpu.VMEM((3, C), F32),
            pltpu.SemaphoreType.DMA((5,)),
            pltpu.SemaphoreType.DMA((12,)),
        ],
        compiler_params=pltpu.CompilerParams(vmem_limit_bytes=62 * 1024 * 1024),
    )(out, field_grad, summed)


def solution(mesh):
    placed = (P(None, None, "tiles"), P(None, None, "tiles"), P(), P(), P(None, "tiles"), P())
    return jax.shard_map(
        shards,
        mesh=mesh,
        in_specs=placed,
        out_specs=(P(None, None, "tiles"), P(None, None, "tiles"), P(), P()),
        check_vma=False,
    )
```

```python
import functools

import jax
import jax.numpy as jnp
from jax import lax
from jax.experimental import pallas as pl
from jax.experimental.pallas import tpu as pltpu
from jax.sharding import PartitionSpec as P

C = 192
ROWS = 8
LANES = 128
CELLS = ROWS * LANES
WIDE = 640
TOTAL = 2048
HALF = TOTAL // 2
BAND = C // 4
BF = jnp.bfloat16
F32 = jnp.float32
MESH = pl.DeviceIdType.MESH

CORE = (1, 2)
Y = (2, 4)
X = (8, 4)
Z = (32, 4)
PARTS = (
    (pl.ds(0, 384), (Y, X, Z)),
    (pl.ds(384, 384), (Z, Y, X)),
    (pl.ds(768, 256), (X, Z, Y)),
)


def coordinate(me, axis):
    return lax.rem(lax.div(me, axis[0]), axis[1])


def with_coordinate(me, axis, value):
    return me + (value - coordinate(me, axis)) * axis[0]


def copy_to(src, dst, send_sem, recv_sem, device):
    return pltpu.make_async_remote_copy(
        src_ref=src,
        dst_ref=dst,
        send_sem=send_sem,
        recv_sem=recv_sem,
        device_id=(device,),
        device_id_type=MESH,
    )


def start_if(condition, copy):
    @pl.when(condition)
    def _():
        copy.start()


def dot(a, b):
    return jnp.dot(a, b, preferred_element_type=F32)


def dot_nt(a, b):
    return lax.dot_general(a, b, (((1,), (1,)), ((), ())), preferred_element_type=F32)


def kernel(
    n,
    x_hbm,
    ct_hbm,
    w_hbm,
    bias_hbm,
    ocean_ref,
    velocity_hbm,
    out_hbm,
    fg_hbm,
    dw_hbm,
    s0,
    s1,
    s2,
    t0,
    t1,
    t2,
    x_ref,
    ct_ref,
    bias_ref,
    velocity_ref,
    w_ref,
    out_ref,
    fg_ref,
    spread_rows,
    cols_ref,
    slope,
    acc,
    grad,
    w_side,
    v_mid,
    v_side,
    v_over,
    packed,
    side_tile,
    own_tile,
    strip_cols,
    w_own,
    w_turn,
    corner,
    turned,
    rims,
    corners,
    partial,
    to_mate,
    from_mate,
    a_out,
    a_in,
    b_in,
    c_in,
    full,
    w_sem,
    out_sem,
    ex_send,
    ex_recv,
    ar_send,
    ar_recv,
):
    me = lax.axis_index("tiles")
    east = lax.rem(me + 1, n)
    west = lax.rem(me + n - 1, n)
    mirror = n - 1 - me
    fold_a = lax.rem(n - me, n)
    fold_b = lax.rem(2 * n - 2 - me, n)
    mate = with_coordinate(me, CORE, 1 - coordinate(me, CORE))
    core = coordinate(me, CORE)
    a_away = fold_a != me
    b_away = fold_b != me

    barrier = pltpu.get_barrier_semaphore()
    partners = [east, west, mirror, mate]
    for axis in (Y, X, Z):
        for step in (1, 2, 3):
            partners.append(
                with_coordinate(me, axis, lax.rem(coordinate(me, axis) + step, axis[1]))
            )
    for partner in partners:
        pl.semaphore_signal(barrier, inc=1, device_id=(partner,), device_id_type=MESH)

    @pl.when(a_away)
    def _():
        pl.semaphore_signal(barrier, inc=1, device_id=(fold_a,), device_id_type=MESH)

    @pl.when(b_away)
    def _():
        pl.semaphore_signal(barrier, inc=1, device_id=(fold_b,), device_id_type=MESH)

    small = [
        pltpu.make_async_copy(src, dst, w_sem.at[3 + number])
        for number, (src, dst) in enumerate(
            (
                (bias_hbm, bias_ref),
                (velocity_hbm, velocity_ref),
                (x_hbm, x_ref),
                (ct_hbm, ct_ref),
            )
        )
    ]
    loads = [
        pltpu.make_async_copy(w_hbm.at[l], w_ref.at[l], w_sem.at[l]) for l in range(3)
    ]
    for load in small + loads:
        load.start()

    lane = lax.broadcasted_iota(jnp.int32, (C, LANES), 1)
    flip_matrix = (
        lax.broadcasted_iota(jnp.int32, (LANES, LANES), 0)
        + lax.broadcasted_iota(jnp.int32, (LANES, LANES), 1)
        == LANES - 1
    ).astype(F32).astype(BF)
    cols_ref[...] = jnp.zeros((LANES, 2 * LANES), F32)
    small[0].wait()
    small[1].wait()
    cols_ref[0:3, 0:C] = bias_ref[...]
    cols_ref[3:4, 0:C] = (1 - 2 * velocity_ref[...]).astype(F32).reshape(1, C)
    turned_cols = cols_ref[...].T[0:C]
    bias_cols = [turned_cols[:, l : l + 1] for l in range(3)]
    flip_sign = turned_cols[:, 3:4]
    mask = ocean_ref[0, 0].astype(F32)
    sends = []

    stores = []

    def store(src, dst):
        copy = pltpu.make_async_copy(src, dst, out_sem.at[len(stores)])
        copy.start()
        stores.append(copy)

    def columns(row, count=1):
        return slice(row * LANES, (row + count) * LANES)

    def dense(tile, groups):
        size = C // groups
        total = tile[0:size]
        for q in range(1, groups):
            piece = tile[q * size : (q + 1) * size]
            total = total + pltpu.roll(piece, q * LANES // groups, 1)
        return total.astype(BF)

    def loose(total, groups):
        total = total.astype(F32)
        return jnp.concatenate(
            [total]
            + [pltpu.roll(total, LANES - q * LANES // groups, 1) for q in range(1, groups)],
            axis=0,
        )

    def slots(rows, count):
        tile = jnp.zeros((C, LANES), F32)
        for r in range(count):
            here = jnp.logical_and(lane >= 8 * r, lane < 8 * r + 8)
            tile = jnp.where(here, pltpu.roll(rows(r).astype(F32), (8 * r + 4) % LANES, 1), tile)
        return tile

    def widen(buf, rim, row, d):
        center = buf[0:C, columns(row)].astype(F32)
        left = pltpu.roll(rim, (-(8 * row + 4 - d)) % LANES, 1)
        right = pltpu.roll(rim, (-(8 * row + 4 + d)) % LANES, 1)
        buf[C : 2 * C, columns(row)] = jnp.where(
            lane < d, left, pltpu.roll(center, d, 1)
        ).astype(BF)
        buf[2 * C : 3 * C, columns(row)] = jnp.where(
            lane >= LANES - d, right, pltpu.roll(center, LANES - d, 1)
        ).astype(BF)

    class Rims:
        def __init__(self, e, buf, d, signed):
            self.e, self.buf, self.d, self.signed = e, buf, d, signed
            self.folds = []
            self.groups = 4 if d <= 2 else 2

        def turn(self, first, last):
            for k in range(first, last):
                row = dot(self.buf[0:C, columns(ROWS - 1 - k)], flip_matrix)
                if self.signed:
                    row = row * flip_sign
                turned[self.e, :, columns(k)] = row.astype(BF)

        def send_fold(self, first, last):
            slot = 4 + len(self.folds)
            fold = copy_to(
                turned.at[self.e, :, pl.ds(first * LANES, (last - first) * LANES)],
                self.buf.at[pl.ds(0, C), pl.ds(CELLS + first * LANES, (last - first) * LANES)],
                ex_send.at[self.e, slot],
                ex_recv.at[self.e, slot],
                mirror,
            )
            fold.start()
            self.folds.append((fold, first, last))
            sends.append((None, fold))

        def pack(self, tile, rows, first, last):
            d = self.d
            for r in range(first, last):
                at = 2 * d * r
                here = jnp.logical_and(lane >= at, lane < at + 2 * d)
                tile = jnp.where(here, pltpu.roll(rows(r).astype(F32), (at + d) % LANES, 1), tile)
            return tile

        def pack_sides(self, first, last):
            tile = jnp.zeros((C, LANES), F32) if first == 0 else side_tile[...]
            side_tile[...] = self.pack(
                tile, lambda r: self.buf[0:C, columns(r)], first, last
            )
            if last == ROWS:
                packed[self.e, 0 : C // self.groups] = dense(side_tile[...], self.groups)

        def pack_corners(self):
            tile = self.pack(
                jnp.zeros((C, LANES), F32), lambda k: turned[self.e, :, columns(k)], 0, self.d
            )
            corner[self.e] = dense(tile, 4)

        def send_sides(self):
            self.sides = []
            for slot, target in enumerate((east, west)):
                copy = copy_to(
                    packed.at[self.e, pl.ds(0, C // self.groups)],
                    rims.at[self.e, slot, pl.ds(0, C // self.groups)],
                    ex_send.at[self.e, slot],
                    ex_recv.at[self.e, slot],
                    target,
                )
                copy.start()
                self.sides.append(copy)
                sends.append((None, copy))

        def send_corners(self):
            self.turns = []
            for slot, target, away in ((0, fold_a, a_away), (1, fold_b, b_away)):
                copy = copy_to(
                    corner.at[self.e],
                    corners.at[self.e, slot],
                    ex_send.at[self.e, 2 + slot],
                    ex_recv.at[self.e, 2 + slot],
                    target,
                )
                start_if(away, copy)
                self.turns.append((away, copy))
                sends.append((away, copy))

        def unpack(self, rim, row, slot):
            buf, d = self.buf, self.d
            center = buf[0:C, columns(row)].astype(F32)
            edge = pltpu.roll(rim, (-(2 * d * slot + d)) % LANES, 1)
            left = pltpu.roll(jnp.where(lane >= LANES - d, edge, center), d, 1)
            right = pltpu.roll(jnp.where(lane < d, edge, center), LANES - d, 1)
            buf[C : 2 * C, columns(row)] = left.astype(BF)
            buf[2 * C : 3 * C, columns(row)] = right.astype(BF)

        def roll_sides(self):
            buf, d = self.buf, self.d
            for r in range(ROWS):
                center = buf[0:C, columns(r)].astype(F32)
                left = jnp.where(lane < d, 0.0, pltpu.roll(center, d, 1))
                right = jnp.where(lane >= LANES - d, 0.0, pltpu.roll(center, LANES - d, 1))
                buf[C : 2 * C, columns(r)] = left.astype(BF)
                buf[2 * C : 3 * C, columns(r)] = right.astype(BF)

        def receive_sides(self):
            buf, d = self.buf, self.d
            for copy in self.sides:
                copy.wait_recv()
            size = C // self.groups
            low = lax.rem(lane, 2 * d) < d
            rim = jnp.where(
                low,
                loose(rims[self.e, 0, 0:size], self.groups),
                loose(rims[self.e, 1, 0:size], self.groups),
            )
            for r in range(ROWS + 1):
                edge = pltpu.roll(rim, (-2 * d * r) % LANES, 1) if r > 0 else rim
                if r < ROWS:
                    old = buf[C : 2 * C, columns(r)].astype(F32)
                    buf[C : 2 * C, columns(r)] = jnp.where(lane < d, edge, old).astype(BF)
                if r > 0:
                    old = buf[2 * C : 3 * C, columns(r - 1)].astype(F32)
                    buf[2 * C : 3 * C, columns(r - 1)] = jnp.where(
                        lane >= LANES - d, edge, old
                    ).astype(BF)

        def receive_edges(self, l):
            d = self.d
            for copy in self.sides:
                copy.wait_recv()
            size = C // self.groups
            low = lax.rem(lane, 2 * d) < d
            rim = jnp.where(
                low,
                loose(rims[self.e, 0, 0:size], self.groups),
                loose(rims[self.e, 1, 0:size], self.groups),
            )
            rim = jnp.where(lane < 2 * d * ROWS, rim, 0.0)
            left = right = 0.0
            for a, shift in ((1, 0), (2, 2 * d * d), (0, LANES - 2 * d * d)):
                moved = (pltpu.roll(rim, shift, 1) if shift else rim).astype(BF)
                left = left + dot(v_side[l, a, :, 0:C], moved)
                right = right + dot(v_side[l, a, :, C : 2 * C], moved)
            both = jnp.where(low, left, right)
            edge = both
            for r in range(ROWS):
                after = pltpu.roll(both, (-2 * d * (r + 1)) % LANES, 1)
                acc[:, columns(r)] += jnp.where(
                    lane < d, edge, jnp.where(lane >= LANES - d, after, 0.0)
                )
                edge = after

        def receive_corners(self):
            for slot, (away, copy) in enumerate(self.turns):

                @pl.when(away)
                def _():
                    copy.wait_recv()

                @pl.when(jnp.logical_not(away))
                def _():
                    corners[self.e, slot] = corner[self.e]

            low = lax.rem(lane, 2 * self.d) < self.d
            tiles = [loose(corners[self.e, slot], 4) for slot in range(2)]
            self.rim = jnp.where(low, tiles[0], tiles[1])

        def receive_fold(self, number):
            fold, first, last = self.folds[number]
            fold.wait_recv()
            for k in range(first, last):
                self.unpack(self.rim, ROWS + k, k)

    def all_reduce(l):
        half = pl.ds(pl.multiple_of(core * HALF, LANES), HALF)
        other = pl.ds(pl.multiple_of((1 - core) * HALF, LANES), HALF)
        count = [0]

        def post(src, dst, target):
            number = count[0]
            count[0] += 1
            copy = copy_to(src, dst, ar_send.at[l, number], ar_recv.at[l, number], target)
            copy.start()
            sends.append((None, copy))
            return copy

        def around(axis):
            for step in (2, 1, 3):
                to = lax.rem(coordinate(me, axis) + step, 4)
                yield step - 1, to, with_coordinate(me, axis, to)

        def exchange(total, landing, axis, lanes):
            mine = coordinate(me, axis)
            landing[mine, :, lanes] = total.astype(BF)
            piece = landing.at[mine, :, lanes]
            return [post(piece, piece, target) for slot, to, target in around(axis)]

        def arrived(landing, copies, lanes):
            for copy in copies:
                copy.wait_recv()
            total = landing[0, :, lanes].astype(F32)
            for slot in range(1, 4):
                total = total + landing[slot, :, lanes].astype(F32)
            return total

        to_mate[l] = partial[l, :, other].astype(BF)
        copy = post(to_mate.at[l], from_mate.at[l], mate)
        yield
        copy.wait_recv()
        a_out[l] = (partial[l, :, half] + from_mate[l].astype(F32)).astype(BF)
        waits = []
        for lanes, axes in PARTS:
            waits.append(
                [
                    post(
                        a_out.at[l, pl.ds(pl.multiple_of(to * BAND, 16), BAND), lanes],
                        a_in.at[l, slot, :, lanes],
                        target,
                    )
                    for slot, to, target in around(axes[0])
                ]
            )
        yield
        for part, (lanes, axes) in enumerate(PARTS):
            for copy in waits[part]:
                copy.wait_recv()
            band = pl.ds(pl.multiple_of(coordinate(me, axes[0]) * BAND, 16), BAND)
            total = a_out[l, band, lanes].astype(F32)
            for slot in range(3):
                total = total + a_in[l, slot, :, lanes].astype(F32)
            waits[part] = exchange(total, b_in.at[l], axes[1], lanes)
        yield
        for part, (lanes, axes) in enumerate(PARTS):
            total = arrived(b_in.at[l], waits[part], lanes)
            waits[part] = exchange(total, c_in.at[l], axes[2], lanes)
        yield
        for part, (lanes, axes) in enumerate(PARTS):
            total = arrived(c_in.at[l], waits[part], lanes)
            band = pl.ds(pl.multiple_of(coordinate(me, axes[0]) * BAND, 16), BAND)
            here = pl.ds(pl.multiple_of(core * HALF + lanes.start, LANES), lanes.size)
            full[l, band, here] = total.astype(BF)
            piece = full.at[l, band, here]
            waits[part] = [post(piece, piece, target) for slot, to, target in around(axes[0])]
        yield
        final = []
        for part, (lanes, axes) in enumerate(PARTS):
            for copy in waits[part]:
                copy.wait_recv()
            here = pl.ds(pl.multiple_of(core * HALF + lanes.start, LANES), lanes.size)
            piece = full.at[l, :, here]
            final.append(post(piece, piece, mate))
        yield
        for copy in final:
            copy.wait_recv()
        store(full.at[l], dw_hbm.at[l])
        yield

    def block_sums(l, first, last):
        delta, stored = backward_buffers[l], forward_buffers[l]
        for a in range(3):
            shift = (a - 1) * 2**l * LANES
            low = max(first, -shift)
            block = dot_nt(delta[0:C, low:last], stored[:, low + shift : last + shift])
            if first == 0:
                partial[l, :, a * WIDE + 512 : (a + 1) * WIDE] = jnp.zeros((C, LANES), F32)
                partial[l, :, a * WIDE : a * WIDE + 3 * C] = block
            else:
                partial[l, :, a * WIDE : a * WIDE + 3 * C] += block

    def weight_sums(l):
        block_sums(l, 0 if l > 0 else 6 * LANES, CELLS)
        delta = backward_buffers[l]
        partial[l, :, 3 * WIDE : TOTAL] = jnp.broadcast_to(
            jnp.sum(delta[0:C, 0:CELLS].astype(F32), axis=1, keepdims=True), (C, LANES)
        )
        reduction = all_reduce(l)
        next(reduction)
        return reduction

    def cells_first(rows, cells):
        for r in range(ROWS):
            spread_rows[pl.ds(r, C, stride=ROWS), :] = rows[r].astype(F32)
        cells[...] = spread_rows[...].reshape(C, ROWS, LANES).astype(BF)

    def prepare_forward(l):
        for a in range(3):
            w_side[l, a, :, 0:C] = w_ref[l, 3 * a]
            w_side[l, a, :, C : 2 * C] = w_ref[l, 3 * a + 2]

    def prepare_backward(l):
        for a in range(3):
            v_mid[l, a] = w_ref[l, 3 * a + 1].T
            v_side[l, a, :, 0:C] = w_ref[l, 3 * a + 2].T
            v_side[l, a, :, C : 2 * C] = w_ref[l, 3 * a].T
        for place, tap in enumerate((7, 6, 8)):
            v_over[l, :, place * C : (place + 1) * C] = (
                w_ref[l, tap].T.astype(F32) * flip_sign
            ).astype(BF)

    forward_buffers = (s0, s1, s2)
    backward_buffers = (t0, t1, t2)

    small[2].wait()
    spread_rows[...] = x_ref[...].astype(F32).reshape(C * ROWS, LANES)
    for r in range(ROWS):
        row = spread_rows[pl.ds(r, C, stride=ROWS), :]
        s0[0:C, columns(r)] = (row * mask).astype(BF)
    rim = Rims(0, s0, 1, True)
    rim.turn(0, 3)
    own_tile[...] = slots(lambda r: s0[0:C, columns(r)], ROWS)
    packed[0, 0 : C // 2] = dense(own_tile[...], 2)
    packed[0, C // 2 : C // 2 + 16] = jnp.full((16, LANES), mask, F32).astype(BF)
    tile = slots(lambda k: turned[0, :, columns(k)], 3)
    tile = jnp.where(jnp.logical_and(lane >= 24, lane < 32), mask, tile)
    corner[0] = dense(tile, 4)
    pl.semaphore_wait(
        barrier, len(partners) + a_away.astype(jnp.int32) + b_away.astype(jnp.int32)
    )
    sides = [
        copy_to(
            packed.at[0, pl.ds(0, C // 2 + 16)],
            rims.at[0, slot, pl.ds(0, C // 2 + 16)],
            ex_send.at[0, slot],
            ex_recv.at[0, slot],
            target,
        )
        for slot, target in enumerate((east, west))
    ]
    over = copy_to(
        corner.at[0], corners.at[0, 2], ex_send.at[0, 5], ex_recv.at[0, 5], mirror
    )
    for copy in sides + [over]:
        copy.start()
        sends.append((None, copy))
    rim.send_corners()
    rim.send_fold(0, 3)

    def activate(l, buf, first, last):
        v = acc[:, first:last]
        s = jax.nn.sigmoid(v)
        after = mask * (buf[0:C, first:last].astype(F32) + v * s)
        s = s * (1.0 + v * (1.0 - s))
        slope[l, :, first:last] = s
        if l < 2:
            forward_buffers[l + 1][0:C, first:last] = after.astype(BF)
        else:
            for r in range(first // LANES, last // LANES):
                out_ref[r] = after[:, r * LANES - first : (r + 1) * LANES - first].astype(BF)
            t2[0:C, first:last] = (grad[:, first:last] * s).astype(BF)

    loads[0].wait()
    prepare_forward(0)
    for a in range(3):
        for place, b in enumerate((1, 0, 2)):
            part = slice(place * C, (place + 1) * C)
            w_own[a, :, part] = w_ref[0, 3 * a + b]
            w_turn[a, :, part] = (w_ref[0, 8 - 3 * a - b].astype(F32) * cols_ref[3:4, 0:C]).astype(
                BF
            )
    small[3].wait()
    spread_rows[...] = ct_ref[...].astype(F32).reshape(C * ROWS, LANES)
    for r in range(ROWS):
        grad[:, columns(r)] = mask * spread_rows[pl.ds(r, C, stride=ROWS), :]
    loads[1].wait()
    loads[2].wait()
    rest = CELLS - LANES
    acc[...] = dot(w_ref[0, 4], s0[0:C, 0:CELLS]) + bias_cols[0]
    acc[:, 0:rest] += dot(w_ref[0, 7], s0[0:C, LANES:CELLS])
    acc[:, LANES:CELLS] += dot(w_ref[0, 1], s0[0:C, 0:rest])
    prepare_forward(1)
    prepare_backward(2)
    for copy in sides:
        copy.wait_recv()
    low = lax.rem(lane, 8) < 4
    west_tile = loose(rims[0, 0, 0 : C // 2], 2)
    east_tile = loose(rims[0, 1, 0 : C // 2], 2)
    rim_tile = jnp.where(low, west_tile, east_tile)
    for r in range(ROWS):
        widen(s0, rim_tile, r, 1)
    acc[...] += dot(w_side[0, 1], s0[C : 3 * C, 0:CELLS])
    acc[:, 0:rest] += dot(w_side[0, 2], s0[C : 3 * C, LANES:CELLS])
    acc[:, LANES:CELLS] += dot(w_side[0, 0], s0[C : 3 * C, 0:rest])
    activate(0, s0, 0, rest)

    for slot, (away, copy) in enumerate(rim.turns):

        @pl.when(away)
        def _():
            copy.wait_recv()

        @pl.when(jnp.logical_not(away))
        def _():
            corners[0, slot] = corner[0]

    over.wait_recv()
    far_a, far_b, far = (pltpu.roll(loose(corners[0, slot], 4), 64, 1) for slot in range(3))
    inside = lane < 64
    beyond = lane < 88
    strips = [
        jnp.where(
            inside,
            jnp.where(low, west_tile, own_tile[...]),
            jnp.where(beyond, jnp.where(low, far_a, far), 0.0),
        ),
        jnp.where(
            inside,
            jnp.where(low, own_tile[...], east_tile),
            jnp.where(beyond, jnp.where(low, far, far_b), 0.0),
        ),
    ]
    rim_tile = jnp.where(low, strips[0], strips[1])
    for a in range(3):
        for place, b in enumerate((0, -1, 1)):
            shift = (-(8 * (a - 1) + b)) % LANES
            for side in range(2):
                moved = pltpu.roll(strips[side], shift, 1) if shift else strips[side]
                strip_cols[
                    (3 * a + place) * C : (3 * a + place + 1) * C, columns(side)
                ] = moved.astype(BF)
    own_sum = bias_cols[0]
    far_sum = bias_cols[0]
    for a in range(3):
        taps = strip_cols[3 * C * a : 3 * C * (a + 1), :]
        own_sum = own_sum + dot(w_own[a], taps)
        far_sum = far_sum + dot(w_turn[a], taps)
    after = []
    for side in range(2):
        v = jnp.where(inside, own_sum[:, columns(side)], far_sum[:, columns(side)])
        v = v * jax.nn.sigmoid(v)
        v = jnp.where(inside, v, v * flip_sign)
        near_mask = rims[0, side, C // 2 : C // 2 + 1, 0:1].astype(F32)
        far_mask = corners[0, side, 0:1, 24:25].astype(F32)
        side_mask = jnp.where(inside[0:1], near_mask, far_mask)
        after.append((side_mask * (strips[side] + v)).astype(BF).astype(F32))
    next_tile = jnp.where(low, after[0], after[1])
    for r in range(ROWS - 1):
        widen(s1, next_tile, r, 2)

    def second(first, last):
        step = 2 * LANES
        acc[:, first:last] = (
            dot(w_ref[1, 4], s1[0:C, first:last])
            + dot(w_side[1, 1], s1[C : 3 * C, first:last])
            + bias_cols[1]
        )
        acc[:, first:last] += dot(w_ref[1, 7], s1[0:C, first + step : last + step]) + dot(
            w_side[1, 2], s1[C : 3 * C, first + step : last + step]
        )
        low_row = max(first, step)
        acc[:, low_row:last] += dot(w_ref[1, 1], s1[0:C, low_row - step : last - step]) + dot(
            w_side[1, 0], s1[C : 3 * C, low_row - step : last - step]
        )
        activate(1, s1, first, last)

    second(0, 5 * LANES)
    later = Rims(2, s2, 4, True)
    later.turn(3, 4)
    later.send_fold(3, 4)
    later.pack_sides(0, 5)
    prepare_forward(2)

    rim.folds[0][0].wait_recv()
    for k in range(3):
        widen(s0, rim_tile, ROWS + k, 1)
    acc[:, rest:CELLS] += dot(w_ref[0, 7], s0[0:C, CELLS : CELLS + LANES]) + dot(
        w_side[0, 2], s0[C : 3 * C, CELLS : CELLS + LANES]
    )
    activate(0, s0, rest, CELLS)
    v = bias_cols[0]
    for a in range(3):
        v = v + dot(w_turn[a], s0[:, columns(7 + a, 2)])
    v = v * jax.nn.sigmoid(v) * flip_sign
    far_mask = corners[0, 2, 0:1, 24:25].astype(F32)
    s1[0:C, columns(ROWS, 2)] = (far_mask * (s0[0:C, columns(ROWS, 2)].astype(F32) + v)).astype(BF)
    for r in range(ROWS - 1, ROWS + 2):
        widen(s1, next_tile, r, 2)
    second(5 * LANES, CELLS)
    rim = later
    rim.turn(0, 3)
    rim.pack_corners()
    rim.send_corners()
    rim.send_fold(0, 2)
    rim.send_fold(2, 3)
    rim.pack_sides(5, ROWS)
    rim.send_sides()

    d = 4
    rest = CELLS - d * LANES
    acc[...] = dot(w_ref[2, 4], s2[0:C, 0:CELLS]) + bias_cols[2]
    acc[:, 0:rest] += dot(w_ref[2, 7], s2[0:C, d * LANES : CELLS])
    acc[:, d * LANES : CELLS] += dot(w_ref[2, 1], s2[0:C, 0:rest])
    rim.roll_sides()
    prepare_backward(1)
    prepare_backward(0)
    rim.receive_sides()
    acc[...] += dot(w_side[2, 1], s2[C : 3 * C, 0:CELLS])
    acc[:, 0:rest] += dot(w_side[2, 2], s2[C : 3 * C, d * LANES : CELLS])
    acc[:, d * LANES : CELLS] += dot(w_side[2, 0], s2[C : 3 * C, 0:rest])
    activate(2, s2, 0, rest)
    later = Rims(3, t2, d, False)
    later.pack_sides(0, ROWS - d)
    rim.receive_corners()
    for first, last, numbers in ((0, 2, (1,)), (2, 4, (2, 0))):
        for number in numbers:
            rim.receive_fold(number)
        top = slice(rest + first * LANES, rest + last * LANES)
        over = slice(CELLS + first * LANES, CELLS + last * LANES)
        acc[:, top] += dot(w_ref[2, 7], s2[0:C, over]) + dot(w_side[2, 2], s2[C : 3 * C, over])
        activate(2, s2, top.start, top.stop)
        later.turn(d - last, d - first)
        if first == 0:
            later.send_fold(d - last, d - first)
    rim = later
    rim.pack_corners()
    rim.send_corners()
    rim.send_fold(0, d // 2)
    rim.pack_sides(ROWS - d, ROWS)
    rim.send_sides()

    reductions = {}
    for l in (2, 1, 0):
        d = 2**l
        rest = CELLS - d * LANES
        buf = backward_buffers[l]
        if l == 0:
            reductions[0] = weight_sums(0)
            rim.pack_sides(0, ROWS)
            rim.send_sides()
            for older in (0, 1, 2):
                next(reductions[older])
        else:
            reductions[l] = weight_sums(l)
            for older in range(l + 1, 3):
                next(reductions[older])
        acc[...] = dot(v_mid[l, 1], buf[0:C, 0:CELLS])
        acc[:, d * LANES : CELLS] += dot(v_mid[l, 2], buf[0:C, 0:rest])
        acc[:, 0:rest] += dot(v_mid[l, 0], buf[0:C, d * LANES : CELLS])
        rim.roll_sides()
        acc[...] += dot(v_side[l, 1], buf[C : 3 * C, 0:CELLS])
        acc[:, d * LANES : CELLS] += dot(v_side[l, 2], buf[C : 3 * C, 0:rest])
        acc[:, 0:rest] += dot(v_side[l, 0], buf[C : 3 * C, d * LANES : CELLS])
        if l == 2:
            cells_first(out_ref, x_ref)
            store(x_ref, out_hbm)
        rim.receive_edges(l)
        if l == 0:
            for older in (0, 1, 2):
                next(reductions[older])

        def descend(first, last):
            g = mask * (grad[:, first:last] + acc[:, first:last])
            if l > 0:
                grad[:, first:last] = g
                backward_buffers[l - 1][0:C, first:last] = (
                    g * slope[l - 1, :, first:last]
                ).astype(BF)
            else:
                for r in range(first // LANES, last // LANES):
                    fg_ref[r] = g[:, r * LANES - first : (r + 1) * LANES - first].astype(BF)

        descend(0, rest)
        if l > 0:
            next(reductions[l])
        if l == 1:
            block_sums(0, 0, 6 * LANES)
        rim.receive_corners()
        middle = d // 2
        for number, (fold, first, last) in enumerate(rim.folds):
            rim.receive_fold(number)
            top = slice(rest + first * LANES, rest + last * LANES)
            acc[:, top] += dot(
                v_over[l], buf[:, CELLS + first * LANES : CELLS + last * LANES]
            )
            descend(top.start, top.stop)
            if l > 0 and number == 0:
                later = Rims(6 - l, backward_buffers[l - 1], middle, False)
                later.turn(0, middle)
                later.pack_corners()
                later.send_corners()
                if middle > 1:
                    later.send_fold(middle // 2, middle)
                    later.send_fold(0, middle // 2)
                else:
                    later.send_fold(0, 1)
        if l > 0:
            rim = later
        if l > 1:
            rim.pack_sides(0, ROWS)
            rim.send_sides()

    cells_first(fg_ref, ct_ref)
    store(ct_ref, fg_hbm)
    done = object()
    running = [reductions[l] for l in range(3)]
    while running:
        running = [reduction for reduction in running if next(reduction, done) is not done]
    for condition, copy in sends:
        if condition is None:
            copy.wait_send()
        else:

            @pl.when(condition)
            def _():
                copy.wait_send()

    for copy in stores:
        copy.wait()


def finish(
    cells_a,
    cells_b,
    summed,
    out_a,
    out_b,
    kernel_grad,
    bias_grad,
    sums,
    cells,
    kernels,
    bias_rows,
    in_sem,
    out_sem,
):
    loads = [pltpu.make_async_copy(summed.at[l], sums.at[l], in_sem.at[l]) for l in range(3)]
    for number, src in enumerate((cells_a, cells_b)):
        loads.append(pltpu.make_async_copy(src, cells.at[number], in_sem.at[3 + number]))
    for load in loads:
        load.start()
    stores = []

    def store(src, dst):
        copy = pltpu.make_async_copy(src, dst, out_sem.at[len(stores)])
        copy.start()
        stores.append(copy)

    for l in range(3):
        loads[l].wait()
        if l > 0:
            loads[2 + l].wait()
            store(cells.at[l - 1], (out_a, out_b)[l - 1])
        for a in range(3):
            for b in range(3):
                first = a * WIDE + (1, 0, 2)[b] * C
                kernels[l, 3 * a + b] = sums[l, :, first : first + C].astype(F32)
            taps = pl.ds(3 * a, 3)
            store(kernels.at[l, taps], kernel_grad.at[l, taps])
        bias_rows[l : l + 1, :] = sums[l, :, 3 * WIDE : TOTAL].astype(F32).T[0:1]
    store(bias_rows, bias_grad)
    for copy in stores:
        copy.wait()


def shards(fields, cotangent, weights, biases, ocean_tiles, velocity_mask):
    n = lax.axis_size("tiles")
    hbm = pl.BlockSpec(memory_space=pltpu.HBM)
    out, field_grad, summed = pl.pallas_call(
        functools.partial(kernel, n),
        out_shape=(
            jax.ShapeDtypeStruct((C, ROWS, LANES), BF),
            jax.ShapeDtypeStruct((C, ROWS, LANES), BF),
            jax.ShapeDtypeStruct((3, C, TOTAL), BF),
        ),
        in_specs=[
            hbm,
            hbm,
            hbm,
            hbm,
            pl.BlockSpec(memory_space=pltpu.SMEM),
            hbm,
        ],
        out_specs=(hbm,) * 3,
        scratch_shapes=[
            pltpu.VMEM((3 * C, CELLS + 3 * LANES), BF),
            pltpu.VMEM((3 * C, CELLS + 2 * LANES), BF),
            pltpu.VMEM((3 * C, CELLS + 4 * LANES), BF),
            pltpu.VMEM((3 * C, CELLS + LANES), BF),
            pltpu.VMEM((3 * C, CELLS + 2 * LANES), BF),
            pltpu.VMEM((3 * C, CELLS + 4 * LANES), BF),
            pltpu.VMEM((C, ROWS, LANES), BF),
            pltpu.VMEM((C, ROWS, LANES), BF),
            pltpu.VMEM((3, C), F32),
            pltpu.VMEM((C,), jnp.int32),
            pltpu.VMEM((3, 9, C, C), BF),
            pltpu.VMEM((ROWS, C, LANES), BF),
            pltpu.VMEM((ROWS, C, LANES), BF),
            pltpu.VMEM((C * ROWS, LANES), F32),
            pltpu.VMEM((LANES, 2 * LANES), F32),
            pltpu.VMEM((3, C, CELLS), F32),
            pltpu.VMEM((C, CELLS), F32),
            pltpu.VMEM((C, CELLS), F32),
            pltpu.VMEM((3, 3, C, 2 * C), BF),
            pltpu.VMEM((3, 3, C, C), BF),
            pltpu.VMEM((3, 3, C, 2 * C), BF),
            pltpu.VMEM((3, C, 3 * C), BF),
            pltpu.VMEM((6, C, LANES), BF),
            pltpu.VMEM((C, LANES), F32),
            pltpu.VMEM((C, LANES), F32),
            pltpu.VMEM((9 * C, 2 * LANES), BF),
            pltpu.VMEM((3, C, 3 * C), BF),
            pltpu.VMEM((3, C, 3 * C), BF),
            pltpu.VMEM((6, BAND, LANES), BF),
            pltpu.VMEM((6, C, 4 * LANES), BF),
            pltpu.VMEM((6, 2, C, LANES), BF),
            pltpu.VMEM((6, 3, BAND, LANES), BF),
            pltpu.VMEM((3, C, TOTAL), F32),
            pltpu.VMEM((3, C, HALF), BF),
            pltpu.VMEM((3, C, HALF), BF),
            pltpu.VMEM((3, C, HALF), BF),
            pltpu.VMEM((3, 3, BAND, HALF), BF),
            pltpu.VMEM((3, 4, BAND, HALF), BF),
            pltpu.VMEM((3, 4, BAND, HALF), BF),
            pltpu.VMEM((3, C, TOTAL), BF),
            pltpu.SemaphoreType.DMA((7,)),
            pltpu.SemaphoreType.DMA((5,)),
            pltpu.SemaphoreType.DMA((6, 7)),
            pltpu.SemaphoreType.DMA((6, 7)),
            pltpu.SemaphoreType.DMA((3, 40)),
            pltpu.SemaphoreType.DMA((3, 40)),
        ],
        compiler_params=pltpu.CompilerParams(
            collective_id=0, has_side_effects=True, vmem_limit_bytes=62 * 1024 * 1024
        ),
        cost_estimate=pl.CostEstimate(
            flops=18 * 9 * C * C * CELLS, bytes_accessed=8 * 1024 * 1024, transcendentals=9 * C * CELLS
        ),
    )(fields, cotangent, weights, biases, ocean_tiles, velocity_mask)
    return pl.pallas_call(
        finish,
        out_shape=(
            jax.ShapeDtypeStruct((C, ROWS, LANES), BF),
            jax.ShapeDtypeStruct((C, ROWS, LANES), BF),
            jax.ShapeDtypeStruct((3, 9, C, C), F32),
            jax.ShapeDtypeStruct((3, C), F32),
        ),
        in_specs=[hbm] * 3,
        out_specs=(hbm,) * 4,
        scratch_shapes=[
            pltpu.VMEM((3, C, TOTAL), BF),
            pltpu.VMEM((2, C, ROWS, LANES), BF),
            pltpu.VMEM((3, 9, C, C), F32),
            pltpu.VMEM((3, C), F32),
            pltpu.SemaphoreType.DMA((5,)),
            pltpu.SemaphoreType.DMA((12,)),
        ],
        compiler_params=pltpu.CompilerParams(vmem_limit_bytes=62 * 1024 * 1024),
    )(out, field_grad, summed)


def solution(mesh):
    placed = (P(None, None, "tiles"), P(None, None, "tiles"), P(), P(), P(None, "tiles"), P())
    return jax.shard_map(
        shards,
        mesh=mesh,
        in_specs=placed,
        out_specs=(P(None, None, "tiles"), P(None, None, "tiles"), P(), P()),
        check_vma=False,
    )
```

```python
import functools

import jax
import jax.numpy as jnp
from jax import lax
from jax.experimental import pallas as pl
from jax.experimental.pallas import tpu as pltpu
from jax.sharding import PartitionSpec as P

C = 192
ROWS = 8
LANES = 128
CELLS = ROWS * LANES
WIDE = 640
TOTAL = 2048
HALF = TOTAL // 2
BAND = C // 4
BF = jnp.bfloat16
F32 = jnp.float32
MESH = pl.DeviceIdType.MESH

CORE = (1, 2)
Y = (2, 4)
X = (8, 4)
Z = (32, 4)
PARTS = (
    (pl.ds(0, 384), (Y, X, Z)),
    (pl.ds(384, 384), (Z, Y, X)),
    (pl.ds(768, 256), (X, Z, Y)),
)


def coordinate(me, axis):
    return lax.rem(lax.div(me, axis[0]), axis[1])


def with_coordinate(me, axis, value):
    return me + (value - coordinate(me, axis)) * axis[0]


def copy_to(src, dst, send_sem, recv_sem, device):
    return pltpu.make_async_remote_copy(
        src_ref=src,
        dst_ref=dst,
        send_sem=send_sem,
        recv_sem=recv_sem,
        device_id=(device,),
        device_id_type=MESH,
    )


def start_if(condition, copy):
    @pl.when(condition)
    def _():
        copy.start()


def dot(a, b):
    return jnp.dot(a, b, preferred_element_type=F32)


def dot_nt(a, b):
    return lax.dot_general(a, b, (((1,), (1,)), ((), ())), preferred_element_type=F32)


def kernel(
    n,
    x_hbm,
    ct_hbm,
    w_hbm,
    bias_hbm,
    ocean_ref,
    velocity_hbm,
    out_hbm,
    fg_hbm,
    dw_hbm,
    s0,
    s1,
    s2,
    t0,
    t1,
    t2,
    x_ref,
    ct_ref,
    bias_ref,
    velocity_ref,
    w_ref,
    out_ref,
    fg_ref,
    spread_rows,
    cols_ref,
    slope,
    acc,
    grad,
    w_side,
    v_mid,
    v_side,
    v_over,
    packed,
    side_tile,
    own_tile,
    strip_cols,
    w_own,
    w_turn,
    corner,
    turned,
    rims,
    corners,
    partial,
    to_mate,
    from_mate,
    a_out,
    a_in,
    b_in,
    c_in,
    full,
    w_sem,
    out_sem,
    ex_send,
    ex_recv,
    ar_send,
    ar_recv,
):
    me = lax.axis_index("tiles")
    east = lax.rem(me + 1, n)
    west = lax.rem(me + n - 1, n)
    mirror = n - 1 - me
    fold_a = lax.rem(n - me, n)
    fold_b = lax.rem(2 * n - 2 - me, n)
    mate = with_coordinate(me, CORE, 1 - coordinate(me, CORE))
    core = coordinate(me, CORE)
    a_away = fold_a != me
    b_away = fold_b != me

    barrier = pltpu.get_barrier_semaphore()
    partners = [east, west, mirror, mate]
    for axis in (Y, X, Z):
        for step in (1, 2, 3):
            partners.append(
                with_coordinate(me, axis, lax.rem(coordinate(me, axis) + step, axis[1]))
            )
    for partner in partners:
        pl.semaphore_signal(barrier, inc=1, device_id=(partner,), device_id_type=MESH)

    @pl.when(a_away)
    def _():
        pl.semaphore_signal(barrier, inc=1, device_id=(fold_a,), device_id_type=MESH)

    @pl.when(b_away)
    def _():
        pl.semaphore_signal(barrier, inc=1, device_id=(fold_b,), device_id_type=MESH)

    small = [
        pltpu.make_async_copy(src, dst, w_sem.at[3 + number])
        for number, (src, dst) in enumerate(
            (
                (bias_hbm, bias_ref),
                (velocity_hbm, velocity_ref),
                (x_hbm, x_ref),
                (ct_hbm, ct_ref),
            )
        )
    ]
    loads = [
        pltpu.make_async_copy(w_hbm.at[l], w_ref.at[l], w_sem.at[l]) for l in range(3)
    ]
    for load in small[2:3] + small[:2] + loads[:1] + small[3:] + loads[1:]:
        load.start()

    lane = lax.broadcasted_iota(jnp.int32, (C, LANES), 1)
    flip_matrix = (
        lax.broadcasted_iota(jnp.int32, (LANES, LANES), 0)
        + lax.broadcasted_iota(jnp.int32, (LANES, LANES), 1)
        == LANES - 1
    ).astype(F32).astype(BF)
    cols_ref[...] = jnp.zeros((LANES, 2 * LANES), F32)
    small[0].wait()
    small[1].wait()
    cols_ref[0:3, 0:C] = bias_ref[...]
    cols_ref[3:4, 0:C] = (1 - 2 * velocity_ref[...]).astype(F32).reshape(1, C)
    turned_cols = cols_ref[...].T[0:C]
    bias_cols = [turned_cols[:, l : l + 1] for l in range(3)]
    flip_sign = turned_cols[:, 3:4]
    mask = ocean_ref[0, 0].astype(F32)
    sends = []

    stores = []

    def store(src, dst):
        copy = pltpu.make_async_copy(src, dst, out_sem.at[len(stores)])
        copy.start()
        stores.append(copy)

    def columns(row, count=1):
        return slice(row * LANES, (row + count) * LANES)

    def dense(tile, groups):
        size = C // groups
        total = tile[0:size]
        for q in range(1, groups):
            piece = tile[q * size : (q + 1) * size]
            total = total + pltpu.roll(piece, q * LANES // groups, 1)
        return total.astype(BF)

    def loose(total, groups):
        total = total.astype(F32)
        return jnp.concatenate(
            [total]
            + [pltpu.roll(total, LANES - q * LANES // groups, 1) for q in range(1, groups)],
            axis=0,
        )

    def slots(rows, count):
        tile = jnp.zeros((C, LANES), F32)
        for r in range(count):
            here = jnp.logical_and(lane >= 8 * r, lane < 8 * r + 8)
            tile = jnp.where(here, pltpu.roll(rows(r).astype(F32), (8 * r + 4) % LANES, 1), tile)
        return tile

    def widen(buf, rim, row, d):
        center = buf[0:C, columns(row)].astype(F32)
        left = pltpu.roll(rim, (-(8 * row + 4 - d)) % LANES, 1)
        right = pltpu.roll(rim, (-(8 * row + 4 + d)) % LANES, 1)
        buf[C : 2 * C, columns(row)] = jnp.where(
            lane < d, left, pltpu.roll(center, d, 1)
        ).astype(BF)
        buf[2 * C : 3 * C, columns(row)] = jnp.where(
            lane >= LANES - d, right, pltpu.roll(center, LANES - d, 1)
        ).astype(BF)

    class Rims:
        def __init__(self, e, buf, d, signed):
            self.e, self.buf, self.d, self.signed = e, buf, d, signed
            self.folds = []
            self.groups = 4 if d <= 2 else 2

        def turn(self, first, last):
            for k in range(first, last):
                row = dot(self.buf[0:C, columns(ROWS - 1 - k)], flip_matrix)
                if self.signed:
                    row = row * flip_sign
                turned[self.e, :, columns(k)] = row.astype(BF)

        def send_fold(self, first, last):
            slot = 4 + len(self.folds)
            fold = copy_to(
                turned.at[self.e, :, pl.ds(first * LANES, (last - first) * LANES)],
                self.buf.at[pl.ds(0, C), pl.ds(CELLS + first * LANES, (last - first) * LANES)],
                ex_send.at[self.e, slot],
                ex_recv.at[self.e, slot],
                mirror,
            )
            fold.start()
            self.folds.append((fold, first, last))
            sends.append((None, fold))

        def pack(self, tile, rows, first, last):
            d = self.d
            for r in range(first, last):
                at = 2 * d * r
                here = jnp.logical_and(lane >= at, lane < at + 2 * d)
                tile = jnp.where(here, pltpu.roll(rows(r).astype(F32), (at + d) % LANES, 1), tile)
            return tile

        def pack_sides(self, first, last):
            tile = jnp.zeros((C, LANES), F32) if first == 0 else side_tile[...]
            side_tile[...] = self.pack(
                tile, lambda r: self.buf[0:C, columns(r)], first, last
            )
            if last == ROWS:
                packed[self.e, 0 : C // self.groups] = dense(side_tile[...], self.groups)

        def pack_corners(self):
            tile = self.pack(
                jnp.zeros((C, LANES), F32), lambda k: turned[self.e, :, columns(k)], 0, self.d
            )
            corner[self.e] = dense(tile, 4)

        def send_sides(self):
            self.sides = []
            for slot, target in enumerate((east, west)):
                copy = copy_to(
                    packed.at[self.e, pl.ds(0, C // self.groups)],
                    rims.at[self.e, slot, pl.ds(0, C // self.groups)],
                    ex_send.at[self.e, slot],
                    ex_recv.at[self.e, slot],
                    target,
                )
                copy.start()
                self.sides.append(copy)
                sends.append((None, copy))

        def send_corners(self):
            self.turns = []
            for slot, target, away in ((0, fold_a, a_away), (1, fold_b, b_away)):
                copy = copy_to(
                    corner.at[self.e],
                    corners.at[self.e, slot],
                    ex_send.at[self.e, 2 + slot],
                    ex_recv.at[self.e, 2 + slot],
                    target,
                )
                start_if(away, copy)
                self.turns.append((away, copy))
                sends.append((away, copy))

        def unpack(self, rim, row, slot):
            buf, d = self.buf, self.d
            center = buf[0:C, columns(row)].astype(F32)
            edge = pltpu.roll(rim, (-(2 * d * slot + d)) % LANES, 1)
            left = pltpu.roll(jnp.where(lane >= LANES - d, edge, center), d, 1)
            right = pltpu.roll(jnp.where(lane < d, edge, center), LANES - d, 1)
            buf[C : 2 * C, columns(row)] = left.astype(BF)
            buf[2 * C : 3 * C, columns(row)] = right.astype(BF)

        def roll_sides(self):
            buf, d = self.buf, self.d
            for r in range(ROWS):
                center = buf[0:C, columns(r)].astype(F32)
                left = jnp.where(lane < d, 0.0, pltpu.roll(center, d, 1))
                right = jnp.where(lane >= LANES - d, 0.0, pltpu.roll(center, LANES - d, 1))
                buf[C : 2 * C, columns(r)] = left.astype(BF)
                buf[2 * C : 3 * C, columns(r)] = right.astype(BF)

        def receive_sides(self):
            buf, d = self.buf, self.d
            for copy in self.sides:
                copy.wait_recv()
            size = C // self.groups
            low = lax.rem(lane, 2 * d) < d
            rim = jnp.where(
                low,
                loose(rims[self.e, 0, 0:size], self.groups),
                loose(rims[self.e, 1, 0:size], self.groups),
            )
            for r in range(ROWS + 1):
                edge = pltpu.roll(rim, (-2 * d * r) % LANES, 1) if r > 0 else rim
                if r < ROWS:
                    old = buf[C : 2 * C, columns(r)].astype(F32)
                    buf[C : 2 * C, columns(r)] = jnp.where(lane < d, edge, old).astype(BF)
                if r > 0:
                    old = buf[2 * C : 3 * C, columns(r - 1)].astype(F32)
                    buf[2 * C : 3 * C, columns(r - 1)] = jnp.where(
                        lane >= LANES - d, edge, old
                    ).astype(BF)

        def receive_edges(self, l):
            d = self.d
            for copy in self.sides:
                copy.wait_recv()
            size = C // self.groups
            low = lax.rem(lane, 2 * d) < d
            rim = jnp.where(
                low,
                loose(rims[self.e, 0, 0:size], self.groups),
                loose(rims[self.e, 1, 0:size], self.groups),
            )
            rim = jnp.where(lane < 2 * d * ROWS, rim, 0.0)
            left = right = 0.0
            for a, shift in ((1, 0), (2, 2 * d * d), (0, LANES - 2 * d * d)):
                moved = (pltpu.roll(rim, shift, 1) if shift else rim).astype(BF)
                left = left + dot(v_side[l, a, :, 0:C], moved)
                right = right + dot(v_side[l, a, :, C : 2 * C], moved)
            both = jnp.where(low, left, right)
            edge = both
            for r in range(ROWS):
                after = pltpu.roll(both, (-2 * d * (r + 1)) % LANES, 1)
                acc[:, columns(r)] += jnp.where(
                    lane < d, edge, jnp.where(lane >= LANES - d, after, 0.0)
                )
                edge = after

        def receive_corners(self):
            for slot, (away, copy) in enumerate(self.turns):

                @pl.when(away)
                def _():
                    copy.wait_recv()

                @pl.when(jnp.logical_not(away))
                def _():
                    corners[self.e, slot] = corner[self.e]

            low = lax.rem(lane, 2 * self.d) < self.d
            tiles = [loose(corners[self.e, slot], 4) for slot in range(2)]
            self.rim = jnp.where(low, tiles[0], tiles[1])

        def receive_fold(self, number):
            fold, first, last = self.folds[number]
            fold.wait_recv()
            for k in range(first, last):
                self.unpack(self.rim, ROWS + k, k)

    def all_reduce(l):
        half = pl.ds(pl.multiple_of(core * HALF, LANES), HALF)
        other = pl.ds(pl.multiple_of((1 - core) * HALF, LANES), HALF)
        count = [0]

        def post(src, dst, target):
            number = count[0]
            count[0] += 1
            copy = copy_to(src, dst, ar_send.at[l, number], ar_recv.at[l, number], target)
            copy.start()
            sends.append((None, copy))
            return copy

        def around(axis):
            for step in (2, 1, 3):
                to = lax.rem(coordinate(me, axis) + step, 4)
                yield step - 1, to, with_coordinate(me, axis, to)

        def exchange(total, landing, axis, lanes):
            mine = coordinate(me, axis)
            landing[mine, :, lanes] = total.astype(BF)
            piece = landing.at[mine, :, lanes]
            return [post(piece, piece, target) for slot, to, target in around(axis)]

        def arrived(landing, copies, lanes):
            for copy in copies:
                copy.wait_recv()
            total = landing[0, :, lanes].astype(F32)
            for slot in range(1, 4):
                total = total + landing[slot, :, lanes].astype(F32)
            return total

        to_mate[l] = partial[l, :, other].astype(BF)
        copy = post(to_mate.at[l], from_mate.at[l], mate)
        yield
        copy.wait_recv()
        a_out[l] = (partial[l, :, half] + from_mate[l].astype(F32)).astype(BF)
        waits = []
        for lanes, axes in PARTS:
            waits.append(
                [
                    post(
                        a_out.at[l, pl.ds(pl.multiple_of(to * BAND, 16), BAND), lanes],
                        a_in.at[l, slot, :, lanes],
                        target,
                    )
                    for slot, to, target in around(axes[0])
                ]
            )
        yield
        for part, (lanes, axes) in enumerate(PARTS):
            for copy in waits[part]:
                copy.wait_recv()
            band = pl.ds(pl.multiple_of(coordinate(me, axes[0]) * BAND, 16), BAND)
            total = a_out[l, band, lanes].astype(F32)
            for slot in range(3):
                total = total + a_in[l, slot, :, lanes].astype(F32)
            waits[part] = exchange(total, b_in.at[l], axes[1], lanes)
        yield
        for part, (lanes, axes) in enumerate(PARTS):
            total = arrived(b_in.at[l], waits[part], lanes)
            waits[part] = exchange(total, c_in.at[l], axes[2], lanes)
        yield
        for part, (lanes, axes) in enumerate(PARTS):
            total = arrived(c_in.at[l], waits[part], lanes)
            band = pl.ds(pl.multiple_of(coordinate(me, axes[0]) * BAND, 16), BAND)
            here = pl.ds(pl.multiple_of(core * HALF + lanes.start, LANES), lanes.size)
            full[l, band, here] = total.astype(BF)
            piece = full.at[l, band, here]
            waits[part] = [post(piece, piece, target) for slot, to, target in around(axes[0])]
        yield
        final = []
        for part, (lanes, axes) in enumerate(PARTS):
            for copy in waits[part]:
                copy.wait_recv()
            here = pl.ds(pl.multiple_of(core * HALF + lanes.start, LANES), lanes.size)
            piece = full.at[l, :, here]
            final.append(post(piece, piece, mate))
        yield
        for copy in final:
            copy.wait_recv()
        store(full.at[l], dw_hbm.at[l])
        yield

    def block_sums(l, first, last):
        delta, stored = backward_buffers[l], forward_buffers[l]
        for a in range(3):
            shift = (a - 1) * 2**l * LANES
            low = max(first, -shift)
            block = dot_nt(delta[0:C, low:last], stored[:, low + shift : last + shift])
            if first == 0:
                partial[l, :, a * WIDE + 512 : (a + 1) * WIDE] = jnp.zeros((C, LANES), F32)
                partial[l, :, a * WIDE : a * WIDE + 3 * C] = block
            else:
                partial[l, :, a * WIDE : a * WIDE + 3 * C] += block

    def weight_sums(l):
        block_sums(l, 0 if l > 0 else 6 * LANES, CELLS)
        delta = backward_buffers[l]
        partial[l, :, 3 * WIDE : TOTAL] = jnp.broadcast_to(
            jnp.sum(delta[0:C, 0:CELLS].astype(F32), axis=1, keepdims=True), (C, LANES)
        )
        reduction = all_reduce(l)
        next(reduction)
        return reduction

    def cells_first(rows, cells):
        for r in range(ROWS):
            spread_rows[pl.ds(r, C, stride=ROWS), :] = rows[r].astype(F32)
        cells[...] = spread_rows[...].reshape(C, ROWS, LANES).astype(BF)

    def prepare_forward(l):
        for a in range(3):
            w_side[l, a, :, 0:C] = w_ref[l, 3 * a]
            w_side[l, a, :, C : 2 * C] = w_ref[l, 3 * a + 2]

    def prepare_backward(l):
        for a in range(3):
            v_mid[l, a] = w_ref[l, 3 * a + 1].T
            v_side[l, a, :, 0:C] = w_ref[l, 3 * a + 2].T
            v_side[l, a, :, C : 2 * C] = w_ref[l, 3 * a].T
        for place, tap in enumerate((7, 6, 8)):
            v_over[l, :, place * C : (place + 1) * C] = (
                w_ref[l, tap].T.astype(F32) * flip_sign
            ).astype(BF)

    forward_buffers = (s0, s1, s2)
    backward_buffers = (t0, t1, t2)

    small[2].wait()
    spread_rows[...] = x_ref[...].astype(F32).reshape(C * ROWS, LANES)
    for r in range(ROWS):
        row = spread_rows[pl.ds(r, C, stride=ROWS), :]
        s0[0:C, columns(r)] = (row * mask).astype(BF)
    rim = Rims(0, s0, 1, True)
    rim.turn(0, 3)
    own_tile[...] = slots(lambda r: s0[0:C, columns(r)], ROWS)
    packed[0, 0 : C // 2] = dense(own_tile[...], 2)
    packed[0, C // 2 : C // 2 + 16] = jnp.full((16, LANES), mask, F32).astype(BF)
    tile = slots(lambda k: turned[0, :, columns(k)], 3)
    tile = jnp.where(jnp.logical_and(lane >= 24, lane < 32), mask, tile)
    corner[0] = dense(tile, 4)
    pl.semaphore_wait(
        barrier, len(partners) + a_away.astype(jnp.int32) + b_away.astype(jnp.int32)
    )
    sides = [
        copy_to(
            packed.at[0, pl.ds(0, C // 2 + 16)],
            rims.at[0, slot, pl.ds(0, C // 2 + 16)],
            ex_send.at[0, slot],
            ex_recv.at[0, slot],
            target,
        )
        for slot, target in enumerate((east, west))
    ]
    over = copy_to(
        corner.at[0], corners.at[0, 2], ex_send.at[0, 5], ex_recv.at[0, 5], mirror
    )
    for copy in sides + [over]:
        copy.start()
        sends.append((None, copy))
    rim.send_corners()
    rim.send_fold(0, 3)

    def activate(l, buf, first, last):
        v = acc[:, first:last]
        s = jax.nn.sigmoid(v)
        after = mask * (buf[0:C, first:last].astype(F32) + v * s)
        s = s * (1.0 + v * (1.0 - s))
        slope[l, :, first:last] = s
        if l < 2:
            forward_buffers[l + 1][0:C, first:last] = after.astype(BF)
        else:
            for r in range(first // LANES, last // LANES):
                out_ref[r] = after[:, r * LANES - first : (r + 1) * LANES - first].astype(BF)
            t2[0:C, first:last] = (grad[:, first:last] * s).astype(BF)

    loads[0].wait()
    prepare_forward(0)
    for a in range(3):
        for place, b in enumerate((1, 0, 2)):
            part = slice(place * C, (place + 1) * C)
            w_own[a, :, part] = w_ref[0, 3 * a + b]
            w_turn[a, :, part] = (w_ref[0, 8 - 3 * a - b].astype(F32) * cols_ref[3:4, 0:C]).astype(
                BF
            )
    small[3].wait()
    spread_rows[...] = ct_ref[...].astype(F32).reshape(C * ROWS, LANES)
    for r in range(ROWS):
        grad[:, columns(r)] = mask * spread_rows[pl.ds(r, C, stride=ROWS), :]
    loads[1].wait()
    loads[2].wait()
    rest = CELLS - LANES
    acc[...] = dot(w_ref[0, 4], s0[0:C, 0:CELLS]) + bias_cols[0]
    acc[:, 0:rest] += dot(w_ref[0, 7], s0[0:C, LANES:CELLS])
    acc[:, LANES:CELLS] += dot(w_ref[0, 1], s0[0:C, 0:rest])
    prepare_forward(1)
    prepare_backward(2)
    for copy in sides:
        copy.wait_recv()
    low = lax.rem(lane, 8) < 4
    west_tile = loose(rims[0, 0, 0 : C // 2], 2)
    east_tile = loose(rims[0, 1, 0 : C // 2], 2)
    rim_tile = jnp.where(low, west_tile, east_tile)
    for r in range(ROWS):
        widen(s0, rim_tile, r, 1)
    acc[...] += dot(w_side[0, 1], s0[C : 3 * C, 0:CELLS])
    acc[:, 0:rest] += dot(w_side[0, 2], s0[C : 3 * C, LANES:CELLS])
    acc[:, LANES:CELLS] += dot(w_side[0, 0], s0[C : 3 * C, 0:rest])
    activate(0, s0, 0, rest)

    for slot, (away, copy) in enumerate(rim.turns):

        @pl.when(away)
        def _():
            copy.wait_recv()

        @pl.when(jnp.logical_not(away))
        def _():
            corners[0, slot] = corner[0]

    over.wait_recv()
    far_a, far_b, far = (pltpu.roll(loose(corners[0, slot], 4), 64, 1) for slot in range(3))
    inside = lane < 64
    beyond = lane < 88
    strips = [
        jnp.where(
            inside,
            jnp.where(low, west_tile, own_tile[...]),
            jnp.where(beyond, jnp.where(low, far_a, far), 0.0),
        ),
        jnp.where(
            inside,
            jnp.where(low, own_tile[...], east_tile),
            jnp.where(beyond, jnp.where(low, far, far_b), 0.0),
        ),
    ]
    rim_tile = jnp.where(low, strips[0], strips[1])
    for a in range(3):
        for place, b in enumerate((0, -1, 1)):
            shift = (-(8 * (a - 1) + b)) % LANES
            for side in range(2):
                moved = pltpu.roll(strips[side], shift, 1) if shift else strips[side]
                strip_cols[
                    (3 * a + place) * C : (3 * a + place + 1) * C, columns(side)
                ] = moved.astype(BF)
    own_sum = bias_cols[0]
    far_sum = bias_cols[0]
    for a in range(3):
        taps = strip_cols[3 * C * a : 3 * C * (a + 1), :]
        own_sum = own_sum + dot(w_own[a], taps)
        far_sum = far_sum + dot(w_turn[a], taps)
    after = []
    for side in range(2):
        v = jnp.where(inside, own_sum[:, columns(side)], far_sum[:, columns(side)])
        v = v * jax.nn.sigmoid(v)
        v = jnp.where(inside, v, v * flip_sign)
        near_mask = rims[0, side, C // 2 : C // 2 + 1, 0:1].astype(F32)
        far_mask = corners[0, side, 0:1, 24:25].astype(F32)
        side_mask = jnp.where(inside[0:1], near_mask, far_mask)
        after.append((side_mask * (strips[side] + v)).astype(BF).astype(F32))
    next_tile = jnp.where(low, after[0], after[1])
    for r in range(ROWS - 1):
        widen(s1, next_tile, r, 2)

    def second(first, last):
        step = 2 * LANES
        acc[:, first:last] = (
            dot(w_ref[1, 4], s1[0:C, first:last])
            + dot(w_side[1, 1], s1[C : 3 * C, first:last])
            + bias_cols[1]
        )
        acc[:, first:last] += dot(w_ref[1, 7], s1[0:C, first + step : last + step]) + dot(
            w_side[1, 2], s1[C : 3 * C, first + step : last + step]
        )
        low_row = max(first, step)
        acc[:, low_row:last] += dot(w_ref[1, 1], s1[0:C, low_row - step : last - step]) + dot(
            w_side[1, 0], s1[C : 3 * C, low_row - step : last - step]
        )
        activate(1, s1, first, last)

    second(0, 5 * LANES)
    later = Rims(2, s2, 4, True)
    later.turn(3, 4)
    later.send_fold(3, 4)
    later.pack_sides(0, 5)
    prepare_forward(2)

    rim.folds[0][0].wait_recv()
    for k in range(3):
        widen(s0, rim_tile, ROWS + k, 1)
    acc[:, rest:CELLS] += dot(w_ref[0, 7], s0[0:C, CELLS : CELLS + LANES]) + dot(
        w_side[0, 2], s0[C : 3 * C, CELLS : CELLS + LANES]
    )
    activate(0, s0, rest, CELLS)
    v = bias_cols[0]
    for a in range(3):
        v = v + dot(w_turn[a], s0[:, columns(7 + a, 2)])
    v = v * jax.nn.sigmoid(v) * flip_sign
    far_mask = corners[0, 2, 0:1, 24:25].astype(F32)
    s1[0:C, columns(ROWS, 2)] = (far_mask * (s0[0:C, columns(ROWS, 2)].astype(F32) + v)).astype(BF)
    for r in range(ROWS - 1, ROWS + 2):
        widen(s1, next_tile, r, 2)
    second(5 * LANES, CELLS)
    rim = later
    rim.turn(0, 3)
    rim.pack_corners()
    rim.send_corners()
    rim.send_fold(0, 2)
    rim.send_fold(2, 3)
    rim.pack_sides(5, ROWS)
    rim.send_sides()

    d = 4
    rest = CELLS - d * LANES
    acc[...] = dot(w_ref[2, 4], s2[0:C, 0:CELLS]) + bias_cols[2]
    acc[:, 0:rest] += dot(w_ref[2, 7], s2[0:C, d * LANES : CELLS])
    acc[:, d * LANES : CELLS] += dot(w_ref[2, 1], s2[0:C, 0:rest])
    rim.roll_sides()
    prepare_backward(1)
    prepare_backward(0)
    rim.receive_sides()
    acc[...] += dot(w_side[2, 1], s2[C : 3 * C, 0:CELLS])
    acc[:, 0:rest] += dot(w_side[2, 2], s2[C : 3 * C, d * LANES : CELLS])
    acc[:, d * LANES : CELLS] += dot(w_side[2, 0], s2[C : 3 * C, 0:rest])
    activate(2, s2, 0, rest)
    later = Rims(3, t2, d, False)
    later.pack_sides(0, ROWS - d)
    rim.receive_corners()
    for first, last, numbers in ((0, 2, (1,)), (2, 4, (2, 0))):
        for number in numbers:
            rim.receive_fold(number)
        top = slice(rest + first * LANES, rest + last * LANES)
        over = slice(CELLS + first * LANES, CELLS + last * LANES)
        acc[:, top] += dot(w_ref[2, 7], s2[0:C, over]) + dot(w_side[2, 2], s2[C : 3 * C, over])
        activate(2, s2, top.start, top.stop)
        later.turn(d - last, d - first)
        if first == 0:
            later.send_fold(d - last, d - first)
    rim = later
    rim.pack_corners()
    rim.send_corners()
    rim.send_fold(0, d // 2)
    rim.pack_sides(ROWS - d, ROWS)
    rim.send_sides()

    reductions = {}
    for l in (2, 1, 0):
        d = 2**l
        rest = CELLS - d * LANES
        buf = backward_buffers[l]
        if l == 0:
            reductions[0] = weight_sums(0)
            rim.pack_sides(0, ROWS)
            rim.send_sides()
            for older in (0, 1, 2):
                next(reductions[older])
        else:
            reductions[l] = weight_sums(l)
            for older in range(l + 1, 3):
                next(reductions[older])
        acc[...] = dot(v_mid[l, 1], buf[0:C, 0:CELLS])
        acc[:, d * LANES : CELLS] += dot(v_mid[l, 2], buf[0:C, 0:rest])
        acc[:, 0:rest] += dot(v_mid[l, 0], buf[0:C, d * LANES : CELLS])
        rim.roll_sides()
        acc[...] += dot(v_side[l, 1], buf[C : 3 * C, 0:CELLS])
        acc[:, d * LANES : CELLS] += dot(v_side[l, 2], buf[C : 3 * C, 0:rest])
        acc[:, 0:rest] += dot(v_side[l, 0], buf[C : 3 * C, d * LANES : CELLS])
        if l == 2:
            cells_first(out_ref, x_ref)
            store(x_ref, out_hbm)
        rim.receive_edges(l)
        if l == 0:
            for older in (0, 1, 2):
                next(reductions[older])

        def descend(first, last):
            g = mask * (grad[:, first:last] + acc[:, first:last])
            if l > 0:
                grad[:, first:last] = g
                backward_buffers[l - 1][0:C, first:last] = (
                    g * slope[l - 1, :, first:last]
                ).astype(BF)
            else:
                for r in range(first // LANES, last // LANES):
                    fg_ref[r] = g[:, r * LANES - first : (r + 1) * LANES - first].astype(BF)

        descend(0, rest)
        if l > 0:
            next(reductions[l])
        if l == 1:
            block_sums(0, 0, 6 * LANES)
        rim.receive_corners()
        middle = d // 2
        for number, (fold, first, last) in enumerate(rim.folds):
            rim.receive_fold(number)
            top = slice(rest + first * LANES, rest + last * LANES)
            acc[:, top] += dot(
                v_over[l], buf[:, CELLS + first * LANES : CELLS + last * LANES]
            )
            descend(top.start, top.stop)
            if l > 0 and number == 0:
                later = Rims(6 - l, backward_buffers[l - 1], middle, False)
                later.turn(0, middle)
                later.pack_corners()
                later.send_corners()
                if middle > 1:
                    later.send_fold(middle // 2, middle)
                    later.send_fold(0, middle // 2)
                else:
                    later.send_fold(0, 1)
        if l > 0:
            rim = later
        if l > 1:
            rim.pack_sides(0, ROWS)
            rim.send_sides()

    cells_first(fg_ref, ct_ref)
    store(ct_ref, fg_hbm)
    done = object()
    running = [reductions[l] for l in range(3)]
    while running:
        running = [reduction for reduction in running if next(reduction, done) is not done]
    for condition, copy in sends:
        if condition is None:
            copy.wait_send()
        else:

            @pl.when(condition)
            def _():
                copy.wait_send()

    for copy in stores:
        copy.wait()


def finish(
    cells_a,
    cells_b,
    summed,
    out_a,
    out_b,
    kernel_grad,
    bias_grad,
    sums,
    cells,
    kernels,
    bias_rows,
    in_sem,
    out_sem,
):
    loads = [pltpu.make_async_copy(summed.at[l], sums.at[l], in_sem.at[l]) for l in range(3)]
    for number, src in enumerate((cells_a, cells_b)):
        loads.append(pltpu.make_async_copy(src, cells.at[number], in_sem.at[3 + number]))
    for load in loads:
        load.start()
    stores = []

    def store(src, dst):
        copy = pltpu.make_async_copy(src, dst, out_sem.at[len(stores)])
        copy.start()
        stores.append(copy)

    biases = []
    for l in range(3):
        loads[l].wait()
        if l > 0:
            loads[2 + l].wait()
            store(cells.at[l - 1], (out_a, out_b)[l - 1])
        for a in range(3):
            for b in range(3):
                first = a * WIDE + (1, 0, 2)[b] * C
                kernels[l, 3 * a + b] = sums[l, :, first : first + C].astype(F32)
            taps = pl.ds(3 * a, 3)
            store(kernels.at[l, taps], kernel_grad.at[l, taps])
        biases.append(sums[l, :, 3 * WIDE : TOTAL].astype(F32).T[0:1])
    bias_rows[...] = jnp.concatenate(biases, axis=0)
    store(bias_rows, bias_grad)
    for copy in stores:
        copy.wait()


def shards(fields, cotangent, weights, biases, ocean_tiles, velocity_mask):
    n = lax.axis_size("tiles")
    hbm = pl.BlockSpec(memory_space=pltpu.HBM)
    out, field_grad, summed = pl.pallas_call(
        functools.partial(kernel, n),
        out_shape=(
            jax.ShapeDtypeStruct((C, ROWS, LANES), BF),
            jax.ShapeDtypeStruct((C, ROWS, LANES), BF),
            jax.ShapeDtypeStruct((3, C, TOTAL), BF),
        ),
        in_specs=[
            hbm,
            hbm,
            hbm,
            hbm,
            pl.BlockSpec(memory_space=pltpu.SMEM),
            hbm,
        ],
        out_specs=(hbm,) * 3,
        scratch_shapes=[
            pltpu.VMEM((3 * C, CELLS + 3 * LANES), BF),
            pltpu.VMEM((3 * C, CELLS + 2 * LANES), BF),
            pltpu.VMEM((3 * C, CELLS + 4 * LANES), BF),
            pltpu.VMEM((3 * C, CELLS + LANES), BF),
            pltpu.VMEM((3 * C, CELLS + 2 * LANES), BF),
            pltpu.VMEM((3 * C, CELLS + 4 * LANES), BF),
            pltpu.VMEM((C, ROWS, LANES), BF),
            pltpu.VMEM((C, ROWS, LANES), BF),
            pltpu.VMEM((3, C), F32),
            pltpu.VMEM((C,), jnp.int32),
            pltpu.VMEM((3, 9, C, C), BF),
            pltpu.VMEM((ROWS, C, LANES), BF),
            pltpu.VMEM((ROWS, C, LANES), BF),
            pltpu.VMEM((C * ROWS, LANES), F32),
            pltpu.VMEM((LANES, 2 * LANES), F32),
            pltpu.VMEM((3, C, CELLS), F32),
            pltpu.VMEM((C, CELLS), F32),
            pltpu.VMEM((C, CELLS), F32),
            pltpu.VMEM((3, 3, C, 2 * C), BF),
            pltpu.VMEM((3, 3, C, C), BF),
            pltpu.VMEM((3, 3, C, 2 * C), BF),
            pltpu.VMEM((3, C, 3 * C), BF),
            pltpu.VMEM((6, C, LANES), BF),
            pltpu.VMEM((C, LANES), F32),
            pltpu.VMEM((C, LANES), F32),
            pltpu.VMEM((9 * C, 2 * LANES), BF),
            pltpu.VMEM((3, C, 3 * C), BF),
            pltpu.VMEM((3, C, 3 * C), BF),
            pltpu.VMEM((6, BAND, LANES), BF),
            pltpu.VMEM((6, C, 4 * LANES), BF),
            pltpu.VMEM((6, 2, C, LANES), BF),
            pltpu.VMEM((6, 3, BAND, LANES), BF),
            pltpu.VMEM((3, C, TOTAL), F32),
            pltpu.VMEM((3, C, HALF), BF),
            pltpu.VMEM((3, C, HALF), BF),
            pltpu.VMEM((3, C, HALF), BF),
            pltpu.VMEM((3, 3, BAND, HALF), BF),
            pltpu.VMEM((3, 4, BAND, HALF), BF),
            pltpu.VMEM((3, 4, BAND, HALF), BF),
            pltpu.VMEM((3, C, TOTAL), BF),
            pltpu.SemaphoreType.DMA((7,)),
            pltpu.SemaphoreType.DMA((5,)),
            pltpu.SemaphoreType.DMA((6, 7)),
            pltpu.SemaphoreType.DMA((6, 7)),
            pltpu.SemaphoreType.DMA((3, 40)),
            pltpu.SemaphoreType.DMA((3, 40)),
        ],
        compiler_params=pltpu.CompilerParams(
            collective_id=0, has_side_effects=True, vmem_limit_bytes=62 * 1024 * 1024
        ),
        cost_estimate=pl.CostEstimate(
            flops=18 * 9 * C * C * CELLS, bytes_accessed=8 * 1024 * 1024, transcendentals=9 * C * CELLS
        ),
    )(fields, cotangent, weights, biases, ocean_tiles, velocity_mask)
    return pl.pallas_call(
        finish,
        out_shape=(
            jax.ShapeDtypeStruct((C, ROWS, LANES), BF),
            jax.ShapeDtypeStruct((C, ROWS, LANES), BF),
            jax.ShapeDtypeStruct((3, 9, C, C), F32),
            jax.ShapeDtypeStruct((3, C), F32),
        ),
        in_specs=[hbm] * 3,
        out_specs=(hbm,) * 4,
        scratch_shapes=[
            pltpu.VMEM((3, C, TOTAL), BF),
            pltpu.VMEM((2, C, ROWS, LANES), BF),
            pltpu.VMEM((3, 9, C, C), F32),
            pltpu.VMEM((3, C), F32),
            pltpu.SemaphoreType.DMA((5,)),
            pltpu.SemaphoreType.DMA((12,)),
        ],
        compiler_params=pltpu.CompilerParams(vmem_limit_bytes=62 * 1024 * 1024),
    )(out, field_grad, summed)


def solution(mesh):
    placed = (P(None, None, "tiles"), P(None, None, "tiles"), P(), P(), P(None, "tiles"), P())
    return jax.shard_map(
        shards,
        mesh=mesh,
        in_specs=placed,
        out_specs=(P(None, None, "tiles"), P(None, None, "tiles"), P(), P()),
        check_vma=False,
    )
```
